512 devices in a mesh: dp: 16 (over z, core), dom: 32 (over x, y).
Axes of the slice: x: 4, y: 8, z: 8, core: 2. Of those that a mesh axis runs over, the one named last changes fastest.
Arguments:
- nodes: bfloat16 [16, 65536, 128], P('dp', 'dom'), may hold values from -6 to 6
- cotangent: bfloat16 [16, 65536, 128], P('dp', 'dom'), may hold values from -6 to 6
- weights: bfloat16 [3, 4, 128, 128], replicated, may hold values from -0.5 to 0.5
- fine_tiles: bfloat16 [512, 3, 128, 128], P('dom'), may hold values from -0.3125 to 0.3125
- fine_cols: int32 [512, 3], P('dom'), may hold values from 0 to 17, as said below
- fine_export: int32 [32, 2, 128], P('dom'), may hold values from 0 to 2047
- pool_tiles: bfloat16 [128, 2, 128, 128], P('dom'), may hold values from -0.375 to 0.375
- pool_cols: int32 [128, 2], P('dom'), may hold values from 0 to 15
- mid_tiles: bfloat16 [128, 3, 128, 128], P('dom'), may hold values from -0.3125 to 0.3125
- mid_cols: int32 [128, 3], P('dom'), may hold values from 0 to 5, as said below
- mid_export: int32 [32, 2, 128], P('dom'), may hold values from 0 to 511
- top_pool_tiles: bfloat16 [32, 2, 128, 128], P('dom'), may hold values from -0.375 to 0.375
- top_pool_cols: int32 [32, 2], P('dom'), may hold values from 0 to 3
- top_tiles: bfloat16 [32, 3, 128, 128], P('dom'), may hold values from -1 to 1
- top_cols: int32 [32, 3], P('dom'), may hold values from 0 to 31, as said below
Outputs:
- node_grad: bfloat16 [16, 65536, 128], P('dp', 'dom')
- weight_grad: float32 [3, 4, 128, 128], replicated
The draws below stay inside these ranges and needn't reach their ends.
Inputs may be any that keep to these rules, and one draw needn't show every extreme that they name: `fine_cols`: tile 0 of every fine row block is the block itself; tile 2 of a partition's first row block is block 16, of its last row block block 17. `mid_cols`: tile 0 of every middle row block is the block itself; tile 2 of a partition's first row block is block 4, of its last row block block 5. `top_cols`: tile 0 of every coarsest row block r is r itself, tile 1 is block (r + 16) modulo 32.
All inputs are finite; a program needn't handle non-finite values.
Results may differ from the reference program's by a relative error of at most 0.015.
Values may be sent and summed in bfloat16 or wider, within the bound.
A program may use at most 64 MiB of HBM per device.

```python
import jax
import jax.numpy as jnp
from jax import lax

W = 128
TILE = 128
TPB = 3
TPP = 2
TPC = 3
NF_DEV = 2048
NC1_DEV = 512
NC2_DEV = 128
BL0 = 16
BL1 = 4
BL2 = 1
NF = 65536
NB0 = 512
NB1 = 128
NB2 = 32
SNAP = 16
N_DOM = 32


def local_columns(key, total, local_blocks, number):
    random_cols = jax.random.randint(key, (total, number), 0, local_blocks + 2)
    position = jnp.arange(total, dtype=jnp.int32) % local_blocks
    third = jnp.where(position == 0, local_blocks, jnp.where(position == local_blocks - 1, local_blocks + 1, random_cols[:, 2]))
    columns = random_cols.at[:, 0].set(position)
    return columns.at[:, 2].set(third).astype(jnp.int32)


def draw_fine_cols(key, part):
    key = jax.random.fold_in(key, 11)
    return local_columns(key, NB0, BL0, TPB)


def draw_mid_cols(key, part):
    key = jax.random.fold_in(key, 12)
    return local_columns(key, NB1, BL1, TPB)


def draw_top_cols(key, part):
    key = jax.random.fold_in(key, 13)
    random_cols = jax.random.randint(key, (NB2, TPC), 0, NB2)
    rows = jnp.arange(NB2, dtype=jnp.int32)
    random_cols = random_cols.at[:, 0].set(rows)
    random_cols = random_cols.at[:, 1].set((rows + NB2 // 2) % NB2)
    return random_cols.astype(jnp.int32)


def draw_top_tiles(key, part):
    key = jax.random.fold_in(key, 14)
    values = jax.random.truncated_normal(key, -3.0, 3.0, (NB2, TPC, TILE, TILE), jnp.float32)
    factors = jnp.where(jnp.arange(TPC) == 1, 1.5, 0.5).astype(jnp.float32)
    scaled = values * factors[None, :, None, None] / jnp.sqrt(jnp.float32(TILE))
    return jnp.clip(scaled, -1.0, 1.0).astype(jnp.bfloat16)


def set_ends(drawn, stream_key, low, high):
    longest = drawn.shape.index(max(drawn.shape))
    spots = []
    for shift in (0, 1):
        where = [jax.random.randint(jax.random.fold_in(stream_key, axis), (), 0, length) for axis, length in enumerate(drawn.shape)]
        where[longest] = (where[longest] + shift) % drawn.shape[longest]
        spots.append(tuple(where))
    return drawn.at[spots[0]].set(low).at[spots[1]].set(high)


def block_levels(key, dims, shards, smallest, top_value):
    gain, own = 1.0, jax.random.fold_in(key, 6)
    for axis_at, blocks in shards:
        heights = jnp.exp(jax.random.uniform(jax.random.fold_in(own, axis_at), (blocks,), jnp.float32, smallest / len(shards), top_value / len(shards)))
        gain = gain * jnp.repeat(heights, dims[axis_at] // blocks).reshape([-1 if axis == axis_at else 1 for axis in range(len(dims))])
    return gain


def normal_values(own_key, dims, spread, reach, shards=(), held_as=jnp.bfloat16):
    level = block_levels(own_key, dims, shards, -0.22, 0.18) if shards else 1.0
    drawn = jax.random.normal(own_key, dims, jnp.float32) * spread * level
    return jnp.minimum(jnp.maximum(drawn, -reach), reach).astype(held_as)


def setup_inputs(seed: int = 0) -> dict:
    seeds = jax.random.split(jax.random.key(seed), 16)
    nodes = normal_values(seeds[0], (SNAP, NF, W), 1.0, 6.0, ((0, 16), (1, 32)))
    cotangent = normal_values(seeds[1], (SNAP, NF, W), 1.0, 6.0, ((0, 16), (1, 32)))
    weights = normal_values(seeds[2], (3, 4, W, W), W ** -0.5, 0.5)
    fine_tiles = normal_values(seeds[3], (NB0, TPB, TILE, TILE), (TPB * TILE) ** -0.5, 0.3125, ((0, 32),))
    fine_cols = draw_fine_cols(jax.random.fold_in(seeds[15], 71), 0)
    fine_export = set_ends(jax.random.randint(seeds[5], (N_DOM, 2, TILE), 0, NF_DEV), jax.random.fold_in(seeds[5], 1), 0, NF_DEV - 1).astype(jnp.int32)
    pool_tiles = normal_values(seeds[6], (NB1, TPP, TILE, TILE), (TPP * TILE) ** -0.5, 0.375, ((0, 32),))
    pool_cols = set_ends(jax.random.randint(seeds[7], (NB1, TPP), 0, BL0), jax.random.fold_in(seeds[7], 1), 0, BL0 - 1).astype(jnp.int32)
    mid_tiles = normal_values(seeds[8], (NB1, TPB, TILE, TILE), (TPB * TILE) ** -0.5, 0.3125, ((0, 32),))
    mid_cols = draw_mid_cols(jax.random.fold_in(seeds[15], 71), 0)
    mid_export = set_ends(jax.random.randint(seeds[10], (N_DOM, 2, TILE), 0, NC1_DEV), jax.random.fold_in(seeds[10], 1), 0, NC1_DEV - 1).astype(jnp.int32)
    top_pool_tiles = normal_values(seeds[11], (NB2, TPP, TILE, TILE), (TPP * TILE) ** -0.5, 0.375, ((0, 32),))
    top_pool_cols = set_ends(jax.random.randint(seeds[12], (NB2, TPP), 0, BL1), jax.random.fold_in(seeds[12], 1), 0, BL1 - 1).astype(jnp.int32)
    top_tiles = draw_top_tiles(jax.random.fold_in(seeds[15], 71), 0)
    top_cols = draw_top_cols(jax.random.fold_in(seeds[15], 71), 0)
    return dict(nodes=nodes, cotangent=cotangent, weights=weights, fine_tiles=fine_tiles, fine_cols=fine_cols, fine_export=fine_export, pool_tiles=pool_tiles, pool_cols=pool_cols, mid_tiles=mid_tiles, mid_cols=mid_cols, mid_export=mid_export, top_pool_tiles=top_pool_tiles, top_pool_cols=top_pool_cols, top_tiles=top_tiles, top_cols=top_cols)


def silu_slope(pre_values):
    logistic = jax.nn.sigmoid(pre_values)
    return logistic * (1.0 + pre_values * (1.0 - logistic))


def mixed(left, right):
    return jnp.einsum('...rw,wv->...rv', left.astype(jnp.float32), right.astype(jnp.float32))


def mixed_back(left, right):
    return jnp.einsum('...rv,wv->...rw', left.astype(jnp.float32), right.astype(jnp.float32))


def outer_sum(left, right):
    return jnp.einsum('...rw,...rv->wv', left.astype(jnp.float32), right.astype(jnp.float32))


def node_forward(inputs, message, matrices):
    first_pre = mixed(inputs, matrices[0]) + mixed(message, matrices[1])
    first_act = jax.nn.silu(first_pre).astype(jnp.bfloat16)
    second_pre = mixed(first_act, matrices[2])
    second_act = jax.nn.silu(second_pre).astype(jnp.bfloat16)
    output = (inputs.astype(jnp.float32) + mixed(second_act, matrices[3])).astype(jnp.bfloat16)
    return output, (first_pre, first_act, second_pre, second_act)


def node_backward(grad_out, inputs, message, saved, matrices):
    first_pre, first_act, second_pre, second_act = saved
    grad_low = grad_out.astype(jnp.bfloat16)
    grad_last = outer_sum(second_act, grad_low)
    grad_second = (mixed_back(grad_low, matrices[3]) * silu_slope(second_pre)).astype(jnp.bfloat16)
    grad_hidden = outer_sum(first_act, grad_second)
    grad_first = (mixed_back(grad_second, matrices[2]) * silu_slope(first_pre)).astype(jnp.bfloat16)
    grad_node = outer_sum(inputs, grad_first)
    grad_mess = outer_sum(message, grad_first)
    grad_inputs = grad_out + mixed_back(grad_first, matrices[0])
    grad_message = mixed_back(grad_first, matrices[1])
    return grad_inputs, grad_message, jnp.stack([grad_node, grad_mess, grad_hidden, grad_last])


def blockify(values):
    return values.reshape(values.shape[0], -1, TILE, values.shape[-1])


def tile_apply(adjacency, columns, blocks):
    picked = jax.vmap(lambda source, index: source[index])(blocks, columns)
    return jnp.einsum('pbkij,pbkjw->pbiw', adjacency.astype(jnp.float32), picked.astype(jnp.float32))


def tile_spread(adjacency, columns, gradient, number):
    pieces = jnp.einsum('pbkij,pbiw->pbkjw', adjacency.astype(jnp.float32), gradient.astype(jnp.float32))
    onehot = (columns[..., None] == jnp.arange(number, dtype=jnp.int32)).astype(jnp.float32)
    return jnp.einsum('pbkn,pbkjw->pnjw', onehot, pieces, precision=lax.Precision.HIGHEST)


def with_halo(values, export):
    sent = jax.vmap(lambda source, index: source[index])(values, export)
    zero_block = jnp.zeros((1, TILE, W), values.dtype)
    left_rows = jnp.concatenate([zero_block, sent[:-1, 1]], 0)
    right_rows = jnp.concatenate([sent[1:, 0], zero_block], 0)
    return jnp.concatenate([blockify(values), left_rows[:, None], right_rows[:, None]], 1)


def halo_back(gradient, export, local_blocks):
    left_grad = gradient[:, local_blocks]
    right_grad = gradient[:, local_blocks + 1]
    zero_block = jnp.zeros((1, TILE, W), jnp.float32)
    to_left = jnp.concatenate([zero_block, right_grad[:-1]], 0)
    to_right = jnp.concatenate([left_grad[1:], zero_block], 0)
    own = gradient[:, :local_blocks].reshape(N_DOM, local_blocks * TILE, W)

    def place(rows, index, first, second):
        return rows.at[index[0]].add(first).at[index[1]].add(second)

    return jax.vmap(place)(own, export, to_left, to_right)


def reference(nodes, cotangent, weights, fine_tiles, fine_cols, fine_export, pool_tiles, pool_cols, mid_tiles, mid_cols, mid_export, top_pool_tiles, top_pool_cols, top_tiles, top_cols):
    fine_adj = fine_tiles.reshape(N_DOM, BL0, TPB, TILE, TILE)
    fine_idx = fine_cols.reshape(N_DOM, BL0, TPB)
    pool_adj = pool_tiles.reshape(N_DOM, BL1, TPP, TILE, TILE)
    pool_idx = pool_cols.reshape(N_DOM, BL1, TPP)
    mid_adj = mid_tiles.reshape(N_DOM, BL1, TPB, TILE, TILE)
    mid_idx = mid_cols.reshape(N_DOM, BL1, TPB)
    upper_adj = top_pool_tiles.reshape(N_DOM, BL2, TPP, TILE, TILE)
    upper_idx = top_pool_cols.reshape(N_DOM, BL2, TPP)
    coarse_adj = top_tiles.reshape(1, NB2, TPC, TILE, TILE)
    coarse_idx = top_cols.reshape(1, NB2, TPC)

    def one_snapshot(total, pair):
        snapshot, cot_rows = pair
        fine_in = snapshot.reshape(N_DOM, NF_DEV, W)
        cot_in = cot_rows.reshape(N_DOM, NF_DEV, W)
        fine_msg = tile_apply(fine_adj, fine_idx, with_halo(fine_in, fine_export)).reshape(N_DOM, NF_DEV, W).astype(jnp.bfloat16)
        fine_out, fine_saved = node_forward(fine_in, fine_msg, weights[0])
        mid_in = tile_apply(pool_adj, pool_idx, blockify(fine_out)).reshape(N_DOM, NC1_DEV, W).astype(jnp.bfloat16)
        mid_msg = tile_apply(mid_adj, mid_idx, with_halo(mid_in, mid_export)).reshape(N_DOM, NC1_DEV, W).astype(jnp.bfloat16)
        mid_out, mid_saved = node_forward(mid_in, mid_msg, weights[1])
        top_in = tile_apply(upper_adj, upper_idx, blockify(mid_out)).reshape(N_DOM, NC2_DEV, W).astype(jnp.bfloat16)
        top_msg = tile_apply(coarse_adj, coarse_idx, top_in.reshape(1, NB2, TILE, W)).reshape(N_DOM, NC2_DEV, W).astype(jnp.bfloat16)
        top_out, top_saved = node_forward(top_in, top_msg, weights[2])
        grad_mid = tile_apply(pool_adj, pool_idx, blockify(cot_in)).reshape(N_DOM, NC1_DEV, W)
        grad_top = tile_apply(upper_adj, upper_idx, blockify(grad_mid.astype(jnp.bfloat16))).reshape(N_DOM, NC2_DEV, W)
        grad_top_in, grad_top_msg, top_terms = node_backward(grad_top, top_in, top_msg, top_saved, weights[2])
        spread_top = tile_spread(coarse_adj, coarse_idx, grad_top_msg.astype(jnp.bfloat16).reshape(1, NB2, TILE, W), NB2)
        grad_top_in = grad_top_in + spread_top.reshape(N_DOM, NC2_DEV, W)
        grad_mid = grad_mid + tile_spread(upper_adj, upper_idx, blockify(grad_top_in.astype(jnp.bfloat16)), BL1).reshape(N_DOM, NC1_DEV, W)
        grad_mid_in, grad_mid_msg, mid_terms = node_backward(grad_mid, mid_in, mid_msg, mid_saved, weights[1])
        mid_spread = tile_spread(mid_adj, mid_idx, blockify(grad_mid_msg.astype(jnp.bfloat16)), BL1 + 2)
        grad_mid_in = grad_mid_in + halo_back(mid_spread, mid_export, BL1)
        grad_fine = cot_in.astype(jnp.float32) + tile_spread(pool_adj, pool_idx, blockify(grad_mid_in.astype(jnp.bfloat16)), BL0).reshape(N_DOM, NF_DEV, W)
        grad_nodes, grad_fine_msg, fine_terms = node_backward(grad_fine, fine_in, fine_msg, fine_saved, weights[0])
        fine_spread = tile_spread(fine_adj, fine_idx, blockify(grad_fine_msg.astype(jnp.bfloat16)), BL0 + 2)
        grad_nodes = grad_nodes + halo_back(fine_spread, fine_export, BL0)
        terms = jnp.stack([fine_terms, mid_terms, top_terms])
        return total + terms, grad_nodes.astype(jnp.bfloat16).reshape(NF, W)

    start = jnp.zeros((3, 4, W, W), jnp.float32)
    weight_grad, node_grad = lax.scan(one_snapshot, start, (nodes, cotangent))
    return node_grad, weight_grad
```

```python
import jax
import jax.numpy as jnp
from jax import lax
from jax.experimental import pallas as pl
from jax.experimental.pallas import tpu as pltpu
from jax.sharding import PartitionSpec as P

NY = 8
T = 128
FB, MB, TB = 16, 4, 1
GROUP = 4
F32, BF16 = jnp.float32, jnp.bfloat16
MESH = pl.DeviceIdType.MESH


def dot(a, b):
    return jnp.dot(a, b, preferred_element_type=F32)


def dot_bt(a, b):
    return lax.dot_general(a, b, (((1,), (1,)), ((), ())), preferred_element_type=F32)


def dot_at(a, b):
    return lax.dot_general(a, b, (((0,), (0,)), ((), ())), preferred_element_type=F32)


def logistic(s):
    return 0.5 * jnp.tanh(0.5 * s) + 0.5


def slope(s):
    q = logistic(s)
    return q * (1.0 + s * (1.0 - q))


def flat(blocks):
    return blocks.reshape(-1, T)


def tiled(rows):
    return rows.reshape(-1, T, T)


def picked_rows(export, source):
    columns = [
        jnp.transpose(jnp.broadcast_to(export[i : i + 1].astype(F32), (T, T))) for i in range(2)
    ]
    lane = lax.broadcasted_iota(jnp.int32, (T, T), 1).astype(F32)
    total = jnp.zeros((2 * T, T), F32)
    for pair in range(source.shape[0] // 2):
        onehot = jnp.concatenate(
            [
                jnp.concatenate(
                    [
                        jnp.where(column - T * (2 * pair + half) == lane, 1.0, 0.0)
                        for half in range(2)
                    ],
                    axis=1,
                )
                for column in columns
            ],
            axis=0,
        ).astype(BF16)
        total = total + dot(onehot, flat(source[2 * pair : 2 * pair + 2]))
    return tiled(total.astype(BF16))


def placed_rows(export, block, rows):
    row = lax.broadcasted_iota(jnp.int32, (T, T), 0) + block * T
    onehot = jnp.concatenate(
        [jnp.where(export[i : i + 1] == row, 1.0, 0.0) for i in range(2)], axis=1
    ).astype(BF16)
    return dot(onehot, rows)


def link(column, number, targets, prev, last):
    def before(s, carry):
        mine = column(s)
        best = jnp.int32(-1)
        for t in range(number):
            best = jnp.where((column(t) == mine) & (t < s), t, best)
        prev[s] = best
        return carry

    def final(j, carry):
        best = jnp.int32(-1)
        for t in range(number):
            best = jnp.where(column(t) == j, t, best)
        last[j] = best
        return carry

    lax.fori_loop(0, number, before, 0)
    lax.fori_loop(0, targets, final, 0)


def linked(pieces, at):
    return jnp.where(at >= 0, 1.0, 0.0) * pieces[jnp.maximum(at, 0)]


def chain(pieces, prev, number):
    def step(s, carry):
        pieces[s] = pieces[s] + linked(pieces, prev[s])
        return carry

    lax.fori_loop(0, number, step, 0)


def kernel(
    nx,
    ndp,
    nodes,
    cotangent,
    weights,
    fine_tiles,
    fcols,
    fexport,
    pool_tiles,
    pcols,
    mid_tiles,
    mcols,
    mexport,
    upper_tiles,
    ucols,
    top_tiles,
    tcols,
    node_grad,
    weight_grad,
    S,
    COT,
    M,
    FT,
    PT,
    MT,
    UT,
    TT,
    PART,
    PRE1,
    PRE2,
    ACT1,
    ACT2,
    MSG,
    OUT,
    GN,
    GM,
    PIECE,
    MS,
    MPART,
    MPRE1,
    MPRE2,
    MACT1,
    MACT2,
    MMSG,
    MOUT,
    GRADM,
    GRADML,
    MGN,
    MGM,
    MPIECE,
    PPIECE,
    UPIECE,
    fprev,
    flast,
    mprev,
    mlast,
    pprev,
    plast,
    uprev,
    ulast,
    HALO_S,
    HALO_R,
    MHALO_S,
    MHALO_R,
    BACK_S,
    BACK_R,
    MBACK_S,
    MBACK_R,
    COL_S,
    COL_R,
    YG,
    PARTNER,
    SEL_S,
    SEL_R,
    P1_S,
    P1_R,
    P2_S,
    P2_R,
    PY_S,
    PY_R,
    WACC,
    W1_S,
    W1_R,
    W1_Y,
    W1_X,
    W1_O,
    W0_S,
    W0_R,
    W0_Y,
    W0_X,
    W0_O,
    WOUT,
    ONODE,
    load_sem,
    send_sem,
    recv_sem,
):
    ny = NY
    ndom = nx * ny
    dp = lax.axis_index("dp")
    dom = lax.axis_index("dom")
    x = lax.div(dom, ny)
    y = lax.rem(dom, ny)

    left = (dp, lax.rem(dom + ndom - 1, ndom))
    right = (dp, lax.rem(dom + 1, ndom))

    def at_x(i):
        return (dp, lax.rem(x + i, nx) * ny + y)

    def at_y(i):
        return (dp, x * ny + lax.rem(y + i, ny))

    def at_dp(i):
        return (lax.rem(dp + i, ndp), dom)

    partners = (
        [left, right]
        + [at_x(i) for i in range(1, nx)]
        + [at_y(i) for i in range(1, ny)]
        + [at_dp(i) for i in range(1, ndp)]
    )
    barrier = pltpu.get_barrier_semaphore()
    for partner in partners:
        pl.semaphore_signal(barrier, inc=1, device_id=partner, device_id_type=MESH)

    started = []

    def send(src, dst, device):
        number = len(started)
        copy = pltpu.make_async_remote_copy(
            src_ref=src,
            dst_ref=dst,
            send_sem=send_sem.at[number],
            recv_sem=recv_sem.at[number],
            device_id=device,
            device_id_type=MESH,
        )
        copy.start()
        started.append(copy)
        return copy

    loads = []

    def load(src, dst):
        copy = pltpu.make_async_copy(src, dst, load_sem.at[len(loads)])
        copy.start()
        loads.append(copy)
        return copy

    got_nodes = load(nodes, S.at[pl.ds(0, FB)])
    got_cot = load(cotangent, COT)
    got_pool = load(pool_tiles, PT)
    got_upper = load(upper_tiles, UT)
    got_weights = load(weights, M)
    got_fine = load(fine_tiles, FT)
    got_mid = load(mid_tiles, MT)
    got_top = load(top_tiles, TT)

    has_left = jnp.where(dom > 0, 1.0, 0.0).astype(F32)
    has_right = jnp.where(dom < ndom - 1, 1.0, 0.0).astype(F32)

    def level(l):
        return [M[l, i] for i in range(4)]

    my_col = tcols[0, 2]
    COL_S[...] = jnp.full((8, T), my_col, jnp.int32)
    got_nodes.wait()
    HALO_S[...] = picked_rows(fexport[0], S)
    pl.semaphore_wait(barrier, len(partners))
    halo = [send(HALO_S.at[1], HALO_R.at[0], right), send(HALO_S.at[0], HALO_R.at[1], left)]
    cols_sent = [send(COL_S, COL_R.at[i - 1], at_x(i)) for i in range(1, nx)]

    got_cot.wait()
    got_pool.wait()
    got_upper.wait()
    for m in range(MB):
        pooled = dot(PT[m, 0], COT[pcols[m, 0]]) + dot(PT[m, 1], COT[pcols[m, 1]])
        GRADM[m] = pooled
        GRADML[m] = pooled.astype(BF16)
    grad_top = dot(UT[0, 0], GRADML[ucols[0, 0]]) + dot(UT[0, 1], GRADML[ucols[0, 1]])
    got_weights.wait()
    got_fine.wait()

    def fine_own(g, carry):
        base = g * GROUP
        m0 = M[0, 0]
        u = flat(S[pl.ds(base, GROUP)])
        PRE1[pl.ds(base, GROUP)] = tiled(dot(u, m0))
        for b in range(GROUP):
            PART[base + b] = dot(FT[base + b, 0], S[base + b])
        return carry

    lax.fori_loop(0, FB // GROUP, fine_own, 0)

    for copy in halo:
        copy.wait_recv()
    S[FB] = HALO_R[0] * has_left.astype(BF16)
    S[FB + 1] = HALO_R[1] * has_right.astype(BF16)

    def forward(u, v, own_pre, m):
        pre1 = own_pre + dot(v, m[1])
        act1 = (pre1 * logistic(pre1)).astype(BF16)
        pre2 = dot(act1, m[2])
        act2 = (pre2 * logistic(pre2)).astype(BF16)
        return pre1, act1, pre2, act2

    def fine_forward(g, carry):
        base = g * GROUP
        m = level(0)
        messages = []
        for b in range(GROUP):
            r = base + b
            messages.append(
                (
                    PART[r]
                    + dot(FT[r, 1], S[fcols[r, 1]])
                    + dot(FT[r, 2], S[fcols[r, 2]])
                ).astype(BF16)
            )
        v = jnp.concatenate(messages, axis=0)
        here = pl.ds(base, GROUP)
        u = flat(S[here])
        pre1, act1, pre2, act2 = forward(u, v, flat(PRE1[here]), m)
        MSG[here] = tiled(v)
        PRE1[here] = tiled(pre1)
        ACT1[here] = tiled(act1)
        PRE2[here] = tiled(pre2)
        ACT2[here] = tiled(act2)
        OUT[here] = tiled((u.astype(F32) + dot(act2, m[3])).astype(BF16))
        return carry

    lax.fori_loop(0, FB // GROUP, fine_forward, 0)

    for m in range(MB):
        MS[m] = (dot(PT[m, 0], OUT[pcols[m, 0]]) + dot(PT[m, 1], OUT[pcols[m, 1]])).astype(BF16)
    MHALO_S[...] = picked_rows(mexport[0], MS[0:MB])
    mid_halo = [send(MHALO_S.at[1], MHALO_R.at[0], right), send(MHALO_S.at[0], MHALO_R.at[1], left)]
    got_mid.wait()
    mm = level(1)
    mu = flat(MS[0:MB])
    MPRE1[...] = tiled(dot(mu, mm[0]))
    for r in range(MB):
        MPART[r] = dot(MT[r, 0], MS[r])
    got_top.wait()
    link(lambda s: ucols[0, s], 2, MB, uprev, ulast)
    for copy in mid_halo:
        copy.wait_recv()
    MS[MB] = MHALO_R[0] * has_left.astype(BF16)
    MS[MB + 1] = MHALO_R[1] * has_right.astype(BF16)
    mv = jnp.concatenate(
        [
            (
                MPART[r] + dot(MT[r, 1], MS[mcols[r, 1]]) + dot(MT[r, 2], MS[mcols[r, 2]])
            ).astype(BF16)
            for r in range(MB)
        ],
        axis=0,
    )
    pre1, act1, pre2, act2 = forward(mu, mv, flat(MPRE1[...]), mm)
    MOUT[...] = tiled((mu.astype(F32) + dot(act2, mm[3])).astype(BF16))
    top_in = (dot(UT[0, 0], MOUT[ucols[0, 0]]) + dot(UT[0, 1], MOUT[ucols[0, 1]])).astype(BF16)

    YG[0] = top_in
    along_y = [send(YG.at[0], YG.at[i], at_y(i)) for i in range(1, ny)]
    half = send(YG.at[0], PARTNER, at_x(nx // 2))
    MMSG[...] = tiled(mv)
    MACT1[...] = tiled(act1)
    MACT2[...] = tiled(act2)
    MPRE1[...] = tiled(slope(pre1))
    MPRE2[...] = tiled(slope(pre2))

    def fine_slopes(g, carry):
        here = pl.ds(g * 2, 2)
        PRE1[here] = slope(PRE1[here])
        PRE2[here] = slope(PRE2[here])
        return carry

    lax.fori_loop(0, FB // 2, fine_slopes, 0)
    tm = level(2)
    top_own = dot(top_in, tm[0])
    top_part = dot(TT[0, 0], top_in)
    for copy in cols_sent:
        copy.wait_recv()
    cols = [COL_S[0:1]] + [COL_R[i, 0:1] for i in range(nx - 1)]
    for copy in along_y:
        copy.wait_recv()

    def chosen(column):
        total = jnp.zeros((T, T), BF16)
        for k in range(ny):
            source = x * ny + lax.rem(y + ny - k, ny)
            total = total + jnp.where(column == source, 1.0, 0.0).astype(BF16) * YG[k]
        return total

    along_x = []
    for i in range(1, nx):
        SEL_S[i - 1] = chosen(cols[nx - i])
        along_x.append(send(SEL_S.at[i - 1], SEL_R.at[i - 1], at_x(i)))
    third = chosen(cols[0])
    half.wait_recv()
    top_part = top_part + dot(TT[0, 1], PARTNER[...])
    link(lambda s: pcols[lax.rem(s, MB), lax.div(s, MB)], 2 * MB, FB, pprev, plast)
    link(lambda s: mcols[lax.rem(s, MB), 1 + lax.div(s, MB)], 2 * MB, MB + 2, mprev, mlast)
    for copy in along_x:
        copy.wait_recv()
    for i in range(nx - 1):
        third = third + SEL_R[i]
    top_msg = (top_part + dot(TT[0, 2], third)).astype(BF16)
    pre1, act1, pre2, act2 = forward(top_in, top_msg, top_own, tm)

    def backward(g, slope1, slope2, m):
        gb = g.astype(BF16)
        gs = (dot_bt(gb, m[3]) * slope2).astype(BF16)
        gf = (dot_bt(gs, m[2]) * slope1).astype(BF16)
        return gb, gs, gf, dot_bt(gf, m[1]).astype(BF16)

    def terms(u, v, act1, act2, gb, gs, gf):
        return dot_at(u, gf), dot_at(v, gf), dot_at(act1, gs), dot_at(act2, gb)

    gb, gs, gf, gm = backward(grad_top, slope(pre1), slope(pre2), tm)
    P2_S[...] = dot_at(TT[0, 2], gm).astype(BF16)
    back_x = [send(P2_S, P2_R.at[i - 1], at_x(i)) for i in range(1, nx)]
    P1_S[...] = dot_at(TT[0, 1], gm).astype(BF16)
    back_half = send(P1_S, P1_R, at_x(nx // 2))
    grad_top_in = grad_top + dot_bt(gf, tm[0]) + dot_at(TT[0, 0], gm)
    for i, term in enumerate(terms(top_in, top_msg, act1, act2, gb, gs, gf)):
        W1_S[pl.ds((4 + i) * T, T)] = term.astype(BF16)
    for copy in back_x:
        copy.wait_recv()
    arrived = [P2_S[...].astype(F32)] + [P2_R[i].astype(F32) for i in range(nx - 1)]

    def summed(target):
        total = jnp.zeros((T, T), F32)
        for column, piece in zip(cols, arrived):
            total = total + jnp.where(column == target, 1.0, 0.0) * piece
        return total

    back_y = []
    for i in range(1, ny):
        PY_S[i - 1] = summed(x * ny + lax.rem(y + i, ny)).astype(BF16)
        back_y.append(send(PY_S.at[i - 1], PY_R.at[i - 1], at_y(i)))
    grad_top_in = grad_top_in + summed(dom)
    link(lambda s: fcols[lax.rem(s, FB), 1 + lax.div(s, FB)], 2 * FB, FB + 2, fprev, flast)
    back_half.wait_recv()
    grad_top_in = grad_top_in + P1_R[...].astype(F32)
    for copy in back_y:
        copy.wait_recv()
    for i in range(ny - 1):
        grad_top_in = grad_top_in + PY_R[i].astype(F32)

    low = grad_top_in.astype(BF16)
    for s in range(2):
        UPIECE[s] = dot_at(UT[0, s], low)
    chain(UPIECE, uprev, 2)
    for m in range(MB):
        GRADM[m] = GRADM[m] + linked(UPIECE, ulast[m])
    g = flat(GRADM[...])
    gb, gs, gf, gm = backward(g, flat(MPRE1[...]), flat(MPRE2[...]), mm)
    MGM[...] = tiled(gm)
    for r in range(MB):
        MPIECE[r] = dot_at(MT[r, 1], MGM[r])
        MPIECE[MB + r] = dot_at(MT[r, 2], MGM[r])
    chain(MPIECE, mprev, 2 * MB)
    MBACK_S[0] = linked(MPIECE, mlast[MB]).astype(BF16)
    MBACK_S[1] = linked(MPIECE, mlast[MB + 1]).astype(BF16)
    mid_back = [send(MBACK_S.at[1], MBACK_R.at[0], right), send(MBACK_S.at[0], MBACK_R.at[1], left)]
    MGN[...] = tiled(g + dot_bt(gf, mm[0]))
    for r in range(MB):
        MGN[r] = MGN[r] + dot_at(MT[r, 0], MGM[r]) + linked(MPIECE, mlast[r])
    for i, term in enumerate(
        terms(flat(MS[0:MB]), flat(MMSG[...]), flat(MACT1[...]), flat(MACT2[...]), gb, gs, gf)
    ):
        W1_S[pl.ds(i * T, T)] = term.astype(BF16)

    def scattered(store, slots, rows):
        return [
            send(
                store.at[pl.ds(pl.multiple_of(at_dp(i)[0] * rows, rows), rows)],
                slots.at[i - 1],
                at_dp(i),
            )
            for i in range(1, ndp)
        ]

    def chunk_sum(copies, store, slots, rows):
        for copy in copies:
            copy.wait_recv()
        total = store[pl.ds(pl.multiple_of(dp * rows, rows), rows)].astype(F32)
        for i in range(ndp - 1):
            total = total + slots[i].astype(F32)
        return total.astype(BF16)

    def spread_y(value, slots):
        slots[y] = value
        return [send(slots.at[y], slots.at[y], at_y(i)) for i in range(1, ny)]

    def spread_x(value, slots):
        slots[x] = value
        return [send(slots.at[x], slots.at[x], at_x(i)) for i in range(1, nx)]

    def slot_sum(copies, slots, number):
        for copy in copies:
            copy.wait_recv()
        total = slots[0].astype(F32)
        for i in range(1, number):
            total = total + slots[i].astype(F32)
        return total.astype(BF16)

    def gathered(value, store, rows):
        mine = pl.ds(pl.multiple_of(dp * rows, rows), rows)
        store[mine] = value
        return [send(store.at[mine], store.at[mine], at_dp(i)) for i in range(1, ndp)]

    rows1 = 8 * T // ndp
    rows0 = 4 * T // ndp
    w1 = scattered(W1_S, W1_R, rows1)

    for copy in mid_back:
        copy.wait_recv()
    back_rows = jnp.concatenate(
        [MBACK_R[0] * has_left.astype(BF16), MBACK_R[1] * has_right.astype(BF16)], axis=0
    )
    for r in range(MB):
        MGN[r] = MGN[r] + placed_rows(mexport[0], r, back_rows)
    for m in range(MB):
        low = MGN[m].astype(BF16)
        for k in range(2):
            PPIECE[k * MB + m] = dot_at(PT[m, k], low)
    chain(PPIECE, pprev, 2 * MB)

    WACC[...] = jnp.zeros_like(WACC)

    def fine_backward(g, carry):
        base = g * GROUP
        here = pl.ds(base, GROUP)
        m = level(0)
        grad = jnp.concatenate(
            [COT[base + b].astype(F32) + linked(PPIECE, plast[base + b]) for b in range(GROUP)],
            axis=0,
        )
        gb, gs, gf, gm = backward(grad, flat(PRE1[here]), flat(PRE2[here]), m)
        GM[here] = tiled(gm)
        GN[here] = tiled(grad + dot_bt(gf, m[0]))
        for i, term in enumerate(
            terms(flat(S[here]), flat(MSG[here]), flat(ACT1[here]), flat(ACT2[here]), gb, gs, gf)
        ):
            WACC[i] = WACC[i] + term
        return carry

    lax.fori_loop(0, FB // GROUP, fine_backward, 0)
    W0_S[...] = flat(WACC[...]).astype(BF16)
    w0 = scattered(W0_S, W0_R, rows0)
    w1 = spread_y(chunk_sum(w1, W1_S, W1_R, rows1), W1_Y)

    def fine_pieces(g, carry):
        for b in range(2):
            r = g * 2 + b
            grad = GM[r]
            PIECE[r] = dot_at(FT[r, 1], grad)
            PIECE[FB + r] = dot_at(FT[r, 2], grad)
            GN[r] = GN[r] + dot_at(FT[r, 0], grad)
        return carry

    lax.fori_loop(0, FB // 2, fine_pieces, 0)
    chain(PIECE, fprev, 2 * FB)
    BACK_S[0] = linked(PIECE, flast[FB]).astype(BF16)
    BACK_S[1] = linked(PIECE, flast[FB + 1]).astype(BF16)
    back = [send(BACK_S.at[1], BACK_R.at[0], right), send(BACK_S.at[0], BACK_R.at[1], left)]
    w0 = spread_y(chunk_sum(w0, W0_S, W0_R, rows0), W0_Y)
    w1 = spread_x(slot_sum(w1, W1_Y, ny), W1_X)
    for copy in back:
        copy.wait_recv()
    w0 = spread_x(slot_sum(w0, W0_Y, ny), W0_X)
    w1 = gathered(slot_sum(w1, W1_X, nx), W1_O, rows1)
    back_rows = jnp.concatenate(
        [BACK_R[0] * has_left.astype(BF16), BACK_R[1] * has_right.astype(BF16)], axis=0
    )
    fexp = fexport[0]

    def finish(r, carry):
        ONODE[r] = (
            GN[r] + linked(PIECE, flast[r]) + placed_rows(fexp, r, back_rows)
        ).astype(BF16)
        return carry

    w0 = gathered(slot_sum(w0, W0_X, nx), W0_O, rows0)
    lax.fori_loop(0, FB, finish, 0)
    put_nodes = load(ONODE, node_grad)
    for copy in w1:
        copy.wait_recv()
    WOUT[1:3] = W1_O[...].reshape(2, 4, T, T).astype(F32)
    for copy in w0:
        copy.wait_recv()
    WOUT[0] = W0_O[...].reshape(4, T, T).astype(F32)
    put_weights = load(WOUT, weight_grad)
    for copy in started:
        copy.wait_send()
    put_nodes.wait()
    put_weights.wait()


def on_device(nx, ndp, *args):
    (
        nodes,
        cotangent,
        weights,
        fine_tiles,
        fine_cols,
        fine_export,
        pool_tiles,
        pool_cols,
        mid_tiles,
        mid_cols,
        mid_export,
        top_pool_tiles,
        top_pool_cols,
        top_tiles,
        top_cols,
    ) = args
    ny = NY
    vmem, smem, anywhere = (
        pl.BlockSpec(memory_space=pltpu.VMEM),
        pl.BlockSpec(memory_space=pltpu.SMEM),
        pl.BlockSpec(memory_space=pl.ANY),
    )

    def low(*shape):
        return pltpu.VMEM(shape, BF16)

    def full(*shape):
        return pltpu.VMEM(shape, F32)

    def index(number):
        return pltpu.SMEM((number,), jnp.int32)

    rows1, rows0 = 8 * T // ndp, 4 * T // ndp
    copies = (
        4 * 2 + (nx - 1) * 3 + (ny - 1) * 2 + 2 + 2 * (2 * (ndp - 1) + (ny - 1) + (nx - 1))
    )
    scratch = [
        low(FB + 2, T, T),
        low(FB, T, T),
        low(3, 4, T, T),
        low(FB, 3, T, T),
        low(MB, 2, T, T),
        low(MB, 3, T, T),
        low(1, 2, T, T),
        low(1, 3, T, T),
        full(FB, T, T),
        full(FB, T, T),
        full(FB, T, T),
        low(FB, T, T),
        low(FB, T, T),
        low(FB, T, T),
        low(FB, T, T),
        full(FB, T, T),
        low(FB, T, T),
        full(2 * FB, T, T),
        low(MB + 2, T, T),
        full(MB, T, T),
        full(MB, T, T),
        full(MB, T, T),
        low(MB, T, T),
        low(MB, T, T),
        low(MB, T, T),
        low(MB, T, T),
        full(MB, T, T),
        low(MB, T, T),
        full(MB, T, T),
        low(MB, T, T),
        full(2 * MB, T, T),
        full(2 * MB, T, T),
        full(2, T, T),
        index(2 * FB),
        index(FB + 2),
        index(2 * MB),
        index(MB + 2),
        index(2 * MB),
        index(FB),
        index(2),
        index(MB),
        low(2, T, T),
        low(2, T, T),
        low(2, T, T),
        low(2, T, T),
        low(2, T, T),
        low(2, T, T),
        low(2, T, T),
        low(2, T, T),
        pltpu.VMEM((8, T), jnp.int32),
        pltpu.VMEM((nx - 1, 8, T), jnp.int32),
        low(ny, T, T),
        low(T, T),
        low(nx - 1, T, T),
        low(nx - 1, T, T),
        low(T, T),
        low(T, T),
        low(T, T),
        low(nx - 1, T, T),
        low(ny - 1, T, T),
        low(ny - 1, T, T),
        full(4, T, T),
        low(8 * T, T),
        low(ndp - 1, rows1, T),
        low(ny, rows1, T),
        low(nx, rows1, T),
        low(8 * T, T),
        low(4 * T, T),
        low(ndp - 1, rows0, T),
        low(ny, rows0, T),
        low(nx, rows0, T),
        low(4 * T, T),
        full(3, 4, T, T),
        low(FB, T, T),
        pltpu.SemaphoreType.DMA((10,)),
        pltpu.SemaphoreType.DMA((copies,)),
        pltpu.SemaphoreType.DMA((copies,)),
    ]

    def body(*refs):
        kernel(nx, ndp, *refs)

    node_grad, weight_grad = pl.pallas_call(
        body,
        out_shape=(
            jax.ShapeDtypeStruct((FB, T, T), BF16),
            jax.ShapeDtypeStruct((3, 4, T, T), F32),
        ),
        in_specs=[
            anywhere,
            anywhere,
            anywhere,
            anywhere,
            smem,
            vmem,
            anywhere,
            smem,
            anywhere,
            smem,
            vmem,
            anywhere,
            smem,
            anywhere,
            smem,
        ],
        out_specs=(anywhere, anywhere),
        scratch_shapes=scratch,
        compiler_params=pltpu.CompilerParams(
            collective_id=0, has_side_effects=True, vmem_limit_bytes=48 * 1024 * 1024
        ),
        name="mesh_step",
    )(
        nodes.reshape(FB, T, T),
        cotangent.reshape(FB, T, T),
        weights,
        fine_tiles,
        fine_cols,
        fine_export,
        pool_tiles,
        pool_cols,
        mid_tiles,
        mid_cols,
        mid_export,
        top_pool_tiles,
        top_pool_cols,
        top_tiles,
        top_cols,
    )
    return node_grad.reshape(nodes.shape), weight_grad


def solution(mesh):
    nx, ndp = mesh.shape["dom"] // NY, mesh.shape["dp"]

    def run(*args):
        return on_device(nx, ndp, *args)

    return jax.shard_map(
        run,
        mesh=mesh,
        in_specs=(
            P("dp", "dom", None),
            P("dp", "dom", None),
            P(),
            P("dom", None, None, None),
            P("dom", None),
            P("dom", None, None),
            P("dom", None, None, None),
            P("dom", None),
            P("dom", None, None, None),
            P("dom", None),
            P("dom", None, None),
            P("dom", None, None, None),
            P("dom", None),
            P("dom", None, None, None),
            P("dom", None),
        ),
        out_specs=(P("dp", "dom", None), P()),
        check_vma=False,
    )
```

```python
import jax
import jax.numpy as jnp
from jax import lax
from jax.experimental import pallas as pl
from jax.experimental.pallas import tpu as pltpu
from jax.sharding import PartitionSpec as P

NY = 8
T = 128
FB, MB, TB = 16, 4, 1
GROUP = 4
F32, BF16 = jnp.float32, jnp.bfloat16
MESH = pl.DeviceIdType.MESH


def dot(a, b):
    return jnp.dot(a, b, preferred_element_type=F32)


def dot_bt(a, b):
    return lax.dot_general(a, b, (((1,), (1,)), ((), ())), preferred_element_type=F32)


def dot_at(a, b):
    return lax.dot_general(a, b, (((0,), (0,)), ((), ())), preferred_element_type=F32)


def logistic(s):
    return 0.5 * jnp.tanh(0.5 * s) + 0.5


def slope(s):
    q = logistic(s)
    return q * (1.0 + s * (1.0 - q))


def flat(blocks):
    return blocks.reshape(-1, T)


def tiled(rows):
    return rows.reshape(-1, T, T)


def picked_rows(export, source):
    columns = [
        jnp.transpose(jnp.broadcast_to(export[i : i + 1].astype(F32), (T, T))) for i in range(2)
    ]
    lane = lax.broadcasted_iota(jnp.int32, (T, T), 1).astype(F32)
    total = jnp.zeros((2 * T, T), F32)
    for pair in range(source.shape[0] // 2):
        onehot = jnp.concatenate(
            [
                jnp.concatenate(
                    [
                        jnp.where(column - T * (2 * pair + half) == lane, 1.0, 0.0)
                        for half in range(2)
                    ],
                    axis=1,
                )
                for column in columns
            ],
            axis=0,
        ).astype(BF16)
        total = total + dot(onehot, flat(source[2 * pair : 2 * pair + 2]))
    return tiled(total.astype(BF16))


def placed_rows(export, block, rows):
    row = lax.broadcasted_iota(jnp.int32, (T, T), 0) + block * T
    onehot = jnp.concatenate(
        [jnp.where(export[i : i + 1] == row, 1.0, 0.0) for i in range(2)], axis=1
    ).astype(BF16)
    return dot(onehot, rows)


def link(column, number, targets, prev, last):
    def before(s, carry):
        mine = column(s)
        best = jnp.int32(-1)
        for t in range(number):
            best = jnp.where((column(t) == mine) & (t < s), t, best)
        prev[s] = best
        return carry

    def final(j, carry):
        best = jnp.int32(-1)
        for t in range(number):
            best = jnp.where(column(t) == j, t, best)
        last[j] = best
        return carry

    lax.fori_loop(0, number, before, 0)
    lax.fori_loop(0, targets, final, 0)


def linked(pieces, at):
    return jnp.where(at >= 0, 1.0, 0.0) * pieces[jnp.maximum(at, 0)]


def chain(pieces, prev, number):
    def step(s, carry):
        pieces[s] = pieces[s] + linked(pieces, prev[s])
        return carry

    lax.fori_loop(0, number, step, 0)


def kernel(
    nx,
    ndp,
    nodes,
    cotangent,
    weights,
    fine_tiles,
    fine_cols,
    fine_export,
    pool_tiles,
    pool_cols,
    mid_tiles,
    mid_cols,
    mid_export,
    upper_tiles,
    upper_cols,
    top_tiles,
    top_cols,
    node_grad,
    weight_grad,
    fcols,
    fexport,
    pcols,
    mcols,
    mexport,
    ucols,
    tcols,
    S,
    COT,
    M,
    FT,
    PT,
    MT,
    UT,
    TT,
    PART,
    PRE1,
    PRE2,
    ACT1,
    ACT2,
    MSG,
    OUT,
    GN,
    GM,
    PIECE,
    MS,
    MPART,
    MPRE1,
    MPRE2,
    MACT1,
    MACT2,
    MMSG,
    MOUT,
    GRADM,
    GRADML,
    MGN,
    MGM,
    MPIECE,
    PPIECE,
    UPIECE,
    fprev,
    flast,
    mprev,
    mlast,
    pprev,
    plast,
    uprev,
    ulast,
    HALO_S,
    HALO_R,
    MHALO_S,
    MHALO_R,
    BACK_S,
    BACK_R,
    MBACK_S,
    MBACK_R,
    COL_S,
    COL_R,
    YG,
    PARTNER,
    SEL_S,
    SEL_R,
    P1_S,
    P1_R,
    P2_S,
    P2_R,
    PY_S,
    PY_R,
    WACC,
    W1_S,
    W1_R,
    W1_Y,
    W1_X,
    W1_O,
    W0_S,
    W0_R,
    W0_Y,
    W0_X,
    W0_O,
    ONODE,
    load_sem,
    send_sem,
    recv_sem,
):
    ny = NY
    ndom = nx * ny
    dp = lax.axis_index("dp")
    dom = lax.axis_index("dom")
    x = lax.div(dom, ny)
    y = lax.rem(dom, ny)

    left = (dp, lax.rem(dom + ndom - 1, ndom))
    right = (dp, lax.rem(dom + 1, ndom))

    def at_x(i):
        return (dp, lax.rem(x + i, nx) * ny + y)

    def at_y(i):
        return (dp, x * ny + lax.rem(y + i, ny))

    def at_dp(i):
        return (lax.rem(dp + i, ndp), dom)

    partners = (
        [left, right]
        + [at_x(i) for i in range(1, nx)]
        + [at_y(i) for i in range(1, ny)]
        + [at_dp(i) for i in range(1, ndp)]
    )
    barrier = pltpu.get_barrier_semaphore()
    for partner in partners:
        pl.semaphore_signal(barrier, inc=1, device_id=partner, device_id_type=MESH)

    started = []

    def send(src, dst, device):
        number = len(started)
        copy = pltpu.make_async_remote_copy(
            src_ref=src,
            dst_ref=dst,
            send_sem=send_sem.at[number],
            recv_sem=recv_sem.at[number],
            device_id=device,
            device_id_type=MESH,
        )
        copy.start()
        started.append(copy)
        return copy

    loads = []

    def load(src, dst):
        copy = pltpu.make_async_copy(src, dst, load_sem.at[len(loads)])
        copy.start()
        loads.append(copy)
        return copy

    got_nodes = load(nodes, S.at[pl.ds(0, FB)])
    got_export = load(fine_export, fexport)
    got_tcols = load(top_cols, tcols)
    got_pcols = load(pool_cols, pcols)
    got_ucols = load(upper_cols, ucols)
    got_cot = load(cotangent, COT)
    got_pool = load(pool_tiles, PT)
    got_upper = load(upper_tiles, UT)
    got_weights = load(weights, M)
    got_fine = load(fine_tiles, FT)
    got_fcols = load(fine_cols, fcols)
    got_mid = load(mid_tiles, MT)
    got_mcols = load(mid_cols, mcols)
    got_mexport = load(mid_export, mexport)
    got_top = load(top_tiles, TT)

    has_left = jnp.where(dom > 0, 1.0, 0.0).astype(F32)
    has_right = jnp.where(dom < ndom - 1, 1.0, 0.0).astype(F32)

    def level(l):
        return [M[l, i] for i in range(4)]

    got_export.wait()
    got_nodes.wait()
    HALO_S[...] = picked_rows(fexport[0], S)
    pl.semaphore_wait(barrier, len(partners))
    halo = [send(HALO_S.at[1], HALO_R.at[0], right), send(HALO_S.at[0], HALO_R.at[1], left)]
    got_tcols.wait()
    COL_S[...] = jnp.full((8, T), tcols[0, 2], jnp.int32)
    cols_sent = [send(COL_S, COL_R.at[i - 1], at_x(i)) for i in range(1, nx)]

    for copy in (got_cot, got_pool, got_pcols, got_upper, got_ucols):
        copy.wait()
    for m in range(MB):
        pooled = dot(PT[m, 0], COT[pcols[0, m]]) + dot(PT[m, 1], COT[pcols[1, m]])
        GRADM[m] = pooled
        GRADML[m] = pooled.astype(BF16)
    grad_top = dot(UT[0, 0], GRADML[ucols[0, 0]]) + dot(UT[0, 1], GRADML[ucols[0, 1]])
    for copy in (got_weights, got_fine, got_fcols):
        copy.wait()

    def fine_own(g, carry):
        base = g * GROUP
        m0 = M[0, 0]
        u = flat(S[pl.ds(base, GROUP)])
        PRE1[pl.ds(base, GROUP)] = tiled(dot(u, m0))
        for b in range(GROUP):
            PART[base + b] = dot(FT[base + b, 0], S[base + b])
        return carry

    lax.fori_loop(0, FB // GROUP, fine_own, 0)

    for copy in halo:
        copy.wait_recv()
    S[FB] = HALO_R[0] * has_left.astype(BF16)
    S[FB + 1] = HALO_R[1] * has_right.astype(BF16)

    def forward(u, v, own_pre, m):
        pre1 = own_pre + dot(v, m[1])
        act1 = (pre1 * logistic(pre1)).astype(BF16)
        pre2 = dot(act1, m[2])
        act2 = (pre2 * logistic(pre2)).astype(BF16)
        return pre1, act1, pre2, act2

    def fine_forward(g, carry):
        base = g * GROUP
        m = level(0)
        messages = []
        for b in range(GROUP):
            r = base + b
            messages.append(
                (
                    PART[r]
                    + dot(FT[r, 1], S[fcols[1, r]])
                    + dot(FT[r, 2], S[fcols[2, r]])
                ).astype(BF16)
            )
        v = jnp.concatenate(messages, axis=0)
        here = pl.ds(base, GROUP)
        u = flat(S[here])
        pre1, act1, pre2, act2 = forward(u, v, flat(PRE1[here]), m)
        MSG[here] = tiled(v)
        PRE1[here] = tiled(pre1)
        ACT1[here] = tiled(act1)
        PRE2[here] = tiled(pre2)
        ACT2[here] = tiled(act2)
        OUT[here] = tiled((u.astype(F32) + dot(act2, m[3])).astype(BF16))
        return carry

    lax.fori_loop(0, FB // GROUP, fine_forward, 0)

    for m in range(MB):
        MS[m] = (dot(PT[m, 0], OUT[pcols[0, m]]) + dot(PT[m, 1], OUT[pcols[1, m]])).astype(BF16)
    got_mexport.wait()
    MHALO_S[...] = picked_rows(mexport[0], MS[0:MB])
    mid_halo = [send(MHALO_S.at[1], MHALO_R.at[0], right), send(MHALO_S.at[0], MHALO_R.at[1], left)]
    got_mid.wait()
    got_mcols.wait()
    mm = level(1)
    mu = flat(MS[0:MB])
    MPRE1[...] = tiled(dot(mu, mm[0]))
    for r in range(MB):
        MPART[r] = dot(MT[r, 0], MS[r])
    got_top.wait()
    link(lambda s: ucols[0, s], 2, MB, uprev, ulast)
    for copy in mid_halo:
        copy.wait_recv()
    MS[MB] = MHALO_R[0] * has_left.astype(BF16)
    MS[MB + 1] = MHALO_R[1] * has_right.astype(BF16)
    mv = jnp.concatenate(
        [
            (
                MPART[r] + dot(MT[r, 1], MS[mcols[r, 1]]) + dot(MT[r, 2], MS[mcols[r, 2]])
            ).astype(BF16)
            for r in range(MB)
        ],
        axis=0,
    )
    pre1, act1, pre2, act2 = forward(mu, mv, flat(MPRE1[...]), mm)
    MOUT[...] = tiled((mu.astype(F32) + dot(act2, mm[3])).astype(BF16))
    top_in = (dot(UT[0, 0], MOUT[ucols[0, 0]]) + dot(UT[0, 1], MOUT[ucols[0, 1]])).astype(BF16)

    YG[0] = top_in
    along_y = [send(YG.at[0], YG.at[i], at_y(i)) for i in range(1, ny)]
    half = send(YG.at[0], PARTNER, at_x(nx // 2))
    MMSG[...] = tiled(mv)
    MACT1[...] = tiled(act1)
    MACT2[...] = tiled(act2)
    MPRE1[...] = tiled(slope(pre1))
    MPRE2[...] = tiled(slope(pre2))

    def fine_slopes(g, carry):
        here = pl.ds(g * 2, 2)
        PRE1[here] = slope(PRE1[here])
        PRE2[here] = slope(PRE2[here])
        return carry

    lax.fori_loop(0, FB // 2, fine_slopes, 0)
    tm = level(2)
    top_own = dot(top_in, tm[0])
    top_part = dot(TT[0, 0], top_in)
    for copy in cols_sent:
        copy.wait_recv()
    cols = [COL_S[0:1]] + [COL_R[i, 0:1] for i in range(nx - 1)]
    for copy in along_y:
        copy.wait_recv()

    def chosen(column):
        total = jnp.zeros((T, T), BF16)
        for k in range(ny):
            source = x * ny + lax.rem(y + ny - k, ny)
            total = total + jnp.where(column == source, 1.0, 0.0).astype(BF16) * YG[k]
        return total

    along_x = []
    for i in range(1, nx):
        SEL_S[i - 1] = chosen(cols[nx - i])
        along_x.append(send(SEL_S.at[i - 1], SEL_R.at[i - 1], at_x(i)))
    third = chosen(cols[0])
    half.wait_recv()
    top_part = top_part + dot(TT[0, 1], PARTNER[...])
    link(lambda s: pcols[lax.div(s, MB), lax.rem(s, MB)], 2 * MB, FB, pprev, plast)
    link(lambda s: mcols[lax.rem(s, MB), 1 + lax.div(s, MB)], 2 * MB, MB + 2, mprev, mlast)
    for copy in along_x:
        copy.wait_recv()
    for i in range(nx - 1):
        third = third + SEL_R[i]
    top_msg = (top_part + dot(TT[0, 2], third)).astype(BF16)
    pre1, act1, pre2, act2 = forward(top_in, top_msg, top_own, tm)

    def backward(g, slope1, slope2, m):
        gb = g.astype(BF16)
        gs = (dot_bt(gb, m[3]) * slope2).astype(BF16)
        gf = (dot_bt(gs, m[2]) * slope1).astype(BF16)
        return gb, gs, gf, dot_bt(gf, m[1]).astype(BF16)

    def terms(u, v, act1, act2, gb, gs, gf):
        return dot_at(u, gf), dot_at(v, gf), dot_at(act1, gs), dot_at(act2, gb)

    gb, gs, gf, gm = backward(grad_top, slope(pre1), slope(pre2), tm)
    P2_S[...] = dot_at(TT[0, 2], gm).astype(BF16)
    back_x = [send(P2_S, P2_R.at[i - 1], at_x(i)) for i in range(1, nx)]
    P1_S[...] = dot_at(TT[0, 1], gm).astype(BF16)
    back_half = send(P1_S, P1_R, at_x(nx // 2))
    grad_top_in = grad_top + dot_bt(gf, tm[0]) + dot_at(TT[0, 0], gm)
    for i, term in enumerate(terms(top_in, top_msg, act1, act2, gb, gs, gf)):
        W1_S[pl.ds((4 + i) * T, T)] = term.astype(BF16)
    for copy in back_x:
        copy.wait_recv()
    arrived = [P2_S[...].astype(F32)] + [P2_R[i].astype(F32) for i in range(nx - 1)]

    def summed(target):
        total = jnp.zeros((T, T), F32)
        for column, piece in zip(cols, arrived):
            total = total + jnp.where(column == target, 1.0, 0.0) * piece
        return total

    back_y = []
    for i in range(1, ny):
        PY_S[i - 1] = summed(x * ny + lax.rem(y + i, ny)).astype(BF16)
        back_y.append(send(PY_S.at[i - 1], PY_R.at[i - 1], at_y(i)))
    grad_top_in = grad_top_in + summed(dom)
    link(lambda s: fcols[1 + lax.div(s, FB), lax.rem(s, FB)], 2 * FB, FB + 2, fprev, flast)
    back_half.wait_recv()
    grad_top_in = grad_top_in + P1_R[...].astype(F32)
    for copy in back_y:
        copy.wait_recv()
    for i in range(ny - 1):
        grad_top_in = grad_top_in + PY_R[i].astype(F32)

    low = grad_top_in.astype(BF16)
    for s in range(2):
        UPIECE[s] = dot_at(UT[0, s], low)
    chain(UPIECE, uprev, 2)
    for m in range(MB):
        GRADM[m] = GRADM[m] + linked(UPIECE, ulast[m])
    g = flat(GRADM[...])
    gb, gs, gf, gm = backward(g, flat(MPRE1[...]), flat(MPRE2[...]), mm)
    MGM[...] = tiled(gm)
    for r in range(MB):
        MPIECE[r] = dot_at(MT[r, 1], MGM[r])
        MPIECE[MB + r] = dot_at(MT[r, 2], MGM[r])
    chain(MPIECE, mprev, 2 * MB)
    MBACK_S[0] = linked(MPIECE, mlast[MB]).astype(BF16)
    MBACK_S[1] = linked(MPIECE, mlast[MB + 1]).astype(BF16)
    mid_back = [send(MBACK_S.at[1], MBACK_R.at[0], right), send(MBACK_S.at[0], MBACK_R.at[1], left)]
    MGN[...] = tiled(g + dot_bt(gf, mm[0]))
    for r in range(MB):
        MGN[r] = MGN[r] + dot_at(MT[r, 0], MGM[r]) + linked(MPIECE, mlast[r])
    for i, term in enumerate(
        terms(flat(MS[0:MB]), flat(MMSG[...]), flat(MACT1[...]), flat(MACT2[...]), gb, gs, gf)
    ):
        W1_S[pl.ds(i * T, T)] = term.astype(BF16)

    def scattered(store, slots, rows):
        return [
            send(
                store.at[pl.ds(pl.multiple_of(at_dp(i)[0] * rows, rows), rows)],
                slots.at[i - 1],
                at_dp(i),
            )
            for i in range(1, ndp)
        ]

    def chunk_sum(copies, store, slots, rows):
        for copy in copies:
            copy.wait_recv()
        total = store[pl.ds(pl.multiple_of(dp * rows, rows), rows)].astype(F32)
        for i in range(ndp - 1):
            total = total + slots[i].astype(F32)
        return total.astype(BF16)

    def spread_y(value, slots):
        slots[y] = value
        return [send(slots.at[y], slots.at[y], at_y(i)) for i in range(1, ny)]

    def spread_x(value, slots):
        slots[x] = value
        return [send(slots.at[x], slots.at[x], at_x(i)) for i in range(1, nx)]

    def slot_sum(copies, slots, number):
        for copy in copies:
            copy.wait_recv()
        total = slots[0].astype(F32)
        for i in range(1, number):
            total = total + slots[i].astype(F32)
        return total.astype(BF16)

    def gathered(value, store, rows):
        mine = pl.ds(pl.multiple_of(dp * rows, rows), rows)
        store[mine] = value
        return [send(store.at[mine], store.at[mine], at_dp(i)) for i in range(1, ndp)]

    rows1 = 8 * T // ndp
    rows0 = 4 * T // ndp
    w1 = scattered(W1_S, W1_R, rows1)

    for copy in mid_back:
        copy.wait_recv()
    back_rows = jnp.concatenate(
        [MBACK_R[0] * has_left.astype(BF16), MBACK_R[1] * has_right.astype(BF16)], axis=0
    )
    for r in range(MB):
        MGN[r] = MGN[r] + placed_rows(mexport[0], r, back_rows)
    for m in range(MB):
        low = MGN[m].astype(BF16)
        for k in range(2):
            PPIECE[k * MB + m] = dot_at(PT[m, k], low)
    chain(PPIECE, pprev, 2 * MB)

    WACC[...] = jnp.zeros_like(WACC)

    def fine_backward(g, carry):
        base = g * GROUP
        here = pl.ds(base, GROUP)
        m = level(0)
        grad = jnp.concatenate(
            [COT[base + b].astype(F32) + linked(PPIECE, plast[base + b]) for b in range(GROUP)],
            axis=0,
        )
        gb, gs, gf, gm = backward(grad, flat(PRE1[here]), flat(PRE2[here]), m)
        GM[here] = tiled(gm)
        GN[here] = tiled(grad + dot_bt(gf, m[0]))
        for i, term in enumerate(
            terms(flat(S[here]), flat(MSG[here]), flat(ACT1[here]), flat(ACT2[here]), gb, gs, gf)
        ):
            WACC[i] = WACC[i] + term
        return carry

    lax.fori_loop(0, FB // GROUP, fine_backward, 0)
    W0_S[...] = flat(WACC[...]).astype(BF16)
    w0 = scattered(W0_S, W0_R, rows0)
    w1 = spread_y(chunk_sum(w1, W1_S, W1_R, rows1), W1_Y)

    def fine_pieces(g, carry):
        for b in range(2):
            r = g * 2 + b
            grad = GM[r]
            PIECE[r] = dot_at(FT[r, 1], grad)
            PIECE[FB + r] = dot_at(FT[r, 2], grad)
            GN[r] = GN[r] + dot_at(FT[r, 0], grad)
        return carry

    lax.fori_loop(0, FB // 2, fine_pieces, 0)
    chain(PIECE, fprev, 2 * FB)
    BACK_S[0] = linked(PIECE, flast[FB]).astype(BF16)
    BACK_S[1] = linked(PIECE, flast[FB + 1]).astype(BF16)
    back = [send(BACK_S.at[1], BACK_R.at[0], right), send(BACK_S.at[0], BACK_R.at[1], left)]
    w0 = spread_y(chunk_sum(w0, W0_S, W0_R, rows0), W0_Y)
    w1 = spread_x(slot_sum(w1, W1_Y, ny), W1_X)
    for copy in back:
        copy.wait_recv()
    w0 = spread_x(slot_sum(w0, W0_Y, ny), W0_X)
    w1 = gathered(slot_sum(w1, W1_X, nx), W1_O, rows1)
    back_rows = jnp.concatenate(
        [BACK_R[0] * has_left.astype(BF16), BACK_R[1] * has_right.astype(BF16)], axis=0
    )
    fexp = fexport[0]

    def finish(r, carry):
        ONODE[r] = (
            GN[r] + linked(PIECE, flast[r]) + placed_rows(fexp, r, back_rows)
        ).astype(BF16)
        return carry

    w0 = gathered(slot_sum(w0, W0_X, nx), W0_O, rows0)
    lax.fori_loop(0, FB, finish, 0)
    put_nodes = load(ONODE, node_grad)
    for copy in w1:
        copy.wait_recv()
    put_upper = load(W1_O, weight_grad.at[pl.ds(4 * T, 8 * T)])
    for copy in w0:
        copy.wait_recv()
    put_fine = load(W0_O, weight_grad.at[pl.ds(0, 4 * T)])
    for copy in started:
        copy.wait_send()
    put_nodes.wait()
    put_upper.wait()
    put_fine.wait()


def on_device(nx, ndp, *args):
    (
        nodes,
        cotangent,
        weights,
        fine_tiles,
        fine_cols,
        fine_export,
        pool_tiles,
        pool_cols,
        mid_tiles,
        mid_cols,
        mid_export,
        top_pool_tiles,
        top_pool_cols,
        top_tiles,
        top_cols,
    ) = args
    ny = NY
    anywhere = pl.BlockSpec(memory_space=pl.ANY)

    def low(*shape):
        return pltpu.VMEM(shape, BF16)

    def full(*shape):
        return pltpu.VMEM(shape, F32)

    def index(number):
        return pltpu.SMEM((number,), jnp.int32)

    rows1, rows0 = 8 * T // ndp, 4 * T // ndp
    copies = (
        4 * 2 + (nx - 1) * 3 + (ny - 1) * 2 + 2 + 2 * (2 * (ndp - 1) + (ny - 1) + (nx - 1))
    )
    scratch = [
        pltpu.SMEM((3, FB), jnp.int32),
        pltpu.VMEM((1, 2, T), jnp.int32),
        pltpu.SMEM((2, MB), jnp.int32),
        pltpu.SMEM((MB, 3), jnp.int32),
        pltpu.VMEM((1, 2, T), jnp.int32),
        pltpu.SMEM((1, 2), jnp.int32),
        pltpu.SMEM((1, 3), jnp.int32),
        low(FB + 2, T, T),
        low(FB, T, T),
        low(3, 4, T, T),
        low(FB, 3, T, T),
        low(MB, 2, T, T),
        low(MB, 3, T, T),
        low(1, 2, T, T),
        low(1, 3, T, T),
        full(FB, T, T),
        full(FB, T, T),
        full(FB, T, T),
        low(FB, T, T),
        low(FB, T, T),
        low(FB, T, T),
        low(FB, T, T),
        full(FB, T, T),
        low(FB, T, T),
        full(2 * FB, T, T),
        low(MB + 2, T, T),
        full(MB, T, T),
        full(MB, T, T),
        full(MB, T, T),
        low(MB, T, T),
        low(MB, T, T),
        low(MB, T, T),
        low(MB, T, T),
        full(MB, T, T),
        low(MB, T, T),
        full(MB, T, T),
        low(MB, T, T),
        full(2 * MB, T, T),
        full(2 * MB, T, T),
        full(2, T, T),
        index(2 * FB),
        index(FB + 2),
        index(2 * MB),
        index(MB + 2),
        index(2 * MB),
        index(FB),
        index(2),
        index(MB),
        low(2, T, T),
        low(2, T, T),
        low(2, T, T),
        low(2, T, T),
        low(2, T, T),
        low(2, T, T),
        low(2, T, T),
        low(2, T, T),
        pltpu.VMEM((8, T), jnp.int32),
        pltpu.VMEM((nx - 1, 8, T), jnp.int32),
        low(ny, T, T),
        low(T, T),
        low(nx - 1, T, T),
        low(nx - 1, T, T),
        low(T, T),
        low(T, T),
        low(T, T),
        low(nx - 1, T, T),
        low(ny - 1, T, T),
        low(ny - 1, T, T),
        full(4, T, T),
        low(8 * T, T),
        low(ndp - 1, rows1, T),
        low(ny, rows1, T),
        low(nx, rows1, T),
        low(8 * T, T),
        low(4 * T, T),
        low(ndp - 1, rows0, T),
        low(ny, rows0, T),
        low(nx, rows0, T),
        low(4 * T, T),
        low(FB, T, T),
        pltpu.SemaphoreType.DMA((20,)),
        pltpu.SemaphoreType.DMA((copies,)),
        pltpu.SemaphoreType.DMA((copies,)),
    ]

    def body(*refs):
        kernel(nx, ndp, *refs)

    node_grad, weight_grad = pl.pallas_call(
        body,
        out_shape=(
            jax.ShapeDtypeStruct((FB, T, T), BF16),
            jax.ShapeDtypeStruct((12 * T, T), BF16),
        ),
        in_specs=[anywhere] * 15,
        out_specs=(anywhere, anywhere),
        scratch_shapes=scratch,
        compiler_params=pltpu.CompilerParams(
            collective_id=0, has_side_effects=True, vmem_limit_bytes=64 * 1024 * 1024
        ),
        name="mesh_step",
    )(
        nodes.reshape(FB, T, T),
        cotangent.reshape(FB, T, T),
        weights,
        fine_tiles,
        fine_cols.T,
        fine_export,
        pool_tiles,
        pool_cols.T,
        mid_tiles,
        mid_cols,
        mid_export,
        top_pool_tiles,
        top_pool_cols,
        top_tiles,
        top_cols,
    )
    return node_grad.reshape(nodes.shape), weight_grad.reshape(weights.shape).astype(F32)


def solution(mesh):
    nx, ndp = mesh.shape["dom"] // NY, mesh.shape["dp"]

    def run(*args):
        return on_device(nx, ndp, *args)

    return jax.shard_map(
        run,
        mesh=mesh,
        in_specs=(
            P("dp", "dom", None),
            P("dp", "dom", None),
            P(),
            P("dom", None, None, None),
            P("dom", None),
            P("dom", None, None),
            P("dom", None, None, None),
            P("dom", None),
            P("dom", None, None, None),
            P("dom", None),
            P("dom", None, None),
            P("dom", None, None, None),
            P("dom", None),
            P("dom", None, None, None),
            P("dom", None),
        ),
        out_specs=(P("dp", "dom", None), P()),
        check_vma=False,
    )
```

```python
import jax
import jax.numpy as jnp
from jax import lax
from jax.experimental import pallas as pl
from jax.experimental.pallas import tpu as pltpu
from jax.sharding import PartitionSpec as P

NY = 8
NC = 2
T = 128
FB, MB, TB = 16, 4, 1
GROUP = 4
F32, BF16 = jnp.float32, jnp.bfloat16
MESH = pl.DeviceIdType.MESH


def dot(a, b):
    return jnp.dot(a, b, preferred_element_type=F32)


def dot_bt(a, b):
    return lax.dot_general(a, b, (((1,), (1,)), ((), ())), preferred_element_type=F32)


def dot_at(a, b):
    return lax.dot_general(a, b, (((0,), (0,)), ((), ())), preferred_element_type=F32)


def logistic(s):
    return 0.5 * jnp.tanh(0.5 * s) + 0.5


def slope(s):
    q = logistic(s)
    return q * (1.0 + s * (1.0 - q))


def far_first(number):
    return sorted(range(1, number), key=lambda i: -min(i, number - i))


def flat(blocks):
    return blocks.reshape(-1, T)


def tiled(rows):
    return rows.reshape(-1, T, T)


def picked_rows(export, source):
    columns = [
        jnp.transpose(jnp.broadcast_to(export[i : i + 1].astype(F32), (T, T))) for i in range(2)
    ]
    lane = lax.broadcasted_iota(jnp.int32, (T, T), 1).astype(F32)
    total = jnp.zeros((2 * T, T), F32)
    for pair in range(source.shape[0] // 2):
        onehot = jnp.concatenate(
            [
                jnp.concatenate(
                    [
                        jnp.where(column - T * (2 * pair + half) == lane, 1.0, 0.0)
                        for half in range(2)
                    ],
                    axis=1,
                )
                for column in columns
            ],
            axis=0,
        ).astype(BF16)
        total = total + dot(onehot, flat(source[2 * pair : 2 * pair + 2]))
    return tiled(total.astype(BF16))


def placed_rows(export, block, rows):
    row = lax.broadcasted_iota(jnp.int32, (T, T), 0) + block * T
    onehot = jnp.concatenate(
        [jnp.where(export[i : i + 1] == row, 1.0, 0.0) for i in range(2)], axis=1
    ).astype(BF16)
    return dot(onehot, rows)


def link(column, number, targets, prev, last):
    def before(s, carry):
        mine = column(s)
        best = jnp.int32(-1)
        for t in range(number):
            best = jnp.where((column(t) == mine) & (t < s), t, best)
        prev[s] = best
        return carry

    def final(j, carry):
        best = jnp.int32(-1)
        for t in range(number):
            best = jnp.where(column(t) == j, t, best)
        last[j] = best
        return carry

    lax.fori_loop(0, number, before, 0)
    lax.fori_loop(0, targets, final, 0)


def linked(pieces, at):
    return jnp.where(at >= 0, 1.0, 0.0) * pieces[jnp.maximum(at, 0)]


def chain(pieces, prev, number):
    def step(s, carry):
        pieces[s] = pieces[s] + linked(pieces, prev[s])
        return carry

    lax.fori_loop(0, number, step, 0)


def kernel(
    nx,
    ndp,
    nodes,
    cotangent,
    weights,
    fine_tiles,
    fine_cols,
    fine_export,
    pool_tiles,
    pool_cols,
    mid_tiles,
    mid_cols,
    mid_export,
    upper_tiles,
    upper_cols,
    top_tiles,
    top_cols,
    node_grad,
    weight_grad,
    fcols,
    fexport,
    pcols,
    mcols,
    mexport,
    ucols,
    tcols,
    S,
    COT,
    M,
    FT,
    PT,
    MT,
    UT,
    TT,
    PART,
    PRE1,
    PRE2,
    ACT1,
    ACT2,
    MSG,
    OUT,
    GN,
    GM,
    PIECE,
    MS,
    MPART,
    MPRE1,
    MPRE2,
    MACT1,
    MACT2,
    MMSG,
    MOUT,
    GRADM,
    GRADML,
    MGN,
    MGM,
    MPIECE,
    PPIECE,
    UPIECE,
    fprev,
    flast,
    mprev,
    mlast,
    pprev,
    plast,
    uprev,
    ulast,
    HALO_S,
    HALO_R,
    MHALO_S,
    MHALO_R,
    BACK_S,
    BACK_R,
    MBACK_S,
    MBACK_R,
    COL_S,
    COL_R,
    YG,
    PARTNER,
    SEL_S,
    SEL_R,
    P1_S,
    P1_R,
    P2_S,
    P2_R,
    PY_S,
    PY_R,
    WACC,
    W_S,
    W_R,
    W_Y,
    W_Z,
    W_O,
    GF,
    ONODE,
    load_sem,
    send_sem,
    recv_sem,
):
    ny = NY
    ndom = nx * ny
    dp = lax.axis_index("dp")
    dom = lax.axis_index("dom")
    x = lax.div(dom, ny)
    y = lax.rem(dom, ny)
    nz = ndp // NC
    z = lax.div(dp, NC)
    core = lax.rem(dp, NC)

    left = (dp, lax.rem(dom + ndom - 1, ndom))
    right = (dp, lax.rem(dom + 1, ndom))

    def at_x(i):
        return (dp, lax.rem(x + i, nx) * ny + y)

    def at_y(i):
        return (dp, x * ny + lax.rem(y + i, ny))

    def at_z(i):
        return (lax.rem(z + i, nz) * NC + core, dom)

    def at_cx(c, i):
        return (z * NC + lax.rem(core + c, NC), lax.rem(x + i, nx) * ny + y)

    x_order = far_first(nx)
    y_order = far_first(ny)
    z_order = far_first(nz)
    cx_order = [(c, i) for c in range(NC) for i in range(nx) if (c, i) != (0, 0)]
    partners = (
        [left, right]
        + [at_cx(c, i) for c, i in cx_order]
        + [at_y(i) for i in y_order]
        + [at_z(i) for i in z_order]
    )
    barrier = pltpu.get_barrier_semaphore()
    for partner in partners:
        pl.semaphore_signal(barrier, inc=1, device_id=partner, device_id_type=MESH)

    started = []

    def send(src, dst, device):
        number = len(started)
        copy = pltpu.make_async_remote_copy(
            src_ref=src,
            dst_ref=dst,
            send_sem=send_sem.at[number],
            recv_sem=recv_sem.at[number],
            device_id=device,
            device_id_type=MESH,
        )
        copy.start()
        started.append(copy)
        return copy

    loads = []

    def load(src, dst):
        copy = pltpu.make_async_copy(src, dst, load_sem.at[len(loads)])
        copy.start()
        loads.append(copy)
        return copy

    got_nodes = load(nodes, S.at[pl.ds(0, FB)])
    got_export = load(fine_export, fexport)
    got_tcols = load(top_cols, tcols)
    got_pcols = load(pool_cols, pcols)
    got_ucols = load(upper_cols, ucols)
    got_cot = load(cotangent, COT)
    got_pool = load(pool_tiles, PT)
    got_upper = load(upper_tiles, UT)
    got_weights = load(weights, M)
    got_fine = load(fine_tiles, FT)
    got_fcols = load(fine_cols, fcols)
    got_mid = load(mid_tiles, MT)
    got_mcols = load(mid_cols, mcols)
    got_mexport = load(mid_export, mexport)
    got_top = load(top_tiles, TT)

    has_left = jnp.where(dom > 0, 1.0, 0.0).astype(F32)
    has_right = jnp.where(dom < ndom - 1, 1.0, 0.0).astype(F32)

    def level(l):
        return [M[l, i] for i in range(4)]

    rows = 4 * T // (NC * nx)

    def chunk(c, i):
        number = lax.rem(core + c, NC) * nx + lax.rem(x + i, nx)
        return pl.ds(pl.multiple_of(number * rows, rows), rows)

    def scattered(store, slots):
        return [
            send(store.at[chunk(c, i)], slots.at[n], at_cx(c, i))
            for n, (c, i) in enumerate(cx_order)
        ]

    def scatter_sum(copies, store, slots):
        for copy in copies:
            copy.wait_recv()
        total = store[chunk(0, 0)].astype(F32)
        for n in range(len(cx_order)):
            total = total + slots[n].astype(F32)
        return total.astype(BF16)

    def shown_y(value, slots):
        slots[y] = value
        return [send(slots.at[y], slots.at[y], at_y(i)) for i in y_order]

    def shown_z(value, slots):
        slots[z] = value
        return [send(slots.at[z], slots.at[z], at_z(i)) for i in z_order]

    def slot_sum(copies, slots, number):
        for copy in copies:
            copy.wait_recv()
        total = slots[0].astype(F32)
        for i in range(1, number):
            total = total + slots[i].astype(F32)
        return total.astype(BF16)

    def gathered(store):
        mine = store.at[chunk(0, 0)]
        return [send(mine, mine, at_cx(c, i)) for c, i in cx_order]

    got_export.wait()
    got_nodes.wait()
    HALO_S[...] = picked_rows(fexport[0], S.at[pl.ds(0, FB)])
    pl.semaphore_wait(barrier, len(partners))
    halo = [send(HALO_S.at[1], HALO_R.at[0], right), send(HALO_S.at[0], HALO_R.at[1], left)]
    got_tcols.wait()
    COL_S[...] = jnp.full((8, T), tcols[0, 2], jnp.int32)
    cols_sent = [send(COL_S, COL_R.at[i - 1], at_x(i)) for i in range(1, nx)]

    for copy in (got_cot, got_pool, got_pcols, got_upper, got_ucols):
        copy.wait()
    for m in range(MB):
        pooled = dot(PT[m, 0], COT[pcols[0, m]]) + dot(PT[m, 1], COT[pcols[1, m]])
        GRADM[m] = pooled
        GRADML[m] = pooled.astype(BF16)
    grad_top = dot(UT[0, 0], GRADML[ucols[0, 0]]) + dot(UT[0, 1], GRADML[ucols[0, 1]])
    for copy in (got_weights, got_fine, got_fcols):
        copy.wait()

    def fine_own(g, carry):
        base = g * GROUP
        m0 = M[0, 0]
        u = flat(S[pl.ds(base, GROUP)])
        PRE1[pl.ds(base, GROUP)] = tiled(dot(u, m0))
        for b in range(GROUP):
            PART[base + b] = dot(FT[base + b, 0], S[base + b])
        return carry

    lax.fori_loop(0, FB // GROUP, fine_own, 0)

    for copy in halo:
        copy.wait_recv()
    S[FB] = HALO_R[0] * has_left.astype(BF16)
    S[FB + 1] = HALO_R[1] * has_right.astype(BF16)

    def forward(u, v, own_pre, m):
        pre1 = own_pre + dot(v, m[1])
        act1 = (pre1 * logistic(pre1)).astype(BF16)
        pre2 = dot(act1, m[2])
        act2 = (pre2 * logistic(pre2)).astype(BF16)
        return pre1, act1, pre2, act2

    def fine_forward(g, carry):
        base = g * GROUP
        m = level(0)
        messages = []
        for b in range(GROUP):
            r = base + b
            messages.append(
                (
                    PART[r]
                    + dot(FT[r, 1], S[fcols[1, r]])
                    + dot(FT[r, 2], S[fcols[2, r]])
                ).astype(BF16)
            )
        v = jnp.concatenate(messages, axis=0)
        here = pl.ds(base, GROUP)
        u = flat(S[here])
        pre1, act1, pre2, act2 = forward(u, v, flat(PRE1[here]), m)
        MSG[here] = tiled(v)
        PRE1[here] = tiled(pre1)
        ACT1[here] = tiled(act1)
        PRE2[here] = tiled(pre2)
        ACT2[here] = tiled(act2)
        OUT[here] = tiled((u.astype(F32) + dot(act2, m[3])).astype(BF16))
        return carry

    lax.fori_loop(0, FB // GROUP, fine_forward, 0)

    for m in range(MB):
        MS[m] = (dot(PT[m, 0], OUT[pcols[0, m]]) + dot(PT[m, 1], OUT[pcols[1, m]])).astype(BF16)
    got_mexport.wait()
    MHALO_S[...] = picked_rows(mexport[0], MS[0:MB])
    mid_halo = [send(MHALO_S.at[1], MHALO_R.at[0], right), send(MHALO_S.at[0], MHALO_R.at[1], left)]
    got_mid.wait()
    got_mcols.wait()
    mm = level(1)
    mu = flat(MS[0:MB])
    MPRE1[...] = tiled(dot(mu, mm[0]))
    for r in range(MB):
        MPART[r] = dot(MT[r, 0], MS[r])
    got_top.wait()
    link(lambda s: ucols[0, s], 2, MB, uprev, ulast)
    for copy in mid_halo:
        copy.wait_recv()
    MS[MB] = MHALO_R[0] * has_left.astype(BF16)
    MS[MB + 1] = MHALO_R[1] * has_right.astype(BF16)
    mv = jnp.concatenate(
        [
            (
                MPART[r] + dot(MT[r, 1], MS[mcols[r, 1]]) + dot(MT[r, 2], MS[mcols[r, 2]])
            ).astype(BF16)
            for r in range(MB)
        ],
        axis=0,
    )
    pre1, act1, pre2, act2 = forward(mu, mv, flat(MPRE1[...]), mm)
    MOUT[...] = tiled((mu.astype(F32) + dot(act2, mm[3])).astype(BF16))
    top_in = (dot(UT[0, 0], MOUT[ucols[0, 0]]) + dot(UT[0, 1], MOUT[ucols[0, 1]])).astype(BF16)

    YG[0] = top_in
    along_y = [send(YG.at[0], YG.at[i], at_y(i)) for i in y_order]
    half = send(YG.at[0], PARTNER, at_x(nx // 2))
    MMSG[...] = tiled(mv)
    MACT1[...] = tiled(act1)
    MACT2[...] = tiled(act2)
    MPRE1[...] = tiled(slope(pre1))
    MPRE2[...] = tiled(slope(pre2))

    def fine_slopes(g, carry):
        here = pl.ds(g * 2, 2)
        PRE1[here] = slope(PRE1[here])
        PRE2[here] = slope(PRE2[here])
        return carry

    lax.fori_loop(0, FB // 2, fine_slopes, 0)
    tm = level(2)
    top_own = dot(top_in, tm[0])
    top_part = dot(TT[0, 0], top_in)
    for copy in cols_sent:
        copy.wait_recv()
    cols = [COL_S[0:1]] + [COL_R[i, 0:1] for i in range(nx - 1)]
    for copy in along_y:
        copy.wait_recv()

    def chosen(column):
        total = jnp.zeros((T, T), BF16)
        for k in range(ny):
            source = x * ny + lax.rem(y + ny - k, ny)
            total = total + jnp.where(column == source, 1.0, 0.0).astype(BF16) * YG[k]
        return total

    along_x = []
    for i in x_order:
        SEL_S[i - 1] = chosen(cols[nx - i])
        along_x.append(send(SEL_S.at[i - 1], SEL_R.at[i - 1], at_x(i)))
    third = chosen(cols[0])
    half.wait_recv()
    top_part = top_part + dot(TT[0, 1], PARTNER[...])
    link(lambda s: pcols[lax.div(s, MB), lax.rem(s, MB)], 2 * MB, FB, pprev, plast)
    link(lambda s: mcols[lax.rem(s, MB), 1 + lax.div(s, MB)], 2 * MB, MB + 2, mprev, mlast)
    for copy in along_x:
        copy.wait_recv()
    for i in range(nx - 1):
        third = third + SEL_R[i]
    top_msg = (top_part + dot(TT[0, 2], third)).astype(BF16)
    pre1, act1, pre2, act2 = forward(top_in, top_msg, top_own, tm)

    def back_to_first(g, slope1, slope2, m):
        gb = g.astype(BF16)
        gs = (dot_bt(gb, m[3]) * slope2).astype(BF16)
        gf = (dot_bt(gs, m[2]) * slope1).astype(BF16)
        return gb, gs, gf

    def backward(g, slope1, slope2, m):
        gb, gs, gf = back_to_first(g, slope1, slope2, m)
        return gb, gs, gf, dot_bt(gf, m[1]).astype(BF16)

    def terms(u, v, act1, act2, gb, gs, gf):
        return dot_at(u, gf), dot_at(v, gf), dot_at(act1, gs), dot_at(act2, gb)

    gb, gs, gf, gm = backward(grad_top, slope(pre1), slope(pre2), tm)
    P2_S[...] = dot_at(TT[0, 2], gm).astype(BF16)
    back_x = [send(P2_S, P2_R.at[i - 1], at_x(i)) for i in x_order]
    P1_S[...] = dot_at(TT[0, 1], gm).astype(BF16)
    back_half = send(P1_S, P1_R, at_x(nx // 2))
    grad_top_in = grad_top + dot_bt(gf, tm[0]) + dot_at(TT[0, 0], gm)
    for i, term in enumerate(terms(top_in, top_msg, act1, act2, gb, gs, gf)):
        W_S[2, pl.ds(i * T, T)] = term.astype(BF16)
    for copy in back_x:
        copy.wait_recv()
    arrived = [P2_S[...].astype(F32)] + [P2_R[i].astype(F32) for i in range(nx - 1)]

    def summed(target):
        total = jnp.zeros((T, T), F32)
        for column, piece in zip(cols, arrived):
            total = total + jnp.where(column == target, 1.0, 0.0) * piece
        return total

    back_y = []
    for i in y_order:
        PY_S[i - 1] = summed(x * ny + lax.rem(y + i, ny)).astype(BF16)
        back_y.append(send(PY_S.at[i - 1], PY_R.at[i - 1], at_y(i)))
    top_sum = scattered(W_S.at[2], W_R.at[2])
    grad_top_in = grad_top_in + summed(dom)
    link(lambda s: fcols[1 + lax.div(s, FB), lax.rem(s, FB)], 2 * FB, FB + 2, fprev, flast)
    back_half.wait_recv()
    grad_top_in = grad_top_in + P1_R[...].astype(F32)
    for copy in back_y:
        copy.wait_recv()
    for i in range(ny - 1):
        grad_top_in = grad_top_in + PY_R[i].astype(F32)

    top_sum = shown_z(scatter_sum(top_sum, W_S.at[2], W_R.at[2]), W_Z.at[2])

    low = grad_top_in.astype(BF16)
    for s in range(2):
        UPIECE[s] = dot_at(UT[0, s], low)
    chain(UPIECE, uprev, 2)
    for m in range(MB):
        GRADM[m] = GRADM[m] + linked(UPIECE, ulast[m])
    g = flat(GRADM[...])
    gb, gs, gf, gm = backward(g, flat(MPRE1[...]), flat(MPRE2[...]), mm)
    MGM[...] = tiled(gm)
    for r in range(MB):
        MPIECE[r] = dot_at(MT[r, 1], MGM[r])
        MPIECE[MB + r] = dot_at(MT[r, 2], MGM[r])
    chain(MPIECE, mprev, 2 * MB)
    MBACK_S[0] = linked(MPIECE, mlast[MB]).astype(BF16)
    MBACK_S[1] = linked(MPIECE, mlast[MB + 1]).astype(BF16)
    mid_back = [send(MBACK_S.at[1], MBACK_R.at[0], right), send(MBACK_S.at[0], MBACK_R.at[1], left)]
    MGN[...] = tiled(g + dot_bt(gf, mm[0]))
    for r in range(MB):
        MGN[r] = MGN[r] + dot_at(MT[r, 0], MGM[r]) + linked(MPIECE, mlast[r])
    for i, term in enumerate(
        terms(flat(MS[0:MB]), flat(MMSG[...]), flat(MACT1[...]), flat(MACT2[...]), gb, gs, gf)
    ):
        W_S[1, pl.ds(i * T, T)] = term.astype(BF16)

    mid_sum = scattered(W_S.at[1], W_R.at[1])

    for copy in mid_back:
        copy.wait_recv()
    back_rows = jnp.concatenate(
        [MBACK_R[0] * has_left.astype(BF16), MBACK_R[1] * has_right.astype(BF16)], axis=0
    )
    for r in range(MB):
        MGN[r] = MGN[r] + placed_rows(mexport[0], r, back_rows)
    for m in range(MB):
        low = MGN[m].astype(BF16)
        for k in range(2):
            PPIECE[k * MB + m] = dot_at(PT[m, k], low)
    chain(PPIECE, pprev, 2 * MB)

    top_sum = shown_y(slot_sum(top_sum, W_Z.at[2], nz), W_Y.at[2])

    WACC[...] = jnp.zeros_like(WACC)

    def fine_backward(g, carry):
        base = g * GROUP
        here = pl.ds(base, GROUP)
        m = level(0)
        grad = jnp.concatenate(
            [COT[base + b].astype(F32) + linked(PPIECE, plast[base + b]) for b in range(GROUP)],
            axis=0,
        )
        gb, gs, gf = back_to_first(grad, flat(PRE1[here]), flat(PRE2[here]), m)
        GN[here] = tiled(grad)
        GF[here] = tiled(gf)
        for i, term in enumerate(
            terms(flat(S[here]), flat(MSG[here]), flat(ACT1[here]), flat(ACT2[here]), gb, gs, gf)
        ):
            WACC[i] = WACC[i] + term
        return carry

    lax.fori_loop(0, FB // GROUP, fine_backward, 0)
    W_S[0] = flat(WACC[...]).astype(BF16)
    fine_sum = scattered(W_S.at[0], W_R.at[0])
    mid_sum = shown_y(scatter_sum(mid_sum, W_S.at[1], W_R.at[1]), W_Y.at[1])

    def fine_rows(g, carry):
        here = pl.ds(g * GROUP, GROUP)
        gf = flat(GF[here])
        GM[here] = tiled(dot_bt(gf, M[0, 1]).astype(BF16))
        GN[here] = GN[here] + tiled(dot_bt(gf, M[0, 0]))
        return carry

    lax.fori_loop(0, FB // GROUP, fine_rows, 0)

    def fine_pieces(g, carry):
        for b in range(2):
            r = g * 2 + b
            grad = GM[r]
            PIECE[r] = dot_at(FT[r, 1], grad)
            PIECE[FB + r] = dot_at(FT[r, 2], grad)
            GN[r] = GN[r] + dot_at(FT[r, 0], grad)
        return carry

    lax.fori_loop(0, FB // 2, fine_pieces, 0)
    chain(PIECE, fprev, 2 * FB)
    BACK_S[0] = linked(PIECE, flast[FB]).astype(BF16)
    BACK_S[1] = linked(PIECE, flast[FB + 1]).astype(BF16)
    back = [send(BACK_S.at[1], BACK_R.at[0], right), send(BACK_S.at[0], BACK_R.at[1], left)]

    half = rows // 2
    value = scatter_sum(fine_sum, W_S.at[0], W_R.at[0])
    first = shown_y(value[0:half], W_Y.at[0, :, 0:half])
    second = shown_z(value[half:rows], W_Z.at[0, :, half:rows])
    mid_sum = shown_z(slot_sum(mid_sum, W_Y.at[1], ny), W_Z.at[1])
    W_O[2, chunk(0, 0)] = slot_sum(top_sum, W_Y.at[2], ny)
    top_sum = gathered(W_O.at[2])

    for copy in back:
        copy.wait_recv()
    back_rows = jnp.concatenate(
        [BACK_R[0] * has_left.astype(BF16), BACK_R[1] * has_right.astype(BF16)], axis=0
    )
    fexp = fexport[0]

    def finish(r, carry):
        ONODE[r] = (
            GN[r] + linked(PIECE, flast[r]) + placed_rows(fexp, r, back_rows)
        ).astype(BF16)
        return carry

    lax.fori_loop(0, FB // 2, finish, 0)
    first = shown_z(slot_sum(first, W_Y.at[0, :, 0:half], ny), W_Z.at[0, :, 0:half])
    second = shown_y(slot_sum(second, W_Z.at[0, :, half:rows], nz), W_Y.at[0, :, half:rows])
    W_O[1, chunk(0, 0)] = slot_sum(mid_sum, W_Z.at[1], nz)
    mid_sum = gathered(W_O.at[1])
    lax.fori_loop(FB // 2, FB, finish, 0)
    put_nodes = load(ONODE, node_grad)
    W_O[0, chunk(0, 0)] = jnp.concatenate(
        [
            slot_sum(first, W_Z.at[0, :, 0:half], nz),
            slot_sum(second, W_Y.at[0, :, half:rows], ny),
        ],
        axis=0,
    )
    fine_sum = gathered(W_O.at[0])
    for copy in top_sum + mid_sum:
        copy.wait_recv()
    put_upper = load(W_O.at[pl.ds(1, 2)], weight_grad.at[pl.ds(1, 2)])
    for copy in fine_sum:
        copy.wait_recv()
    put_fine = load(W_O.at[0], weight_grad.at[0])
    for copy in started:
        copy.wait_send()
    put_nodes.wait()
    put_upper.wait()
    put_fine.wait()


def write_kernel(node_in, weight_in, node_out, weight_out, low, full, sem):
    nodes = pltpu.make_async_copy(node_in, node_out, sem.at[0])
    nodes.start()
    fetch = [pltpu.make_async_copy(weight_in.at[l], low.at[l], sem.at[1 + l]) for l in range(3)]
    put = [pltpu.make_async_copy(full.at[l], weight_out.at[l], sem.at[4 + l]) for l in range(3)]
    for copy in fetch:
        copy.start()
    for l in range(3):
        fetch[l].wait()
        full[l] = low[l].astype(F32)
        put[l].start()
    for copy in put:
        copy.wait()
    nodes.wait()


def written(node_grad, weight_grad):
    anywhere = pl.BlockSpec(memory_space=pl.ANY)
    return pl.pallas_call(
        write_kernel,
        out_shape=(
            jax.ShapeDtypeStruct(node_grad.shape, BF16),
            jax.ShapeDtypeStruct(weight_grad.shape, F32),
        ),
        in_specs=[anywhere] * 2,
        out_specs=(anywhere, anywhere),
        scratch_shapes=[
            pltpu.VMEM(weight_grad.shape, BF16),
            pltpu.VMEM(weight_grad.shape, F32),
            pltpu.SemaphoreType.DMA((7,)),
        ],
        compiler_params=pltpu.CompilerParams(vmem_limit_bytes=64 * 1024 * 1024),
        name="write_results",
    )(node_grad, weight_grad)


def on_device(nx, ndp, *args):
    (
        nodes,
        cotangent,
        weights,
        fine_tiles,
        fine_cols,
        fine_export,
        pool_tiles,
        pool_cols,
        mid_tiles,
        mid_cols,
        mid_export,
        top_pool_tiles,
        top_pool_cols,
        top_tiles,
        top_cols,
    ) = args
    ny = NY
    anywhere = pl.BlockSpec(memory_space=pl.ANY)

    def low(*shape):
        return pltpu.VMEM(shape, BF16)

    def full(*shape):
        return pltpu.VMEM(shape, F32)

    def index(number):
        return pltpu.SMEM((number,), jnp.int32)

    nz = ndp // NC
    rows = 4 * T // (NC * nx)
    copies = (
        4 * 2
        + (nx - 1) * 3
        + (ny - 1) * 2
        + 2
        + 3 * 2 * (NC * nx - 1)
        + 4 * (ny - 1 + nz - 1)
    )
    scratch = [
        pltpu.SMEM((3, FB), jnp.int32),
        pltpu.VMEM((1, 2, T), jnp.int32),
        pltpu.SMEM((2, MB), jnp.int32),
        pltpu.SMEM((MB, 3), jnp.int32),
        pltpu.VMEM((1, 2, T), jnp.int32),
        pltpu.SMEM((1, 2), jnp.int32),
        pltpu.SMEM((1, 3), jnp.int32),
        low(FB + 2, T, T),
        low(FB, T, T),
        low(3, 4, T, T),
        low(FB, 3, T, T),
        low(MB, 2, T, T),
        low(MB, 3, T, T),
        low(1, 2, T, T),
        low(1, 3, T, T),
        full(FB, T, T),
        full(FB, T, T),
        full(FB, T, T),
        low(FB, T, T),
        low(FB, T, T),
        low(FB, T, T),
        low(FB, T, T),
        full(FB, T, T),
        low(FB, T, T),
        full(2 * FB, T, T),
        low(MB + 2, T, T),
        full(MB, T, T),
        full(MB, T, T),
        full(MB, T, T),
        low(MB, T, T),
        low(MB, T, T),
        low(MB, T, T),
        low(MB, T, T),
        full(MB, T, T),
        low(MB, T, T),
        full(MB, T, T),
        low(MB, T, T),
        full(2 * MB, T, T),
        full(2 * MB, T, T),
        full(2, T, T),
        index(2 * FB),
        index(FB + 2),
        index(2 * MB),
        index(MB + 2),
        index(2 * MB),
        index(FB),
        index(2),
        index(MB),
        low(2, T, T),
        low(2, T, T),
        low(2, T, T),
        low(2, T, T),
        low(2, T, T),
        low(2, T, T),
        low(2, T, T),
        low(2, T, T),
        pltpu.VMEM((8, T), jnp.int32),
        pltpu.VMEM((nx - 1, 8, T), jnp.int32),
        low(ny, T, T),
        low(T, T),
        low(nx - 1, T, T),
        low(nx - 1, T, T),
        low(T, T),
        low(T, T),
        low(T, T),
        low(nx - 1, T, T),
        low(ny - 1, T, T),
        low(ny - 1, T, T),
        full(4, T, T),
        low(3, 4 * T, T),
        low(3, NC * nx - 1, rows, T),
        low(3, ny, rows, T),
        low(3, nz, rows, T),
        low(3, 4 * T, T),
        low(FB, T, T),
        low(FB, T, T),
        pltpu.SemaphoreType.DMA((20,)),
        pltpu.SemaphoreType.DMA((copies,)),
        pltpu.SemaphoreType.DMA((copies,)),
    ]

    def body(*refs):
        kernel(nx, ndp, *refs)

    node_grad, weight_grad = pl.pallas_call(
        body,
        out_shape=(
            jax.ShapeDtypeStruct((FB, T, T), BF16),
            jax.ShapeDtypeStruct((3, 4 * T, T), BF16),
        ),
        in_specs=[anywhere] * 15,
        out_specs=(anywhere, anywhere),
        scratch_shapes=scratch,
        compiler_params=pltpu.CompilerParams(
            collective_id=0, has_side_effects=True, vmem_limit_bytes=64 * 1024 * 1024
        ),
        name="mesh_step",
    )(
        nodes.reshape(FB, T, T),
        cotangent.reshape(FB, T, T),
        weights,
        fine_tiles,
        fine_cols.T,
        fine_export,
        pool_tiles,
        pool_cols.T,
        mid_tiles,
        mid_cols,
        mid_export,
        top_pool_tiles,
        top_pool_cols,
        top_tiles,
        top_cols,
    )
    node_grad, weight_grad = written(node_grad, weight_grad)
    return node_grad.reshape(nodes.shape), weight_grad.reshape(weights.shape)


def solution(mesh):
    nx, ndp = mesh.shape["dom"] // NY, mesh.shape["dp"]

    def run(*args):
        return on_device(nx, ndp, *args)

    return jax.shard_map(
        run,
        mesh=mesh,
        in_specs=(
            P("dp", "dom", None),
            P("dp", "dom", None),
            P(),
            P("dom", None, None, None),
            P("dom", None),
            P("dom", None, None),
            P("dom", None, None, None),
            P("dom", None),
            P("dom", None, None, None),
            P("dom", None),
            P("dom", None, None),
            P("dom", None, None, None),
            P("dom", None),
            P("dom", None, None, None),
            P("dom", None),
        ),
        out_specs=(P("dp", "dom", None), P()),
        check_vma=False,
    )
```

```python
import jax
import jax.numpy as jnp
from jax import lax
from jax.experimental import pallas as pl
from jax.experimental.pallas import tpu as pltpu
from jax.sharding import PartitionSpec as P

NY = 8
NC = 2
T = 128
FB, MB, TB = 16, 4, 1
GROUP = 4
F32, BF16 = jnp.float32, jnp.bfloat16
MESH = pl.DeviceIdType.MESH


def dot(a, b):
    return jnp.dot(a, b, preferred_element_type=F32)


def dot_bt(a, b):
    return lax.dot_general(a, b, (((1,), (1,)), ((), ())), preferred_element_type=F32)


def dot_at(a, b):
    return lax.dot_general(a, b, (((0,), (0,)), ((), ())), preferred_element_type=F32)


def logistic(s):
    return 0.5 * jnp.tanh(0.5 * s) + 0.5


def slope(s):
    q = logistic(s)
    return q * (1.0 + s * (1.0 - q))


def far_first(number):
    return sorted(range(1, number), key=lambda i: -min(i, number - i))


def flat(blocks):
    return blocks.reshape(-1, T)


def tiled(rows):
    return rows.reshape(-1, T, T)


def picked_rows(export, source):
    columns = [
        jnp.transpose(jnp.broadcast_to(export[i : i + 1].astype(F32), (T, T))) for i in range(2)
    ]
    lane = lax.broadcasted_iota(jnp.int32, (T, T), 1).astype(F32)
    total = jnp.zeros((2 * T, T), F32)
    for pair in range(source.shape[0] // 2):
        onehot = jnp.concatenate(
            [
                jnp.concatenate(
                    [
                        jnp.where(column - T * (2 * pair + half) == lane, 1.0, 0.0)
                        for half in range(2)
                    ],
                    axis=1,
                )
                for column in columns
            ],
            axis=0,
        ).astype(BF16)
        total = total + dot(onehot, flat(source[2 * pair : 2 * pair + 2]))
    return tiled(total.astype(BF16))


def placed_rows(export, block, rows):
    row = lax.broadcasted_iota(jnp.int32, (T, T), 0) + block * T
    onehot = jnp.concatenate(
        [jnp.where(export[i : i + 1] == row, 1.0, 0.0) for i in range(2)], axis=1
    ).astype(BF16)
    return dot(onehot, rows)


def link(column, number, targets, prev, last):
    def before(s, carry):
        mine = column(s)
        best = jnp.int32(-1)
        for t in range(number):
            best = jnp.where((column(t) == mine) & (t < s), t, best)
        prev[s] = best
        return carry

    def final(j, carry):
        best = jnp.int32(-1)
        for t in range(number):
            best = jnp.where(column(t) == j, t, best)
        last[j] = best
        return carry

    lax.fori_loop(0, number, before, 0)
    lax.fori_loop(0, targets, final, 0)


def linked(pieces, at):
    return jnp.where(at >= 0, 1.0, 0.0) * pieces[jnp.maximum(at, 0)]


def chain(pieces, prev, number):
    def step(s, carry):
        pieces[s] = pieces[s] + linked(pieces, prev[s])
        return carry

    lax.fori_loop(0, number, step, 0)


def kernel(
    nx,
    ndp,
    nodes,
    cotangent,
    weights,
    fine_tiles,
    fine_cols,
    fine_export,
    pool_tiles,
    pool_cols,
    mid_tiles,
    mid_cols,
    mid_export,
    upper_tiles,
    upper_cols,
    top_tiles,
    top_cols,
    node_grad,
    weight_grad,
    fcols,
    fexport,
    pcols,
    mcols,
    mexport,
    ucols,
    tcols,
    S,
    COT,
    M,
    FT,
    PT,
    MT,
    UT,
    TT,
    PART,
    PRE1,
    PRE2,
    ACT1,
    ACT2,
    MSG,
    OUT,
    GN,
    GM,
    PIECE,
    MS,
    MPART,
    MPRE1,
    MPRE2,
    MACT1,
    MACT2,
    MMSG,
    MOUT,
    GRADM,
    GRADML,
    MGN,
    MGM,
    MPIECE,
    PPIECE,
    UPIECE,
    fprev,
    flast,
    mprev,
    mlast,
    pprev,
    plast,
    uprev,
    ulast,
    HALO_S,
    HALO_R,
    MHALO_S,
    MHALO_R,
    BACK_S,
    BACK_R,
    MBACK_S,
    MBACK_R,
    COL_S,
    COL_R,
    YG,
    PARTNER,
    SEL_S,
    SEL_R,
    P1_S,
    P1_R,
    P2_S,
    P2_R,
    PY_S,
    PY_R,
    WACC,
    W_S,
    W_R,
    W_Y,
    W_Z,
    W_O,
    GF,
    ONODE,
    load_sem,
    send_sem,
    recv_sem,
):
    ny = NY
    ndom = nx * ny
    dp = lax.axis_index("dp")
    dom = lax.axis_index("dom")
    x = lax.div(dom, ny)
    y = lax.rem(dom, ny)
    nz = ndp // NC
    z = lax.div(dp, NC)
    core = lax.rem(dp, NC)

    left = (dp, lax.rem(dom + ndom - 1, ndom))
    right = (dp, lax.rem(dom + 1, ndom))

    def at_x(i):
        return (dp, lax.rem(x + i, nx) * ny + y)

    def at_y(i):
        return (dp, x * ny + lax.rem(y + i, ny))

    def at_z(i):
        return (lax.rem(z + i, nz) * NC + core, dom)

    def at_cx(c, i):
        return (z * NC + lax.rem(core + c, NC), lax.rem(x + i, nx) * ny + y)

    x_order = far_first(nx)
    y_order = far_first(ny)
    z_order = far_first(nz)
    cx_order = [(c, i) for c in range(NC) for i in range(nx) if (c, i) != (0, 0)]
    partners = (
        [left, right]
        + [at_cx(c, i) for c, i in cx_order]
        + [at_y(i) for i in y_order]
        + [at_z(i) for i in z_order]
    )
    started = []

    def send(src, dst, device):
        number = len(started)
        copy = pltpu.make_async_remote_copy(
            src_ref=src,
            dst_ref=dst,
            send_sem=send_sem.at[number],
            recv_sem=recv_sem.at[number],
            device_id=device,
            device_id_type=MESH,
        )
        copy.start()
        started.append(copy)
        return copy

    loads = []

    def load(src, dst):
        copy = pltpu.make_async_copy(src, dst, load_sem.at[len(loads)])
        copy.start()
        loads.append(copy)
        return copy

    got_nodes = load(nodes, S.at[pl.ds(0, FB)])
    got_export = load(fine_export, fexport)
    barrier = pltpu.get_barrier_semaphore()
    for partner in partners:
        pl.semaphore_signal(barrier, inc=1, device_id=partner, device_id_type=MESH)
    got_tcols = load(top_cols, tcols)
    got_pcols = load(pool_cols, pcols)
    got_ucols = load(upper_cols, ucols)
    got_cot = load(cotangent, COT)
    got_pool = load(pool_tiles, PT)
    got_upper = load(upper_tiles, UT)
    got_weights = load(weights, M)
    got_fine = load(fine_tiles, FT)
    got_fcols = load(fine_cols, fcols)
    got_mid = load(mid_tiles, MT)
    got_mcols = load(mid_cols, mcols)
    got_mexport = load(mid_export, mexport)
    got_top = load(top_tiles, TT)

    has_left = jnp.where(dom > 0, 1.0, 0.0).astype(F32)
    has_right = jnp.where(dom < ndom - 1, 1.0, 0.0).astype(F32)

    def level(l):
        return [M[l, i] for i in range(4)]

    rows = 4 * T // (NC * nx)

    def chunk(c, i):
        number = lax.rem(core + c, NC) * nx + lax.rem(x + i, nx)
        return pl.ds(pl.multiple_of(number * rows, rows), rows)

    def scattered(store, slots):
        return [
            send(store.at[chunk(c, i)], slots.at[n], at_cx(c, i))
            for n, (c, i) in enumerate(cx_order)
        ]

    def scatter_sum(copies, store, slots):
        for copy in copies:
            copy.wait_recv()
        total = store[chunk(0, 0)].astype(F32)
        for n in range(len(cx_order)):
            total = total + slots[n].astype(F32)
        return total.astype(BF16)

    def shown_y(value, slots):
        slots[y] = value
        return [send(slots.at[y], slots.at[y], at_y(i)) for i in y_order]

    def shown_z(value, slots):
        slots[z] = value
        return [send(slots.at[z], slots.at[z], at_z(i)) for i in z_order]

    def slot_sum(copies, slots, number):
        for copy in copies:
            copy.wait_recv()
        total = slots[0].astype(F32)
        for i in range(1, number):
            total = total + slots[i].astype(F32)
        return total.astype(BF16)

    def gathered(store):
        mine = store.at[chunk(0, 0)]
        return [send(mine, mine, at_cx(c, i)) for c, i in cx_order]

    got_export.wait()
    got_nodes.wait()
    HALO_S[...] = picked_rows(fexport[0], S.at[pl.ds(0, FB)])
    pl.semaphore_wait(barrier, len(partners))
    halo = [send(HALO_S.at[1], HALO_R.at[0], right), send(HALO_S.at[0], HALO_R.at[1], left)]
    got_tcols.wait()
    COL_S[...] = jnp.full((8, T), tcols[0, 2], jnp.int32)
    cols_sent = [send(COL_S, COL_R.at[i - 1], at_x(i)) for i in range(1, nx)]

    for copy in (got_cot, got_pool, got_pcols, got_upper, got_ucols):
        copy.wait()
    for m in range(MB):
        pooled = dot(PT[m, 0], COT[pcols[0, m]]) + dot(PT[m, 1], COT[pcols[1, m]])
        GRADM[m] = pooled
        GRADML[m] = pooled.astype(BF16)
    grad_top = dot(UT[0, 0], GRADML[ucols[0, 0]]) + dot(UT[0, 1], GRADML[ucols[0, 1]])
    for copy in (got_weights, got_fine, got_fcols):
        copy.wait()

    def fine_own(g, carry):
        base = g * GROUP
        m0 = M[0, 0]
        u = flat(S[pl.ds(base, GROUP)])
        PRE1[pl.ds(base, GROUP)] = tiled(dot(u, m0))
        for b in range(GROUP):
            PART[base + b] = dot(FT[base + b, 0], S[base + b])
        return carry

    lax.fori_loop(0, FB // GROUP, fine_own, 0)

    for copy in halo:
        copy.wait_recv()
    S[FB] = HALO_R[0] * has_left.astype(BF16)
    S[FB + 1] = HALO_R[1] * has_right.astype(BF16)

    def forward(u, v, own_pre, m):
        pre1 = own_pre + dot(v, m[1])
        act1 = (pre1 * logistic(pre1)).astype(BF16)
        pre2 = dot(act1, m[2])
        act2 = (pre2 * logistic(pre2)).astype(BF16)
        return pre1, act1, pre2, act2

    def fine_forward(g, carry):
        base = g * GROUP
        m = level(0)
        messages = []
        for b in range(GROUP):
            r = base + b
            messages.append(
                (
                    PART[r]
                    + dot(FT[r, 1], S[fcols[1, r]])
                    + dot(FT[r, 2], S[fcols[2, r]])
                ).astype(BF16)
            )
        v = jnp.concatenate(messages, axis=0)
        here = pl.ds(base, GROUP)
        u = flat(S[here])
        pre1, act1, pre2, act2 = forward(u, v, flat(PRE1[here]), m)
        MSG[here] = tiled(v)
        PRE1[here] = tiled(pre1)
        ACT1[here] = tiled(act1)
        PRE2[here] = tiled(pre2)
        ACT2[here] = tiled(act2)
        OUT[here] = tiled((u.astype(F32) + dot(act2, m[3])).astype(BF16))
        return carry

    lax.fori_loop(0, FB // GROUP, fine_forward, 0)

    for m in range(MB):
        MS[m] = (dot(PT[m, 0], OUT[pcols[0, m]]) + dot(PT[m, 1], OUT[pcols[1, m]])).astype(BF16)
    got_mexport.wait()
    MHALO_S[...] = picked_rows(mexport[0], MS[0:MB])
    mid_halo = [send(MHALO_S.at[1], MHALO_R.at[0], right), send(MHALO_S.at[0], MHALO_R.at[1], left)]
    got_mid.wait()
    got_mcols.wait()
    mm = level(1)
    mu = flat(MS[0:MB])
    MPRE1[...] = tiled(dot(mu, mm[0]))
    for r in range(MB):
        MPART[r] = dot(MT[r, 0], MS[r])
    got_top.wait()
    link(lambda s: ucols[0, s], 2, MB, uprev, ulast)
    for copy in mid_halo:
        copy.wait_recv()
    MS[MB] = MHALO_R[0] * has_left.astype(BF16)
    MS[MB + 1] = MHALO_R[1] * has_right.astype(BF16)
    mv = jnp.concatenate(
        [
            (
                MPART[r] + dot(MT[r, 1], MS[mcols[r, 1]]) + dot(MT[r, 2], MS[mcols[r, 2]])
            ).astype(BF16)
            for r in range(MB)
        ],
        axis=0,
    )
    pre1, act1, pre2, act2 = forward(mu, mv, flat(MPRE1[...]), mm)
    MOUT[...] = tiled((mu.astype(F32) + dot(act2, mm[3])).astype(BF16))
    top_in = (dot(UT[0, 0], MOUT[ucols[0, 0]]) + dot(UT[0, 1], MOUT[ucols[0, 1]])).astype(BF16)

    YG[0] = top_in
    along_y = [send(YG.at[0], YG.at[i], at_y(i)) for i in y_order]
    half = send(YG.at[0], PARTNER, at_x(nx // 2))
    MMSG[...] = tiled(mv)
    MACT1[...] = tiled(act1)
    MACT2[...] = tiled(act2)
    MPRE1[...] = tiled(slope(pre1))
    MPRE2[...] = tiled(slope(pre2))

    def fine_slopes(g, carry):
        here = pl.ds(g * 2, 2)
        PRE1[here] = slope(PRE1[here])
        PRE2[here] = slope(PRE2[here])
        return carry

    lax.fori_loop(0, FB // 2, fine_slopes, 0)
    tm = level(2)
    top_own = dot(top_in, tm[0])
    top_part = dot(TT[0, 0], top_in)
    for copy in cols_sent:
        copy.wait_recv()
    cols = [COL_S[0:1]] + [COL_R[i, 0:1] for i in range(nx - 1)]
    for copy in along_y:
        copy.wait_recv()

    def chosen(column):
        total = jnp.zeros((T, T), BF16)
        for k in range(ny):
            source = x * ny + lax.rem(y + ny - k, ny)
            total = total + jnp.where(column == source, 1.0, 0.0).astype(BF16) * YG[k]
        return total

    along_x = []
    for i in x_order:
        SEL_S[i - 1] = chosen(cols[nx - i])
        along_x.append(send(SEL_S.at[i - 1], SEL_R.at[i - 1], at_x(i)))
    third = chosen(cols[0])
    half.wait_recv()
    top_part = top_part + dot(TT[0, 1], PARTNER[...])
    link(lambda s: pcols[lax.div(s, MB), lax.rem(s, MB)], 2 * MB, FB, pprev, plast)
    link(lambda s: mcols[lax.rem(s, MB), 1 + lax.div(s, MB)], 2 * MB, MB + 2, mprev, mlast)
    for copy in along_x:
        copy.wait_recv()
    for i in range(nx - 1):
        third = third + SEL_R[i]
    top_msg = (top_part + dot(TT[0, 2], third)).astype(BF16)
    pre1, act1, pre2, act2 = forward(top_in, top_msg, top_own, tm)

    def back_to_first(g, slope1, slope2, m):
        gb = g.astype(BF16)
        gs = (dot_bt(gb, m[3]) * slope2).astype(BF16)
        gf = (dot_bt(gs, m[2]) * slope1).astype(BF16)
        return gb, gs, gf

    def backward(g, slope1, slope2, m):
        gb, gs, gf = back_to_first(g, slope1, slope2, m)
        return gb, gs, gf, dot_bt(gf, m[1]).astype(BF16)

    def terms(u, v, act1, act2, gb, gs, gf):
        return dot_at(u, gf), dot_at(v, gf), dot_at(act1, gs), dot_at(act2, gb)

    gb, gs, gf, gm = backward(grad_top, slope(pre1), slope(pre2), tm)
    P2_S[...] = dot_at(TT[0, 2], gm).astype(BF16)
    back_x = [send(P2_S, P2_R.at[i - 1], at_x(i)) for i in x_order]
    P1_S[...] = dot_at(TT[0, 1], gm).astype(BF16)
    back_half = send(P1_S, P1_R, at_x(nx // 2))
    grad_top_in = grad_top + dot_bt(gf, tm[0]) + dot_at(TT[0, 0], gm)
    for i, term in enumerate(terms(top_in, top_msg, act1, act2, gb, gs, gf)):
        W_S[2, pl.ds(i * T, T)] = term.astype(BF16)
    for copy in back_x:
        copy.wait_recv()
    arrived = [P2_S[...].astype(F32)] + [P2_R[i].astype(F32) for i in range(nx - 1)]

    def summed(target):
        total = jnp.zeros((T, T), F32)
        for column, piece in zip(cols, arrived):
            total = total + jnp.where(column == target, 1.0, 0.0) * piece
        return total

    back_y = []
    for i in y_order:
        PY_S[i - 1] = summed(x * ny + lax.rem(y + i, ny)).astype(BF16)
        back_y.append(send(PY_S.at[i - 1], PY_R.at[i - 1], at_y(i)))
    top_sum = scattered(W_S.at[2], W_R.at[2])
    grad_top_in = grad_top_in + summed(dom)
    link(lambda s: fcols[1 + lax.div(s, FB), lax.rem(s, FB)], 2 * FB, FB + 2, fprev, flast)
    back_half.wait_recv()
    grad_top_in = grad_top_in + P1_R[...].astype(F32)
    for copy in back_y:
        copy.wait_recv()
    for i in range(ny - 1):
        grad_top_in = grad_top_in + PY_R[i].astype(F32)

    top_sum = shown_z(scatter_sum(top_sum, W_S.at[2], W_R.at[2]), W_Z.at[2])

    low = grad_top_in.astype(BF16)
    for s in range(2):
        UPIECE[s] = dot_at(UT[0, s], low)
    chain(UPIECE, uprev, 2)
    for m in range(MB):
        GRADM[m] = GRADM[m] + linked(UPIECE, ulast[m])
    g = flat(GRADM[...])
    gb, gs, gf, gm = backward(g, flat(MPRE1[...]), flat(MPRE2[...]), mm)
    MGM[...] = tiled(gm)
    for r in range(MB):
        MPIECE[r] = dot_at(MT[r, 1], MGM[r])
        MPIECE[MB + r] = dot_at(MT[r, 2], MGM[r])
    chain(MPIECE, mprev, 2 * MB)
    MBACK_S[0] = linked(MPIECE, mlast[MB]).astype(BF16)
    MBACK_S[1] = linked(MPIECE, mlast[MB + 1]).astype(BF16)
    mid_back = [send(MBACK_S.at[1], MBACK_R.at[0], right), send(MBACK_S.at[0], MBACK_R.at[1], left)]
    MGN[...] = tiled(g + dot_bt(gf, mm[0]))
    for r in range(MB):
        MGN[r] = MGN[r] + dot_at(MT[r, 0], MGM[r]) + linked(MPIECE, mlast[r])
    for i, term in enumerate(
        terms(flat(MS[0:MB]), flat(MMSG[...]), flat(MACT1[...]), flat(MACT2[...]), gb, gs, gf)
    ):
        W_S[1, pl.ds(i * T, T)] = term.astype(BF16)

    mid_sum = scattered(W_S.at[1], W_R.at[1])

    for copy in mid_back:
        copy.wait_recv()
    top_sum = shown_y(slot_sum(top_sum, W_Z.at[2], nz), W_Y.at[2])
    back_rows = jnp.concatenate(
        [MBACK_R[0] * has_left.astype(BF16), MBACK_R[1] * has_right.astype(BF16)], axis=0
    )
    for r in range(MB):
        MGN[r] = MGN[r] + placed_rows(mexport[0], r, back_rows)
    for m in range(MB):
        low = MGN[m].astype(BF16)
        for k in range(2):
            PPIECE[k * MB + m] = dot_at(PT[m, k], low)
    chain(PPIECE, pprev, 2 * MB)

    WACC[...] = jnp.zeros_like(WACC)

    def fine_backward(g, carry):
        base = g * GROUP
        here = pl.ds(base, GROUP)
        m = level(0)
        grad = jnp.concatenate(
            [COT[base + b].astype(F32) + linked(PPIECE, plast[base + b]) for b in range(GROUP)],
            axis=0,
        )
        gb, gs, gf = back_to_first(grad, flat(PRE1[here]), flat(PRE2[here]), m)
        GN[here] = tiled(grad)
        GF[here] = tiled(gf)
        for i, term in enumerate(
            terms(flat(S[here]), flat(MSG[here]), flat(ACT1[here]), flat(ACT2[here]), gb, gs, gf)
        ):
            WACC[i] = WACC[i] + term
        return carry

    lax.fori_loop(0, FB // GROUP // 2, fine_backward, 0)
    mid_sum = shown_z(scatter_sum(mid_sum, W_S.at[1], W_R.at[1]), W_Z.at[1])
    lax.fori_loop(FB // GROUP // 2, FB // GROUP, fine_backward, 0)
    W_S[0] = flat(WACC[...]).astype(BF16)
    fine_sum = scattered(W_S.at[0], W_R.at[0])

    def fine_rows(g, carry):
        here = pl.ds(g * GROUP, GROUP)
        gf = flat(GF[here])
        GM[here] = tiled(dot_bt(gf, M[0, 1]).astype(BF16))
        GN[here] = GN[here] + tiled(dot_bt(gf, M[0, 0]))
        return carry

    lax.fori_loop(0, FB // GROUP, fine_rows, 0)

    def fine_pieces(g, carry):
        for b in range(2):
            r = g * 2 + b
            grad = GM[r]
            PIECE[r] = dot_at(FT[r, 1], grad)
            PIECE[FB + r] = dot_at(FT[r, 2], grad)
            GN[r] = GN[r] + dot_at(FT[r, 0], grad)
        return carry

    lax.fori_loop(0, FB // 2, fine_pieces, 0)
    chain(PIECE, fprev, 2 * FB)
    BACK_S[0] = linked(PIECE, flast[FB]).astype(BF16)
    BACK_S[1] = linked(PIECE, flast[FB + 1]).astype(BF16)
    back = [send(BACK_S.at[1], BACK_R.at[0], right), send(BACK_S.at[0], BACK_R.at[1], left)]

    half = rows // 2
    value = scatter_sum(fine_sum, W_S.at[0], W_R.at[0])
    first = shown_y(value[0:half], W_Y.at[0, :, 0:half])
    second = shown_z(value[half:rows], W_Z.at[0, :, half:rows])
    W_O[2, chunk(0, 0)] = slot_sum(top_sum, W_Y.at[2], ny)
    top_sum = gathered(W_O.at[2])
    mid_sum = shown_y(slot_sum(mid_sum, W_Z.at[1], nz), W_Y.at[1])

    for copy in back:
        copy.wait_recv()
    back_rows = jnp.concatenate(
        [BACK_R[0] * has_left.astype(BF16), BACK_R[1] * has_right.astype(BF16)], axis=0
    )
    fexp = fexport[0]

    def finish(r, carry):
        ONODE[r] = (
            GN[r] + linked(PIECE, flast[r]) + placed_rows(fexp, r, back_rows)
        ).astype(BF16)
        return carry

    lax.fori_loop(0, FB, finish, 0)
    first = shown_z(slot_sum(first, W_Y.at[0, :, 0:half], ny), W_Z.at[0, :, 0:half])
    second = shown_y(slot_sum(second, W_Z.at[0, :, half:rows], nz), W_Y.at[0, :, half:rows])
    put_nodes = load(ONODE, node_grad)
    W_O[1, chunk(0, 0)] = slot_sum(mid_sum, W_Y.at[1], ny)
    mid_sum = gathered(W_O.at[1])
    W_O[0, chunk(0, 0)] = jnp.concatenate(
        [
            slot_sum(first, W_Z.at[0, :, 0:half], nz),
            slot_sum(second, W_Y.at[0, :, half:rows], ny),
        ],
        axis=0,
    )
    fine_sum = gathered(W_O.at[0])
    for copy in top_sum + mid_sum:
        copy.wait_recv()
    put_upper = load(W_O.at[pl.ds(1, 2)], weight_grad.at[pl.ds(1, 2)])
    for copy in fine_sum:
        copy.wait_recv()
    put_fine = load(W_O.at[0], weight_grad.at[0])
    for copy in started:
        copy.wait_send()
    put_nodes.wait()
    put_upper.wait()
    put_fine.wait()


def write_kernel(node_in, weight_in, node_out, weight_out, nodes, low, full, sem):
    fetch = [pltpu.make_async_copy(weight_in.at[l], low.at[l], sem.at[l]) for l in range(3)]
    put = [pltpu.make_async_copy(full.at[l], weight_out.at[l], sem.at[3 + l]) for l in range(3)]
    node_fetch = pltpu.make_async_copy(node_in, nodes, sem.at[6])
    node_put = pltpu.make_async_copy(nodes, node_out, sem.at[7])
    for copy in fetch:
        copy.start()
    node_fetch.start()
    for l in range(3):
        fetch[l].wait()
        full[l] = low[l].astype(F32)
        put[l].start()
    node_fetch.wait()
    node_put.start()
    for copy in put:
        copy.wait()
    node_put.wait()


def written(node_grad, weight_grad):
    anywhere = pl.BlockSpec(memory_space=pl.ANY)
    return pl.pallas_call(
        write_kernel,
        out_shape=(
            jax.ShapeDtypeStruct(node_grad.shape, BF16),
            jax.ShapeDtypeStruct(weight_grad.shape, F32),
        ),
        in_specs=[anywhere] * 2,
        out_specs=(anywhere, anywhere),
        scratch_shapes=[
            pltpu.VMEM(node_grad.shape, BF16),
            pltpu.VMEM(weight_grad.shape, BF16),
            pltpu.VMEM(weight_grad.shape, F32),
            pltpu.SemaphoreType.DMA((8,)),
        ],
        compiler_params=pltpu.CompilerParams(vmem_limit_bytes=64 * 1024 * 1024),
        name="write_results",
    )(node_grad, weight_grad)


def on_device(nx, ndp, *args):
    (
        nodes,
        cotangent,
        weights,
        fine_tiles,
        fine_cols,
        fine_export,
        pool_tiles,
        pool_cols,
        mid_tiles,
        mid_cols,
        mid_export,
        top_pool_tiles,
        top_pool_cols,
        top_tiles,
        top_cols,
    ) = args
    ny = NY
    anywhere = pl.BlockSpec(memory_space=pl.ANY)

    def low(*shape):
        return pltpu.VMEM(shape, BF16)

    def full(*shape):
        return pltpu.VMEM(shape, F32)

    def index(number):
        return pltpu.SMEM((number,), jnp.int32)

    nz = ndp // NC
    rows = 4 * T // (NC * nx)
    copies = (
        4 * 2
        + (nx - 1) * 3
        + (ny - 1) * 2
        + 2
        + 3 * 2 * (NC * nx - 1)
        + 4 * (ny - 1 + nz - 1)
    )
    scratch = [
        pltpu.SMEM((3, FB), jnp.int32),
        pltpu.VMEM((1, 2, T), jnp.int32),
        pltpu.SMEM((2, MB), jnp.int32),
        pltpu.SMEM((MB, 3), jnp.int32),
        pltpu.VMEM((1, 2, T), jnp.int32),
        pltpu.SMEM((1, 2), jnp.int32),
        pltpu.SMEM((1, 3), jnp.int32),
        low(FB + 2, T, T),
        low(FB, T, T),
        low(3, 4, T, T),
        low(FB, 3, T, T),
        low(MB, 2, T, T),
        low(MB, 3, T, T),
        low(1, 2, T, T),
        low(1, 3, T, T),
        full(FB, T, T),
        full(FB, T, T),
        full(FB, T, T),
        low(FB, T, T),
        low(FB, T, T),
        low(FB, T, T),
        low(FB, T, T),
        full(FB, T, T),
        low(FB, T, T),
        full(2 * FB, T, T),
        low(MB + 2, T, T),
        full(MB, T, T),
        full(MB, T, T),
        full(MB, T, T),
        low(MB, T, T),
        low(MB, T, T),
        low(MB, T, T),
        low(MB, T, T),
        full(MB, T, T),
        low(MB, T, T),
        full(MB, T, T),
        low(MB, T, T),
        full(2 * MB, T, T),
        full(2 * MB, T, T),
        full(2, T, T),
        index(2 * FB),
        index(FB + 2),
        index(2 * MB),
        index(MB + 2),
        index(2 * MB),
        index(FB),
        index(2),
        index(MB),
        low(2, T, T),
        low(2, T, T),
        low(2, T, T),
        low(2, T, T),
        low(2, T, T),
        low(2, T, T),
        low(2, T, T),
        low(2, T, T),
        pltpu.VMEM((8, T), jnp.int32),
        pltpu.VMEM((nx - 1, 8, T), jnp.int32),
        low(ny, T, T),
        low(T, T),
        low(nx - 1, T, T),
        low(nx - 1, T, T),
        low(T, T),
        low(T, T),
        low(T, T),
        low(nx - 1, T, T),
        low(ny - 1, T, T),
        low(ny - 1, T, T),
        full(4, T, T),
        low(3, 4 * T, T),
        low(3, NC * nx - 1, rows, T),
        low(3, ny, rows, T),
        low(3, nz, rows, T),
        low(3, 4 * T, T),
        low(FB, T, T),
        low(FB, T, T),
        pltpu.SemaphoreType.DMA((20,)),
        pltpu.SemaphoreType.DMA((copies,)),
        pltpu.SemaphoreType.DMA((copies,)),
    ]

    def body(*refs):
        kernel(nx, ndp, *refs)

    node_grad, weight_grad = pl.pallas_call(
        body,
        out_shape=(
            jax.ShapeDtypeStruct((FB, T, T), BF16),
            jax.ShapeDtypeStruct((3, 4 * T, T), BF16),
        ),
        in_specs=[anywhere] * 15,
        out_specs=(anywhere, anywhere),
        scratch_shapes=scratch,
        compiler_params=pltpu.CompilerParams(
            collective_id=0, has_side_effects=True, vmem_limit_bytes=64 * 1024 * 1024
        ),
        name="mesh_step",
    )(
        nodes.reshape(FB, T, T),
        cotangent.reshape(FB, T, T),
        weights,
        fine_tiles,
        fine_cols.T,
        fine_export,
        pool_tiles,
        pool_cols.T,
        mid_tiles,
        mid_cols,
        mid_export,
        top_pool_tiles,
        top_pool_cols,
        top_tiles,
        top_cols,
    )
    node_grad, weight_grad = written(node_grad, weight_grad)
    return node_grad.reshape(nodes.shape), weight_grad.reshape(weights.shape)


def solution(mesh):
    nx, ndp = mesh.shape["dom"] // NY, mesh.shape["dp"]

    def run(*args):
        return on_device(nx, ndp, *args)

    return jax.shard_map(
        run,
        mesh=mesh,
        in_specs=(
            P("dp", "dom", None),
            P("dp", "dom", None),
            P(),
            P("dom", None, None, None),
            P("dom", None),
            P("dom", None, None),
            P("dom", None, None, None),
            P("dom", None),
            P("dom", None, None, None),
            P("dom", None),
            P("dom", None, None),
            P("dom", None, None, None),
            P("dom", None),
            P("dom", None, None, None),
            P("dom", None),
        ),
        out_specs=(P("dp", "dom", None), P()),
        check_vma=False,
    )
```

```python
import jax
import jax.numpy as jnp
from jax import lax
from jax.experimental import pallas as pl
from jax.experimental.pallas import tpu as pltpu
from jax.sharding import PartitionSpec as P

NY = 8
NC = 2
T = 128
FB, MB, TB = 16, 4, 1
GROUP = 4
F32, BF16 = jnp.float32, jnp.bfloat16
MESH = pl.DeviceIdType.MESH


def dot(a, b):
    return jnp.dot(a, b, preferred_element_type=F32)


def dot_bt(a, b):
    return lax.dot_general(a, b, (((1,), (1,)), ((), ())), preferred_element_type=F32)


def dot_at(a, b):
    return lax.dot_general(a, b, (((0,), (0,)), ((), ())), preferred_element_type=F32)


def logistic(s):
    return 0.5 * jnp.tanh(0.5 * s) + 0.5


def slope(s):
    q = logistic(s)
    return q * (1.0 + s * (1.0 - q))


def far_first(number):
    return sorted(range(1, number), key=lambda i: -min(i, number - i))


def flat(blocks):
    return blocks.reshape(-1, T)


def tiled(rows):
    return rows.reshape(-1, T, T)


def picked_rows(export, source):
    columns = [
        jnp.transpose(jnp.broadcast_to(export[i : i + 1].astype(F32), (T, T))) for i in range(2)
    ]
    lane = lax.broadcasted_iota(jnp.int32, (T, T), 1).astype(F32)
    total = jnp.zeros((2 * T, T), F32)
    for pair in range(source.shape[0] // 2):
        onehot = jnp.concatenate(
            [
                jnp.concatenate(
                    [
                        jnp.where(column - T * (2 * pair + half) == lane, 1.0, 0.0)
                        for half in range(2)
                    ],
                    axis=1,
                )
                for column in columns
            ],
            axis=0,
        ).astype(BF16)
        total = total + dot(onehot, flat(source[2 * pair : 2 * pair + 2]))
    return tiled(total.astype(BF16))


def placed_rows(export, block, rows):
    row = lax.broadcasted_iota(jnp.int32, (T, T), 0) + block * T
    onehot = jnp.concatenate(
        [jnp.where(export[i : i + 1] == row, 1.0, 0.0) for i in range(2)], axis=1
    ).astype(BF16)
    return dot(onehot, rows)


def link(column, number, targets, prev, last):
    def before(s, carry):
        mine = column(s)
        best = jnp.int32(-1)
        for t in range(number):
            best = jnp.where((column(t) == mine) & (t < s), t, best)
        prev[s] = best
        return carry

    def final(j, carry):
        best = jnp.int32(-1)
        for t in range(number):
            best = jnp.where(column(t) == j, t, best)
        last[j] = best
        return carry

    lax.fori_loop(0, number, before, 0)
    lax.fori_loop(0, targets, final, 0)


def linked(pieces, at):
    return jnp.where(at >= 0, 1.0, 0.0) * pieces[jnp.maximum(at, 0)]


def chain(pieces, prev, number):
    def step(s, carry):
        pieces[s] = pieces[s] + linked(pieces, prev[s])
        return carry

    lax.fori_loop(0, number, step, 0)


def kernel(
    nx,
    ndp,
    nodes,
    cotangent,
    weights,
    fine_tiles,
    fine_cols,
    fine_export,
    pool_tiles,
    pool_cols,
    mid_tiles,
    mid_cols,
    mid_export,
    upper_tiles,
    upper_cols,
    top_tiles,
    top_cols,
    node_grad,
    weight_grad,
    fcols,
    fexport,
    pcols,
    mcols,
    mexport,
    ucols,
    tcols,
    S,
    COT,
    M,
    FT,
    PT,
    MT,
    UT,
    TT,
    PART,
    PRE1,
    PRE2,
    ACT1,
    ACT2,
    MSG,
    OUT,
    GN,
    GM,
    PIECE,
    MS,
    MPART,
    MPRE1,
    MPRE2,
    MACT1,
    MACT2,
    MMSG,
    MOUT,
    GRADM,
    GRADML,
    MGN,
    MGM,
    MPIECE,
    PPIECE,
    UPIECE,
    fprev,
    flast,
    mprev,
    mlast,
    pprev,
    plast,
    uprev,
    ulast,
    HALO_S,
    HALO_R,
    MHALO_S,
    MHALO_R,
    BACK_S,
    BACK_R,
    MBACK_S,
    MBACK_R,
    COL_S,
    COL_R,
    YG,
    PARTNER,
    SEL_S,
    SEL_R,
    P1_S,
    P1_R,
    P2_S,
    P2_R,
    PY_S,
    PY_R,
    WACC,
    W_S,
    W_R,
    W_Y,
    W_Z,
    W_O,
    GF,
    ONODE,
    load_sem,
    send_sem,
    recv_sem,
):
    ny = NY
    ndom = nx * ny
    dp = lax.axis_index("dp")
    dom = lax.axis_index("dom")
    x = lax.div(dom, ny)
    y = lax.rem(dom, ny)
    nz = ndp // NC
    z = lax.div(dp, NC)
    core = lax.rem(dp, NC)

    left = (dp, lax.rem(dom + ndom - 1, ndom))
    right = (dp, lax.rem(dom + 1, ndom))

    def at_x(i):
        return (dp, lax.rem(x + i, nx) * ny + y)

    def at_y(i):
        return (dp, x * ny + lax.rem(y + i, ny))

    def at_z(i):
        return (lax.rem(z + i, nz) * NC + core, dom)

    def at_cx(c, i):
        return (z * NC + lax.rem(core + c, NC), lax.rem(x + i, nx) * ny + y)

    x_order = far_first(nx)
    y_order = far_first(ny)
    z_order = far_first(nz)
    cx_order = [(c, i) for c in range(NC) for i in range(nx) if (c, i) != (0, 0)]
    partners = (
        [left, right]
        + [at_cx(c, i) for c, i in cx_order]
        + [at_y(i) for i in y_order]
        + [at_z(i) for i in z_order]
    )
    started = []

    def send(src, dst, device):
        number = len(started)
        copy = pltpu.make_async_remote_copy(
            src_ref=src,
            dst_ref=dst,
            send_sem=send_sem.at[number],
            recv_sem=recv_sem.at[number],
            device_id=device,
            device_id_type=MESH,
        )
        copy.start()
        started.append(copy)
        return copy

    loads = []

    def load(src, dst):
        copy = pltpu.make_async_copy(src, dst, load_sem.at[len(loads)])
        copy.start()
        loads.append(copy)
        return copy

    got_nodes = load(nodes, S.at[pl.ds(0, FB)])
    got_export = load(fine_export, fexport)
    barrier = pltpu.get_barrier_semaphore()
    for partner in partners:
        pl.semaphore_signal(barrier, inc=1, device_id=partner, device_id_type=MESH)
    got_tcols = load(top_cols, tcols)
    got_pcols = load(pool_cols, pcols)
    got_ucols = load(upper_cols, ucols)
    got_cot = load(cotangent, COT)
    got_pool = load(pool_tiles, PT)
    got_upper = load(upper_tiles, UT)
    got_weights = load(weights, M)
    got_fine = load(fine_tiles, FT)
    got_fcols = load(fine_cols, fcols)
    got_mid = load(mid_tiles, MT)
    got_mcols = load(mid_cols, mcols)
    got_mexport = load(mid_export, mexport)
    got_top = load(top_tiles, TT)

    has_left = jnp.where(dom > 0, 1.0, 0.0).astype(F32)
    has_right = jnp.where(dom < ndom - 1, 1.0, 0.0).astype(F32)

    def level(l):
        return [M[l, i] for i in range(4)]

    rows = 4 * T // (NC * nx)

    def chunk(c, i):
        number = lax.rem(core + c, NC) * nx + lax.rem(x + i, nx)
        return pl.ds(pl.multiple_of(number * rows, rows), rows)

    def scattered(store, slots):
        return [
            send(store.at[chunk(c, i)], slots.at[n], at_cx(c, i))
            for n, (c, i) in enumerate(cx_order)
        ]

    def scatter_sum(copies, store, slots):
        for copy in copies:
            copy.wait_recv()
        total = store[chunk(0, 0)].astype(F32)
        for n in range(len(cx_order)):
            total = total + slots[n].astype(F32)
        return total.astype(BF16)

    def shown_y(value, slots):
        slots[y] = value
        return [send(slots.at[y], slots.at[y], at_y(i)) for i in y_order]

    def shown_z(value, slots):
        slots[z] = value
        return [send(slots.at[z], slots.at[z], at_z(i)) for i in z_order]

    def slot_sum(copies, slots, number):
        for copy in copies:
            copy.wait_recv()
        total = slots[0].astype(F32)
        for i in range(1, number):
            total = total + slots[i].astype(F32)
        return total.astype(BF16)

    def gathered(store):
        mine = store.at[chunk(0, 0)]
        return [send(mine, mine, at_cx(c, i)) for c, i in cx_order]

    got_export.wait()
    got_nodes.wait()
    HALO_S[...] = picked_rows(fexport[0], S.at[pl.ds(0, FB)])
    pl.semaphore_wait(barrier, len(partners))
    halo = [send(HALO_S.at[1], HALO_R.at[0], right), send(HALO_S.at[0], HALO_R.at[1], left)]
    got_tcols.wait()
    COL_S[...] = jnp.full((8, T), tcols[0, 2], jnp.int32)
    cols_sent = [send(COL_S, COL_R.at[i - 1], at_x(i)) for i in range(1, nx)]

    for copy in (got_cot, got_pool, got_pcols, got_upper, got_ucols):
        copy.wait()
    for m in range(MB):
        pooled = dot(PT[m, 0], COT[pcols[0, m]]) + dot(PT[m, 1], COT[pcols[1, m]])
        GRADM[m] = pooled
        GRADML[m] = pooled.astype(BF16)
    grad_top = dot(UT[0, 0], GRADML[ucols[0, 0]]) + dot(UT[0, 1], GRADML[ucols[0, 1]])
    for copy in (got_weights, got_fine, got_fcols):
        copy.wait()

    def fine_own(g, carry):
        base = g * GROUP
        m0 = M[0, 0]
        u = flat(S[pl.ds(base, GROUP)])
        PRE1[pl.ds(base, GROUP)] = tiled(dot(u, m0))
        for b in range(GROUP):
            PART[base + b] = dot(FT[base + b, 0], S[base + b])
        return carry

    lax.fori_loop(0, FB // GROUP, fine_own, 0)

    for copy in halo:
        copy.wait_recv()
    S[FB] = HALO_R[0] * has_left.astype(BF16)
    S[FB + 1] = HALO_R[1] * has_right.astype(BF16)

    def forward(u, v, own_pre, m):
        pre1 = own_pre + dot(v, m[1])
        act1 = (pre1 * logistic(pre1)).astype(BF16)
        pre2 = dot(act1, m[2])
        act2 = (pre2 * logistic(pre2)).astype(BF16)
        return pre1, act1, pre2, act2

    def fine_forward(g, carry):
        base = g * GROUP
        m = level(0)
        messages = []
        for b in range(GROUP):
            r = base + b
            messages.append(
                (
                    PART[r]
                    + dot(FT[r, 1], S[fcols[1, r]])
                    + dot(FT[r, 2], S[fcols[2, r]])
                ).astype(BF16)
            )
        v = jnp.concatenate(messages, axis=0)
        here = pl.ds(base, GROUP)
        u = flat(S[here])
        pre1, act1, pre2, act2 = forward(u, v, flat(PRE1[here]), m)
        MSG[here] = tiled(v)
        PRE1[here] = tiled(pre1)
        ACT1[here] = tiled(act1)
        PRE2[here] = tiled(pre2)
        ACT2[here] = tiled(act2)
        OUT[here] = tiled((u.astype(F32) + dot(act2, m[3])).astype(BF16))
        return carry

    lax.fori_loop(0, FB // GROUP, fine_forward, 0)

    for m in range(MB):
        MS[m] = (dot(PT[m, 0], OUT[pcols[0, m]]) + dot(PT[m, 1], OUT[pcols[1, m]])).astype(BF16)
    got_mexport.wait()
    MHALO_S[...] = picked_rows(mexport[0], MS[0:MB])
    mid_halo = [send(MHALO_S.at[1], MHALO_R.at[0], right), send(MHALO_S.at[0], MHALO_R.at[1], left)]
    got_mid.wait()
    got_mcols.wait()
    mm = level(1)
    mu = flat(MS[0:MB])
    MPRE1[...] = tiled(dot(mu, mm[0]))
    for r in range(MB):
        MPART[r] = dot(MT[r, 0], MS[r])
    got_top.wait()
    link(lambda s: ucols[0, s], 2, MB, uprev, ulast)
    for copy in mid_halo:
        copy.wait_recv()
    MS[MB] = MHALO_R[0] * has_left.astype(BF16)
    MS[MB + 1] = MHALO_R[1] * has_right.astype(BF16)
    mv = jnp.concatenate(
        [
            (
                MPART[r] + dot(MT[r, 1], MS[mcols[r, 1]]) + dot(MT[r, 2], MS[mcols[r, 2]])
            ).astype(BF16)
            for r in range(MB)
        ],
        axis=0,
    )
    pre1, act1, pre2, act2 = forward(mu, mv, flat(MPRE1[...]), mm)
    MOUT[...] = tiled((mu.astype(F32) + dot(act2, mm[3])).astype(BF16))
    top_in = (dot(UT[0, 0], MOUT[ucols[0, 0]]) + dot(UT[0, 1], MOUT[ucols[0, 1]])).astype(BF16)

    YG[0] = top_in
    along_y = [send(YG.at[0], YG.at[i], at_y(i)) for i in y_order]
    half = send(YG.at[0], PARTNER, at_x(nx // 2))
    MMSG[...] = tiled(mv)
    MACT1[...] = tiled(act1)
    MACT2[...] = tiled(act2)
    MPRE1[...] = tiled(slope(pre1))
    MPRE2[...] = tiled(slope(pre2))

    def fine_slopes(g, carry):
        here = pl.ds(g * 2, 2)
        PRE1[here] = slope(PRE1[here])
        PRE2[here] = slope(PRE2[here])
        return carry

    lax.fori_loop(0, FB // 2, fine_slopes, 0)
    tm = level(2)
    top_own = dot(top_in, tm[0])
    top_part = dot(TT[0, 0], top_in)
    for copy in cols_sent:
        copy.wait_recv()
    cols = [COL_S[0:1]] + [COL_R[i, 0:1] for i in range(nx - 1)]
    for copy in along_y:
        copy.wait_recv()

    def chosen(column):
        total = jnp.zeros((T, T), BF16)
        for k in range(ny):
            source = x * ny + lax.rem(y + ny - k, ny)
            total = total + jnp.where(column == source, 1.0, 0.0).astype(BF16) * YG[k]
        return total

    along_x = []
    for i in x_order:
        SEL_S[i - 1] = chosen(cols[nx - i])
        along_x.append(send(SEL_S.at[i - 1], SEL_R.at[i - 1], at_x(i)))
    third = chosen(cols[0])
    half.wait_recv()
    top_part = top_part + dot(TT[0, 1], PARTNER[...])
    link(lambda s: pcols[lax.div(s, MB), lax.rem(s, MB)], 2 * MB, FB, pprev, plast)
    link(lambda s: mcols[lax.rem(s, MB), 1 + lax.div(s, MB)], 2 * MB, MB + 2, mprev, mlast)
    for copy in along_x:
        copy.wait_recv()
    for i in range(nx - 1):
        third = third + SEL_R[i]
    top_msg = (top_part + dot(TT[0, 2], third)).astype(BF16)
    pre1, act1, pre2, act2 = forward(top_in, top_msg, top_own, tm)

    def back_to_first(g, slope1, slope2, m):
        gb = g.astype(BF16)
        gs = (dot_bt(gb, m[3]) * slope2).astype(BF16)
        gf = (dot_bt(gs, m[2]) * slope1).astype(BF16)
        return gb, gs, gf

    def backward(g, slope1, slope2, m):
        gb, gs, gf = back_to_first(g, slope1, slope2, m)
        return gb, gs, gf, dot_bt(gf, m[1]).astype(BF16)

    def terms(u, v, act1, act2, gb, gs, gf):
        return dot_at(u, gf), dot_at(v, gf), dot_at(act1, gs), dot_at(act2, gb)

    gb, gs, gf, gm = backward(grad_top, slope(pre1), slope(pre2), tm)
    P2_S[...] = dot_at(TT[0, 2], gm).astype(BF16)
    back_x = [send(P2_S, P2_R.at[i - 1], at_x(i)) for i in x_order]
    P1_S[...] = dot_at(TT[0, 1], gm).astype(BF16)
    back_half = send(P1_S, P1_R, at_x(nx // 2))
    grad_top_in = grad_top + dot_bt(gf, tm[0]) + dot_at(TT[0, 0], gm)
    for i, term in enumerate(terms(top_in, top_msg, act1, act2, gb, gs, gf)):
        W_S[2, pl.ds(i * T, T)] = term.astype(BF16)
    for copy in back_x:
        copy.wait_recv()
    arrived = [P2_S[...].astype(F32)] + [P2_R[i].astype(F32) for i in range(nx - 1)]

    def summed(target):
        total = jnp.zeros((T, T), F32)
        for column, piece in zip(cols, arrived):
            total = total + jnp.where(column == target, 1.0, 0.0) * piece
        return total

    back_y = []
    for i in y_order:
        PY_S[i - 1] = summed(x * ny + lax.rem(y + i, ny)).astype(BF16)
        back_y.append(send(PY_S.at[i - 1], PY_R.at[i - 1], at_y(i)))
    top_sum = scattered(W_S.at[2], W_R.at[2])
    grad_top_in = grad_top_in + summed(dom)
    link(lambda s: fcols[1 + lax.div(s, FB), lax.rem(s, FB)], 2 * FB, FB + 2, fprev, flast)
    back_half.wait_recv()
    grad_top_in = grad_top_in + P1_R[...].astype(F32)
    for copy in back_y:
        copy.wait_recv()
    for i in range(ny - 1):
        grad_top_in = grad_top_in + PY_R[i].astype(F32)

    top_sum = shown_z(scatter_sum(top_sum, W_S.at[2], W_R.at[2]), W_Z.at[2])

    low = grad_top_in.astype(BF16)
    for s in range(2):
        UPIECE[s] = dot_at(UT[0, s], low)
    chain(UPIECE, uprev, 2)
    for m in range(MB):
        GRADM[m] = GRADM[m] + linked(UPIECE, ulast[m])
    g = flat(GRADM[...])
    gb, gs, gf, gm = backward(g, flat(MPRE1[...]), flat(MPRE2[...]), mm)
    MGM[...] = tiled(gm)
    for r in range(MB):
        MPIECE[r] = dot_at(MT[r, 1], MGM[r])
        MPIECE[MB + r] = dot_at(MT[r, 2], MGM[r])
    chain(MPIECE, mprev, 2 * MB)
    MBACK_S[0] = linked(MPIECE, mlast[MB]).astype(BF16)
    MBACK_S[1] = linked(MPIECE, mlast[MB + 1]).astype(BF16)
    mid_back = [send(MBACK_S.at[1], MBACK_R.at[0], right), send(MBACK_S.at[0], MBACK_R.at[1], left)]
    MGN[...] = tiled(g + dot_bt(gf, mm[0]))
    for r in range(MB):
        MGN[r] = MGN[r] + dot_at(MT[r, 0], MGM[r]) + linked(MPIECE, mlast[r])
    for i, term in enumerate(
        terms(flat(MS[0:MB]), flat(MMSG[...]), flat(MACT1[...]), flat(MACT2[...]), gb, gs, gf)
    ):
        W_S[1, pl.ds(i * T, T)] = term.astype(BF16)

    mid_sum = scattered(W_S.at[1], W_R.at[1])

    for copy in mid_back:
        copy.wait_recv()
    back_rows = jnp.concatenate(
        [MBACK_R[0] * has_left.astype(BF16), MBACK_R[1] * has_right.astype(BF16)], axis=0
    )
    for r in range(MB):
        MGN[r] = MGN[r] + placed_rows(mexport[0], r, back_rows)
    for m in range(MB):
        low = MGN[m].astype(BF16)
        for k in range(2):
            PPIECE[k * MB + m] = dot_at(PT[m, k], low)
    chain(PPIECE, pprev, 2 * MB)

    WACC[...] = jnp.zeros_like(WACC)

    def fine_backward(g, carry):
        base = g * GROUP
        here = pl.ds(base, GROUP)
        m = level(0)
        grad = jnp.concatenate(
            [COT[base + b].astype(F32) + linked(PPIECE, plast[base + b]) for b in range(GROUP)],
            axis=0,
        )
        gb, gs, gf = back_to_first(grad, flat(PRE1[here]), flat(PRE2[here]), m)
        GN[here] = tiled(grad)
        GF[here] = tiled(gf)
        for i, term in enumerate(
            terms(flat(S[here]), flat(MSG[here]), flat(ACT1[here]), flat(ACT2[here]), gb, gs, gf)
        ):
            WACC[i] = WACC[i] + term
        return carry

    lax.fori_loop(0, FB // GROUP, fine_backward, 0)
    W_S[0] = flat(WACC[...]).astype(BF16)
    fine_sum = scattered(W_S.at[0], W_R.at[0])
    top_sum = shown_y(slot_sum(top_sum, W_Z.at[2], nz), W_Y.at[2])
    mid_sum = shown_z(scatter_sum(mid_sum, W_S.at[1], W_R.at[1]), W_Z.at[1])

    def fine_rows(g, carry):
        here = pl.ds(g * GROUP, GROUP)
        gf = flat(GF[here])
        GM[here] = tiled(dot_bt(gf, M[0, 1]).astype(BF16))
        GN[here] = GN[here] + tiled(dot_bt(gf, M[0, 0]))
        return carry

    lax.fori_loop(0, FB // GROUP, fine_rows, 0)

    def fine_pieces(g, carry):
        for b in range(2):
            r = g * 2 + b
            grad = GM[r]
            PIECE[r] = dot_at(FT[r, 1], grad)
            PIECE[FB + r] = dot_at(FT[r, 2], grad)
            GN[r] = GN[r] + dot_at(FT[r, 0], grad)
        return carry

    lax.fori_loop(0, FB // 2, fine_pieces, 0)
    chain(PIECE, fprev, 2 * FB)
    BACK_S[0] = linked(PIECE, flast[FB]).astype(BF16)
    BACK_S[1] = linked(PIECE, flast[FB + 1]).astype(BF16)
    back = [send(BACK_S.at[1], BACK_R.at[0], right), send(BACK_S.at[0], BACK_R.at[1], left)]

    half = rows // 2
    value = scatter_sum(fine_sum, W_S.at[0], W_R.at[0])
    first = shown_y(value[0:half], W_Y.at[0, :, 0:half])
    second = shown_z(value[half:rows], W_Z.at[0, :, half:rows])
    W_O[2, chunk(0, 0)] = slot_sum(top_sum, W_Y.at[2], ny)
    top_sum = gathered(W_O.at[2])
    mid_sum = shown_y(slot_sum(mid_sum, W_Z.at[1], nz), W_Y.at[1])

    first = shown_z(slot_sum(first, W_Y.at[0, :, 0:half], ny), W_Z.at[0, :, 0:half])
    second = shown_y(slot_sum(second, W_Z.at[0, :, half:rows], nz), W_Y.at[0, :, half:rows])

    for copy in back:
        copy.wait_recv()
    back_rows = jnp.concatenate(
        [BACK_R[0] * has_left.astype(BF16), BACK_R[1] * has_right.astype(BF16)], axis=0
    )
    fexp = fexport[0]

    def finish(r, carry):
        ONODE[r] = (
            GN[r] + linked(PIECE, flast[r]) + placed_rows(fexp, r, back_rows)
        ).astype(BF16)
        return carry

    lax.fori_loop(0, FB, finish, 0)
    put_nodes = load(ONODE, node_grad)
    W_O[1, chunk(0, 0)] = slot_sum(mid_sum, W_Y.at[1], ny)
    mid_sum = gathered(W_O.at[1])
    W_O[0, chunk(0, 0)] = jnp.concatenate(
        [
            slot_sum(first, W_Z.at[0, :, 0:half], nz),
            slot_sum(second, W_Y.at[0, :, half:rows], ny),
        ],
        axis=0,
    )
    fine_sum = gathered(W_O.at[0])
    for copy in top_sum + mid_sum:
        copy.wait_recv()
    put_upper = load(W_O.at[pl.ds(1, 2)], weight_grad.at[pl.ds(1, 2)])
    for copy in fine_sum:
        copy.wait_recv()
    put_fine = load(W_O.at[0], weight_grad.at[0])
    for copy in started:
        copy.wait_send()
    put_nodes.wait()
    put_upper.wait()
    put_fine.wait()


def write_kernel(node_in, weight_in, node_out, weight_out, nodes, low, full, sem):
    fetch = [pltpu.make_async_copy(weight_in.at[l], low.at[l], sem.at[l]) for l in range(3)]
    put = [pltpu.make_async_copy(full.at[l], weight_out.at[l], sem.at[3 + l]) for l in range(3)]
    node_fetch = pltpu.make_async_copy(node_in, nodes, sem.at[6])
    node_put = pltpu.make_async_copy(nodes, node_out, sem.at[7])
    for copy in fetch:
        copy.start()
    node_fetch.start()
    for l in range(3):
        fetch[l].wait()
        full[l] = low[l].astype(F32)
        put[l].start()
    node_fetch.wait()
    node_put.start()
    for copy in put:
        copy.wait()
    node_put.wait()


def written(node_grad, weight_grad):
    anywhere = pl.BlockSpec(memory_space=pl.ANY)
    return pl.pallas_call(
        write_kernel,
        out_shape=(
            jax.ShapeDtypeStruct(node_grad.shape, BF16),
            jax.ShapeDtypeStruct(weight_grad.shape, F32),
        ),
        in_specs=[anywhere] * 2,
        out_specs=(anywhere, anywhere),
        scratch_shapes=[
            pltpu.VMEM(node_grad.shape, BF16),
            pltpu.VMEM(weight_grad.shape, BF16),
            pltpu.VMEM(weight_grad.shape, F32),
            pltpu.SemaphoreType.DMA((8,)),
        ],
        compiler_params=pltpu.CompilerParams(vmem_limit_bytes=64 * 1024 * 1024),
        name="write_results",
    )(node_grad, weight_grad)


def on_device(nx, ndp, *args):
    (
        nodes,
        cotangent,
        weights,
        fine_tiles,
        fine_cols,
        fine_export,
        pool_tiles,
        pool_cols,
        mid_tiles,
        mid_cols,
        mid_export,
        top_pool_tiles,
        top_pool_cols,
        top_tiles,
        top_cols,
    ) = args
    ny = NY
    anywhere = pl.BlockSpec(memory_space=pl.ANY)

    def low(*shape):
        return pltpu.VMEM(shape, BF16)

    def full(*shape):
        return pltpu.VMEM(shape, F32)

    def index(number):
        return pltpu.SMEM((number,), jnp.int32)

    nz = ndp // NC
    rows = 4 * T // (NC * nx)
    copies = (
        4 * 2
        + (nx - 1) * 3
        + (ny - 1) * 2
        + 2
        + 3 * 2 * (NC * nx - 1)
        + 4 * (ny - 1 + nz - 1)
    )
    scratch = [
        pltpu.SMEM((3, FB), jnp.int32),
        pltpu.VMEM((1, 2, T), jnp.int32),
        pltpu.SMEM((2, MB), jnp.int32),
        pltpu.SMEM((MB, 3), jnp.int32),
        pltpu.VMEM((1, 2, T), jnp.int32),
        pltpu.SMEM((1, 2), jnp.int32),
        pltpu.SMEM((1, 3), jnp.int32),
        low(FB + 2, T, T),
        low(FB, T, T),
        low(3, 4, T, T),
        low(FB, 3, T, T),
        low(MB, 2, T, T),
        low(MB, 3, T, T),
        low(1, 2, T, T),
        low(1, 3, T, T),
        full(FB, T, T),
        full(FB, T, T),
        full(FB, T, T),
        low(FB, T, T),
        low(FB, T, T),
        low(FB, T, T),
        low(FB, T, T),
        full(FB, T, T),
        low(FB, T, T),
        full(2 * FB, T, T),
        low(MB + 2, T, T),
        full(MB, T, T),
        full(MB, T, T),
        full(MB, T, T),
        low(MB, T, T),
        low(MB, T, T),
        low(MB, T, T),
        low(MB, T, T),
        full(MB, T, T),
        low(MB, T, T),
        full(MB, T, T),
        low(MB, T, T),
        full(2 * MB, T, T),
        full(2 * MB, T, T),
        full(2, T, T),
        index(2 * FB),
        index(FB + 2),
        index(2 * MB),
        index(MB + 2),
        index(2 * MB),
        index(FB),
        index(2),
        index(MB),
        low(2, T, T),
        low(2, T, T),
        low(2, T, T),
        low(2, T, T),
        low(2, T, T),
        low(2, T, T),
        low(2, T, T),
        low(2, T, T),
        pltpu.VMEM((8, T), jnp.int32),
        pltpu.VMEM((nx - 1, 8, T), jnp.int32),
        low(ny, T, T),
        low(T, T),
        low(nx - 1, T, T),
        low(nx - 1, T, T),
        low(T, T),
        low(T, T),
        low(T, T),
        low(nx - 1, T, T),
        low(ny - 1, T, T),
        low(ny - 1, T, T),
        full(4, T, T),
        low(3, 4 * T, T),
        low(3, NC * nx - 1, rows, T),
        low(3, ny, rows, T),
        low(3, nz, rows, T),
        low(3, 4 * T, T),
        low(FB, T, T),
        low(FB, T, T),
        pltpu.SemaphoreType.DMA((20,)),
        pltpu.SemaphoreType.DMA((copies,)),
        pltpu.SemaphoreType.DMA((copies,)),
    ]

    def body(*refs):
        kernel(nx, ndp, *refs)

    node_grad, weight_grad = pl.pallas_call(
        body,
        out_shape=(
            jax.ShapeDtypeStruct((FB, T, T), BF16),
            jax.ShapeDtypeStruct((3, 4 * T, T), BF16),
        ),
        in_specs=[anywhere] * 15,
        out_specs=(anywhere, anywhere),
        scratch_shapes=scratch,
        compiler_params=pltpu.CompilerParams(
            collective_id=0, has_side_effects=True, vmem_limit_bytes=64 * 1024 * 1024
        ),
        name="mesh_step",
    )(
        nodes.reshape(FB, T, T),
        cotangent.reshape(FB, T, T),
        weights,
        fine_tiles,
        fine_cols.T,
        fine_export,
        pool_tiles,
        pool_cols.T,
        mid_tiles,
        mid_cols,
        mid_export,
        top_pool_tiles,
        top_pool_cols,
        top_tiles,
        top_cols,
    )
    node_grad, weight_grad = written(node_grad, weight_grad)
    return node_grad.reshape(nodes.shape), weight_grad.reshape(weights.shape)


def solution(mesh):
    nx, ndp = mesh.shape["dom"] // NY, mesh.shape["dp"]

    def run(*args):
        return on_device(nx, ndp, *args)

    return jax.shard_map(
        run,
        mesh=mesh,
        in_specs=(
            P("dp", "dom", None),
            P("dp", "dom", None),
            P(),
            P("dom", None, None, None),
            P("dom", None),
            P("dom", None, None),
            P("dom", None, None, None),
            P("dom", None),
            P("dom", None, None, None),
            P("dom", None),
            P("dom", None, None),
            P("dom", None, None, None),
            P("dom", None),
            P("dom", None, None, None),
            P("dom", None),
        ),
        out_specs=(P("dp", "dom", None), P()),
        check_vma=False,
    )
```

```python
import jax
import jax.numpy as jnp
from jax import lax
from jax.experimental import pallas as pl
from jax.experimental.pallas import tpu as pltpu
from jax.sharding import PartitionSpec as P

NY = 8
NC = 2
T = 128
HALF = T // 2
FB, MB, TB = 16, 4, 1
GROUP = 4
F32, BF16 = jnp.float32, jnp.bfloat16
MESH = pl.DeviceIdType.MESH


def dot(a, b):
    return jnp.dot(a, b, preferred_element_type=F32)


def dot_bt(a, b):
    return lax.dot_general(a, b, (((1,), (1,)), ((), ())), preferred_element_type=F32)


def dot_at(a, b):
    return lax.dot_general(a, b, (((0,), (0,)), ((), ())), preferred_element_type=F32)


def logistic(s):
    return 0.5 * jnp.tanh(0.5 * s) + 0.5


def slope(s):
    q = logistic(s)
    return q * (1.0 + s * (1.0 - q))


def far_first(number):
    return sorted(range(1, number), key=lambda i: -min(i, number - i))


def flat(blocks):
    return blocks.reshape(-1, T)


def tiled(rows):
    return rows.reshape(-1, T, T)


def picked_rows(export, source):
    columns = [
        jnp.transpose(jnp.broadcast_to(export[i : i + 1].astype(F32), (T, T))) for i in range(2)
    ]
    lane = lax.broadcasted_iota(jnp.int32, (T, T), 1).astype(F32)
    total = jnp.zeros((2 * T, T), F32)
    for pair in range(source.shape[0] // 2):
        onehot = jnp.concatenate(
            [
                jnp.concatenate(
                    [
                        jnp.where(column - T * (2 * pair + half) == lane, 1.0, 0.0)
                        for half in range(2)
                    ],
                    axis=1,
                )
                for column in columns
            ],
            axis=0,
        ).astype(BF16)
        total = total + dot(onehot, flat(source[2 * pair : 2 * pair + 2]))
    return tiled(total.astype(BF16))


def placed_rows(export, block, rows):
    row = lax.broadcasted_iota(jnp.int32, (T, T), 0) + block * T
    onehot = jnp.concatenate(
        [jnp.where(export[i : i + 1] == row, 1.0, 0.0) for i in range(2)], axis=1
    ).astype(BF16)
    return dot(onehot, rows)


def link(column, number, targets, prev, last):
    def before(s, carry):
        mine = column(s)
        best = jnp.int32(-1)
        for t in range(number):
            best = jnp.where((column(t) == mine) & (t < s), t, best)
        prev[s] = best
        return carry

    def final(j, carry):
        best = jnp.int32(-1)
        for t in range(number):
            best = jnp.where(column(t) == j, t, best)
        last[j] = best
        return carry

    lax.fori_loop(0, number, before, 0)
    lax.fori_loop(0, targets, final, 0)


def linked(pieces, at):
    return jnp.where(at >= 0, 1.0, 0.0) * pieces[jnp.maximum(at, 0)]


def chain(pieces, prev, number):
    def step(s, carry):
        pieces[s] = pieces[s] + linked(pieces, prev[s])
        return carry

    lax.fori_loop(0, number, step, 0)


def kernel(
    nx,
    ndp,
    nodes,
    cotangent,
    weights,
    fine_tiles,
    fine_cols,
    fine_export,
    pool_tiles,
    pool_cols,
    mid_tiles,
    mid_cols,
    mid_export,
    upper_tiles,
    upper_cols,
    top_tiles,
    top_cols,
    node_grad,
    weight_grad,
    fcols,
    fexport,
    pcols,
    mcols,
    mexport,
    ucols,
    tcols,
    S,
    COT,
    M,
    FT,
    PT,
    MT,
    UT,
    TT,
    PART,
    PRE1,
    PRE2,
    ACT1,
    ACT2,
    MSG,
    OUT,
    GN,
    GM,
    PIECE,
    MS,
    MPART,
    MPRE1,
    MPRE2,
    MACT1,
    MACT2,
    MMSG,
    MOUT,
    GRADM,
    GRADML,
    MGN,
    MGM,
    MPIECE,
    PPIECE,
    UPIECE,
    fprev,
    flast,
    mprev,
    mlast,
    pprev,
    plast,
    uprev,
    ulast,
    HALO_S,
    HALO_R,
    MHALO_S,
    MHALO_R,
    BACK_S,
    BACK_R,
    MBACK_S,
    MBACK_R,
    COL_S,
    COL_R,
    COLY_R,
    YG,
    XG,
    PARTNER,
    SEL_S,
    SEL_R,
    SELY_S,
    SELY_R,
    P1_S,
    P1_R,
    P2_S,
    P2_R,
    P2Y_R,
    PY_S,
    PY_R,
    PX_S,
    PX_R,
    WACC,
    W_S,
    W_R,
    W_Y,
    W_Z,
    W_O,
    GF,
    ONODE,
    load_sem,
    send_sem,
    recv_sem,
):
    ny = NY
    ndom = nx * ny
    dp = lax.axis_index("dp")
    dom = lax.axis_index("dom")
    x = lax.div(dom, ny)
    y = lax.rem(dom, ny)
    nz = ndp // NC
    z = lax.div(dp, NC)
    core = lax.rem(dp, NC)

    left = (dp, lax.rem(dom + ndom - 1, ndom))
    right = (dp, lax.rem(dom + 1, ndom))

    def at_x(i):
        return (dp, lax.rem(x + i, nx) * ny + y)

    def at_y(i):
        return (dp, x * ny + lax.rem(y + i, ny))

    def at_z(i):
        return (lax.rem(z + i, nz) * NC + core, dom)

    def at_cx(c, i):
        return (z * NC + lax.rem(core + c, NC), lax.rem(x + i, nx) * ny + y)

    x_order = far_first(nx)
    y_order = far_first(ny)
    z_order = far_first(nz)
    cx_order = [(c, i) for c in range(NC) for i in range(nx) if (c, i) != (0, 0)]
    partners = (
        [left, right]
        + [at_cx(c, i) for c, i in cx_order]
        + [at_y(i) for i in y_order]
        + [at_z(i) for i in z_order]
    )
    started = []

    def send(src, dst, device):
        number = len(started)
        copy = pltpu.make_async_remote_copy(
            src_ref=src,
            dst_ref=dst,
            send_sem=send_sem.at[number],
            recv_sem=recv_sem.at[number],
            device_id=device,
            device_id_type=MESH,
        )
        copy.start()
        started.append(copy)
        return copy

    loads = []

    def load(src, dst):
        copy = pltpu.make_async_copy(src, dst, load_sem.at[len(loads)])
        copy.start()
        loads.append(copy)
        return copy

    got_nodes = load(nodes, S.at[pl.ds(0, FB)])
    got_export = load(fine_export, fexport)
    barrier = pltpu.get_barrier_semaphore()
    for partner in partners:
        pl.semaphore_signal(barrier, inc=1, device_id=partner, device_id_type=MESH)
    got_tcols = load(top_cols, tcols)
    got_pcols = load(pool_cols, pcols)
    got_ucols = load(upper_cols, ucols)
    got_cot = load(cotangent, COT)
    got_pool = load(pool_tiles, PT)
    got_upper = load(upper_tiles, UT)
    got_weights = load(weights, M)
    got_fine = load(fine_tiles, FT)
    got_fcols = load(fine_cols, fcols)
    got_mid = load(mid_tiles, MT)
    got_mcols = load(mid_cols, mcols)
    got_mexport = load(mid_export, mexport)
    got_top = load(top_tiles, TT)

    has_left = jnp.where(dom > 0, 1.0, 0.0).astype(F32)
    has_right = jnp.where(dom < ndom - 1, 1.0, 0.0).astype(F32)

    def level(l):
        return [M[l, i] for i in range(4)]

    rows = 4 * T // (NC * nx)

    def chunk(c, i):
        number = lax.rem(core + c, NC) * nx + lax.rem(x + i, nx)
        return pl.ds(pl.multiple_of(number * rows, rows), rows)

    def scattered(store, slots):
        return [
            send(store.at[chunk(c, i)], slots.at[n], at_cx(c, i))
            for n, (c, i) in enumerate(cx_order)
        ]

    def scatter_sum(copies, store, slots):
        for copy in copies:
            copy.wait_recv()
        total = store[chunk(0, 0)].astype(F32)
        for n in range(len(cx_order)):
            total = total + slots[n].astype(F32)
        return total.astype(BF16)

    def shown_y(value, slots):
        slots[y] = value
        return [send(slots.at[y], slots.at[y], at_y(i)) for i in y_order]

    def shown_z(value, slots):
        slots[z] = value
        return [send(slots.at[z], slots.at[z], at_z(i)) for i in z_order]

    def slot_sum(copies, slots, number):
        for copy in copies:
            copy.wait_recv()
        total = slots[0].astype(F32)
        for i in range(1, number):
            total = total + slots[i].astype(F32)
        return total.astype(BF16)

    def gathered(store):
        mine = store.at[chunk(0, 0)]
        return [send(mine, mine, at_cx(c, i)) for c, i in cx_order]

    got_export.wait()
    got_nodes.wait()
    HALO_S[...] = picked_rows(fexport[0], S.at[pl.ds(0, FB)])
    pl.semaphore_wait(barrier, len(partners))
    halo = [send(HALO_S.at[1], HALO_R.at[0], right), send(HALO_S.at[0], HALO_R.at[1], left)]
    got_tcols.wait()
    COL_S[...] = jnp.full((8, T), tcols[0, 2], jnp.int32)
    cols_sent = [send(COL_S, COL_R.at[i - 1], at_x(i)) for i in x_order]
    cols_sent += [send(COL_S, COLY_R.at[i - 1], at_y(i)) for i in y_order]

    for copy in (got_cot, got_pool, got_pcols, got_upper, got_ucols):
        copy.wait()
    for m in range(MB):
        pooled = dot(PT[m, 0], COT[pcols[0, m]]) + dot(PT[m, 1], COT[pcols[1, m]])
        GRADM[m] = pooled
        GRADML[m] = pooled.astype(BF16)
    grad_top = dot(UT[0, 0], GRADML[ucols[0, 0]]) + dot(UT[0, 1], GRADML[ucols[0, 1]])
    for copy in (got_weights, got_fine, got_fcols):
        copy.wait()

    def fine_own(g, carry):
        base = g * GROUP
        m0 = M[0, 0]
        u = flat(S[pl.ds(base, GROUP)])
        PRE1[pl.ds(base, GROUP)] = tiled(dot(u, m0))
        for b in range(GROUP):
            PART[base + b] = dot(FT[base + b, 0], S[base + b])
        return carry

    lax.fori_loop(0, FB // GROUP, fine_own, 0)

    for copy in halo:
        copy.wait_recv()
    S[FB] = HALO_R[0] * has_left.astype(BF16)
    S[FB + 1] = HALO_R[1] * has_right.astype(BF16)

    def forward(u, v, own_pre, m):
        pre1 = own_pre + dot(v, m[1])
        act1 = (pre1 * logistic(pre1)).astype(BF16)
        pre2 = dot(act1, m[2])
        act2 = (pre2 * logistic(pre2)).astype(BF16)
        return pre1, act1, pre2, act2

    def fine_forward(g, carry):
        base = g * GROUP
        m = level(0)
        messages = []
        for b in range(GROUP):
            r = base + b
            messages.append(
                (
                    PART[r]
                    + dot(FT[r, 1], S[fcols[1, r]])
                    + dot(FT[r, 2], S[fcols[2, r]])
                ).astype(BF16)
            )
        v = jnp.concatenate(messages, axis=0)
        here = pl.ds(base, GROUP)
        u = flat(S[here])
        pre1, act1, pre2, act2 = forward(u, v, flat(PRE1[here]), m)
        MSG[here] = tiled(v)
        PRE1[here] = tiled(pre1)
        ACT1[here] = tiled(act1)
        PRE2[here] = tiled(pre2)
        ACT2[here] = tiled(act2)
        OUT[here] = tiled((u.astype(F32) + dot(act2, m[3])).astype(BF16))
        return carry

    lax.fori_loop(0, FB // GROUP, fine_forward, 0)

    for m in range(MB):
        MS[m] = (dot(PT[m, 0], OUT[pcols[0, m]]) + dot(PT[m, 1], OUT[pcols[1, m]])).astype(BF16)
    got_mexport.wait()
    MHALO_S[...] = picked_rows(mexport[0], MS[0:MB])
    mid_halo = [send(MHALO_S.at[1], MHALO_R.at[0], right), send(MHALO_S.at[0], MHALO_R.at[1], left)]
    got_mid.wait()
    got_mcols.wait()
    mm = level(1)
    mu = flat(MS[0:MB])
    MPRE1[...] = tiled(dot(mu, mm[0]))
    for r in range(MB):
        MPART[r] = dot(MT[r, 0], MS[r])
    got_top.wait()
    link(lambda s: ucols[0, s], 2, MB, uprev, ulast)
    for copy in mid_halo:
        copy.wait_recv()
    MS[MB] = MHALO_R[0] * has_left.astype(BF16)
    MS[MB + 1] = MHALO_R[1] * has_right.astype(BF16)
    mv = jnp.concatenate(
        [
            (
                MPART[r] + dot(MT[r, 1], MS[mcols[r, 1]]) + dot(MT[r, 2], MS[mcols[r, 2]])
            ).astype(BF16)
            for r in range(MB)
        ],
        axis=0,
    )
    pre1, act1, pre2, act2 = forward(mu, mv, flat(MPRE1[...]), mm)
    MOUT[...] = tiled((mu.astype(F32) + dot(act2, mm[3])).astype(BF16))
    top_in = (dot(UT[0, 0], MOUT[ucols[0, 0]]) + dot(UT[0, 1], MOUT[ucols[0, 1]])).astype(BF16)

    YG[0] = top_in[0:HALF]
    XG[0] = top_in[HALF:T]
    along_y = [send(YG.at[0], YG.at[i], at_y(i)) for i in y_order]
    along_x = [send(XG.at[0], XG.at[i], at_x(i)) for i in x_order]
    partner = send(YG.at[0], PARTNER, at_x(nx // 2))
    MMSG[...] = tiled(mv)
    MACT1[...] = tiled(act1)
    MACT2[...] = tiled(act2)
    MPRE1[...] = tiled(slope(pre1))
    MPRE2[...] = tiled(slope(pre2))

    def fine_slopes(g, carry):
        here = pl.ds(g * 2, 2)
        PRE1[here] = slope(PRE1[here])
        PRE2[here] = slope(PRE2[here])
        return carry

    lax.fori_loop(0, FB // 2, fine_slopes, 0)
    tm = level(2)
    top_own = dot(top_in, tm[0])
    top_part = dot(TT[0, 0], top_in)
    for copy in cols_sent:
        copy.wait_recv()
    cols = [COL_S[0:1]] + [COL_R[i, 0:1] for i in range(nx - 1)]
    cols_y = [COL_S[0:1]] + [COLY_R[i, 0:1] for i in range(ny - 1)]

    def chosen(column, blocks, sources):
        total = jnp.zeros((HALF, T), BF16)
        for k, source in enumerate(sources):
            total = total + jnp.where(column == source, 1.0, 0.0).astype(BF16) * blocks[k]
        return total

    by_x = [lax.rem(x + nx - k, nx) * ny + y for k in range(nx)]
    by_y = [x * ny + lax.rem(y + ny - k, ny) for k in range(ny)]
    for copy in along_x:
        copy.wait_recv()
    chosen_y = []
    for i in y_order:
        SELY_S[i - 1] = chosen(cols_y[ny - i], XG, by_x)
        chosen_y.append(send(SELY_S.at[i - 1], SELY_R.at[i - 1], at_y(i)))
    lower = chosen(cols[0], XG, by_x)
    for copy in along_y:
        copy.wait_recv()
    chosen_x = []
    for i in x_order:
        SEL_S[i - 1] = chosen(cols[nx - i], YG, by_y)
        chosen_x.append(send(SEL_S.at[i - 1], SEL_R.at[i - 1], at_x(i)))
    upper = chosen(cols[0], YG, by_y)
    partner.wait_recv()
    across = jnp.concatenate([PARTNER[...], XG[nx // 2]], axis=0)
    top_part = top_part + dot(TT[0, 1], across)
    link(lambda s: pcols[lax.div(s, MB), lax.rem(s, MB)], 2 * MB, FB, pprev, plast)
    link(lambda s: mcols[lax.rem(s, MB), 1 + lax.div(s, MB)], 2 * MB, MB + 2, mprev, mlast)
    for copy in chosen_y + chosen_x:
        copy.wait_recv()
    for i in range(ny - 1):
        lower = lower + SELY_R[i]
    for i in range(nx - 1):
        upper = upper + SEL_R[i]
    third = jnp.concatenate([upper, lower], axis=0)
    top_msg = (top_part + dot(TT[0, 2], third)).astype(BF16)
    pre1, act1, pre2, act2 = forward(top_in, top_msg, top_own, tm)

    def back_to_first(g, slope1, slope2, m):
        gb = g.astype(BF16)
        gs = (dot_bt(gb, m[3]) * slope2).astype(BF16)
        gf = (dot_bt(gs, m[2]) * slope1).astype(BF16)
        return gb, gs, gf

    def backward(g, slope1, slope2, m):
        gb, gs, gf = back_to_first(g, slope1, slope2, m)
        return gb, gs, gf, dot_bt(gf, m[1]).astype(BF16)

    def terms(u, v, act1, act2, gb, gs, gf):
        return dot_at(u, gf), dot_at(v, gf), dot_at(act1, gs), dot_at(act2, gb)

    gb, gs, gf, gm = backward(grad_top, slope(pre1), slope(pre2), tm)
    P2_S[...] = dot_at(TT[0, 2], gm).astype(BF16)
    back_x = [send(P2_S.at[pl.ds(0, HALF)], P2_R.at[i - 1], at_x(i)) for i in x_order]
    back_y = [send(P2_S.at[pl.ds(HALF, HALF)], P2Y_R.at[i - 1], at_y(i)) for i in y_order]
    P1_S[...] = dot_at(TT[0, 1], gm).astype(BF16)
    back_half = send(P1_S, P1_R, at_x(nx // 2))
    grad_top_in = grad_top + dot_bt(gf, tm[0]) + dot_at(TT[0, 0], gm)
    for i, term in enumerate(terms(top_in, top_msg, act1, act2, gb, gs, gf)):
        W_S[2, pl.ds(i * T, T)] = term.astype(BF16)
    for copy in back_x:
        copy.wait_recv()
    upper_parts = [P2_S[0:HALF].astype(F32)] + [P2_R[i].astype(F32) for i in range(nx - 1)]

    def summed(target, columns, pieces):
        total = jnp.zeros((HALF, T), F32)
        for column, piece in zip(columns, pieces):
            total = total + jnp.where(column == target, 1.0, 0.0) * piece
        return total

    summed_y = []
    for i in y_order:
        target = x * ny + lax.rem(y + i, ny)
        PY_S[i - 1] = summed(target, cols, upper_parts).astype(BF16)
        summed_y.append(send(PY_S.at[i - 1], PY_R.at[i - 1], at_y(i)))
    upper = summed(dom, cols, upper_parts)
    for copy in back_y:
        copy.wait_recv()
    lower_parts = [P2_S[HALF:T].astype(F32)] + [P2Y_R[i].astype(F32) for i in range(ny - 1)]
    summed_x = []
    for i in x_order:
        target = lax.rem(x + i, nx) * ny + y
        PX_S[i - 1] = summed(target, cols_y, lower_parts).astype(BF16)
        summed_x.append(send(PX_S.at[i - 1], PX_R.at[i - 1], at_x(i)))
    lower = summed(dom, cols_y, lower_parts)
    top_sum = scattered(W_S.at[2], W_R.at[2])
    link(lambda s: fcols[1 + lax.div(s, FB), lax.rem(s, FB)], 2 * FB, FB + 2, fprev, flast)
    back_half.wait_recv()
    grad_top_in = grad_top_in + P1_R[...].astype(F32)
    for copy in summed_y + summed_x:
        copy.wait_recv()
    for i in range(ny - 1):
        upper = upper + PY_R[i].astype(F32)
    for i in range(nx - 1):
        lower = lower + PX_R[i].astype(F32)
    grad_top_in = grad_top_in + jnp.concatenate([upper, lower], axis=0)

    top_sum = shown_z(scatter_sum(top_sum, W_S.at[2], W_R.at[2]), W_Z.at[2])

    low = grad_top_in.astype(BF16)
    for s in range(2):
        UPIECE[s] = dot_at(UT[0, s], low)
    chain(UPIECE, uprev, 2)
    for m in range(MB):
        GRADM[m] = GRADM[m] + linked(UPIECE, ulast[m])
    g = flat(GRADM[...])
    gb, gs, gf, gm = backward(g, flat(MPRE1[...]), flat(MPRE2[...]), mm)
    MGM[...] = tiled(gm)
    for r in range(MB):
        MPIECE[r] = dot_at(MT[r, 1], MGM[r])
        MPIECE[MB + r] = dot_at(MT[r, 2], MGM[r])
    chain(MPIECE, mprev, 2 * MB)
    MBACK_S[0] = linked(MPIECE, mlast[MB]).astype(BF16)
    MBACK_S[1] = linked(MPIECE, mlast[MB + 1]).astype(BF16)
    mid_back = [send(MBACK_S.at[1], MBACK_R.at[0], right), send(MBACK_S.at[0], MBACK_R.at[1], left)]
    MGN[...] = tiled(g + dot_bt(gf, mm[0]))
    for r in range(MB):
        MGN[r] = MGN[r] + dot_at(MT[r, 0], MGM[r]) + linked(MPIECE, mlast[r])
    for i, term in enumerate(
        terms(flat(MS[0:MB]), flat(MMSG[...]), flat(MACT1[...]), flat(MACT2[...]), gb, gs, gf)
    ):
        W_S[1, pl.ds(i * T, T)] = term.astype(BF16)

    mid_sum = scattered(W_S.at[1], W_R.at[1])

    for copy in mid_back:
        copy.wait_recv()
    back_rows = jnp.concatenate(
        [MBACK_R[0] * has_left.astype(BF16), MBACK_R[1] * has_right.astype(BF16)], axis=0
    )
    for r in range(MB):
        MGN[r] = MGN[r] + placed_rows(mexport[0], r, back_rows)
    for m in range(MB):
        low = MGN[m].astype(BF16)
        for k in range(2):
            PPIECE[k * MB + m] = dot_at(PT[m, k], low)
    chain(PPIECE, pprev, 2 * MB)

    WACC[...] = jnp.zeros_like(WACC)

    def fine_backward(g, carry):
        base = g * GROUP
        here = pl.ds(base, GROUP)
        m = level(0)
        grad = jnp.concatenate(
            [COT[base + b].astype(F32) + linked(PPIECE, plast[base + b]) for b in range(GROUP)],
            axis=0,
        )
        gb, gs, gf = back_to_first(grad, flat(PRE1[here]), flat(PRE2[here]), m)
        GN[here] = tiled(grad)
        GF[here] = tiled(gf)
        for i, term in enumerate(
            terms(flat(S[here]), flat(MSG[here]), flat(ACT1[here]), flat(ACT2[here]), gb, gs, gf)
        ):
            WACC[i] = WACC[i] + term
        return carry

    lax.fori_loop(0, FB // GROUP, fine_backward, 0)
    W_S[0] = flat(WACC[...]).astype(BF16)
    fine_sum = scattered(W_S.at[0], W_R.at[0])
    top_sum = shown_y(slot_sum(top_sum, W_Z.at[2], nz), W_Y.at[2])
    mid_sum = shown_z(scatter_sum(mid_sum, W_S.at[1], W_R.at[1]), W_Z.at[1])

    def fine_rows(g, carry):
        here = pl.ds(g * GROUP, GROUP)
        gf = flat(GF[here])
        GM[here] = tiled(dot_bt(gf, M[0, 1]).astype(BF16))
        GN[here] = GN[here] + tiled(dot_bt(gf, M[0, 0]))
        return carry

    lax.fori_loop(0, FB // GROUP, fine_rows, 0)

    def fine_pieces(g, carry):
        for b in range(2):
            r = g * 2 + b
            grad = GM[r]
            PIECE[r] = dot_at(FT[r, 1], grad)
            PIECE[FB + r] = dot_at(FT[r, 2], grad)
            GN[r] = GN[r] + dot_at(FT[r, 0], grad)
        return carry

    lax.fori_loop(0, FB // 2, fine_pieces, 0)
    chain(PIECE, fprev, 2 * FB)
    BACK_S[0] = linked(PIECE, flast[FB]).astype(BF16)
    BACK_S[1] = linked(PIECE, flast[FB + 1]).astype(BF16)
    back = [send(BACK_S.at[1], BACK_R.at[0], right), send(BACK_S.at[0], BACK_R.at[1], left)]

    half = rows // 2
    value = scatter_sum(fine_sum, W_S.at[0], W_R.at[0])
    first = shown_y(value[0:half], W_Y.at[0, :, 0:half])
    second = shown_z(value[half:rows], W_Z.at[0, :, half:rows])
    W_O[2, chunk(0, 0)] = slot_sum(top_sum, W_Y.at[2], ny)
    top_sum = gathered(W_O.at[2])
    mid_sum = shown_y(slot_sum(mid_sum, W_Z.at[1], nz), W_Y.at[1])

    first = shown_z(slot_sum(first, W_Y.at[0, :, 0:half], ny), W_Z.at[0, :, 0:half])
    second = shown_y(slot_sum(second, W_Z.at[0, :, half:rows], nz), W_Y.at[0, :, half:rows])

    for copy in back:
        copy.wait_recv()
    back_rows = jnp.concatenate(
        [BACK_R[0] * has_left.astype(BF16), BACK_R[1] * has_right.astype(BF16)], axis=0
    )
    fexp = fexport[0]

    def finish(r, carry):
        ONODE[r] = (
            GN[r] + linked(PIECE, flast[r]) + placed_rows(fexp, r, back_rows)
        ).astype(BF16)
        return carry

    lax.fori_loop(0, FB, finish, 0)
    put_nodes = load(ONODE, node_grad)
    W_O[1, chunk(0, 0)] = slot_sum(mid_sum, W_Y.at[1], ny)
    mid_sum = gathered(W_O.at[1])
    W_O[0, chunk(0, 0)] = jnp.concatenate(
        [
            slot_sum(first, W_Z.at[0, :, 0:half], nz),
            slot_sum(second, W_Y.at[0, :, half:rows], ny),
        ],
        axis=0,
    )
    fine_sum = gathered(W_O.at[0])
    for copy in top_sum + mid_sum:
        copy.wait_recv()
    put_upper = load(W_O.at[pl.ds(1, 2)], weight_grad.at[pl.ds(1, 2)])
    for copy in fine_sum:
        copy.wait_recv()
    put_fine = load(W_O.at[0], weight_grad.at[0])
    for copy in started:
        copy.wait_send()
    put_nodes.wait()
    put_upper.wait()
    put_fine.wait()


def write_kernel(node_in, weight_in, node_out, weight_out, nodes, low, full, sem):
    fetch = [pltpu.make_async_copy(weight_in.at[l], low.at[l], sem.at[l]) for l in range(3)]
    put = [pltpu.make_async_copy(full.at[l], weight_out.at[l], sem.at[3 + l]) for l in range(3)]
    node_fetch = pltpu.make_async_copy(node_in, nodes, sem.at[6])
    node_put = pltpu.make_async_copy(nodes, node_out, sem.at[7])
    for copy in fetch:
        copy.start()
    node_fetch.start()
    for l in range(3):
        fetch[l].wait()
        full[l] = low[l].astype(F32)
        put[l].start()
    node_fetch.wait()
    node_put.start()
    for copy in put:
        copy.wait()
    node_put.wait()


def written(node_grad, weight_grad):
    anywhere = pl.BlockSpec(memory_space=pl.ANY)
    return pl.pallas_call(
        write_kernel,
        out_shape=(
            jax.ShapeDtypeStruct(node_grad.shape, BF16),
            jax.ShapeDtypeStruct(weight_grad.shape, F32),
        ),
        in_specs=[anywhere] * 2,
        out_specs=(anywhere, anywhere),
        scratch_shapes=[
            pltpu.VMEM(node_grad.shape, BF16),
            pltpu.VMEM(weight_grad.shape, BF16),
            pltpu.VMEM(weight_grad.shape, F32),
            pltpu.SemaphoreType.DMA((8,)),
        ],
        compiler_params=pltpu.CompilerParams(vmem_limit_bytes=64 * 1024 * 1024),
        name="write_results",
    )(node_grad, weight_grad)


def on_device(nx, ndp, *args):
    (
        nodes,
        cotangent,
        weights,
        fine_tiles,
        fine_cols,
        fine_export,
        pool_tiles,
        pool_cols,
        mid_tiles,
        mid_cols,
        mid_export,
        top_pool_tiles,
        top_pool_cols,
        top_tiles,
        top_cols,
    ) = args
    ny = NY
    anywhere = pl.BlockSpec(memory_space=pl.ANY)

    def low(*shape):
        return pltpu.VMEM(shape, BF16)

    def full(*shape):
        return pltpu.VMEM(shape, F32)

    def index(number):
        return pltpu.SMEM((number,), jnp.int32)

    nz = ndp // NC
    rows = 4 * T // (NC * nx)
    copies = (
        4 * 2
        + (nx - 1 + ny - 1) * 5
        + 2
        + 3 * 2 * (NC * nx - 1)
        + 4 * (ny - 1 + nz - 1)
    )
    scratch = [
        pltpu.SMEM((3, FB), jnp.int32),
        pltpu.VMEM((1, 2, T), jnp.int32),
        pltpu.SMEM((2, MB), jnp.int32),
        pltpu.SMEM((MB, 3), jnp.int32),
        pltpu.VMEM((1, 2, T), jnp.int32),
        pltpu.SMEM((1, 2), jnp.int32),
        pltpu.SMEM((1, 3), jnp.int32),
        low(FB + 2, T, T),
        low(FB, T, T),
        low(3, 4, T, T),
        low(FB, 3, T, T),
        low(MB, 2, T, T),
        low(MB, 3, T, T),
        low(1, 2, T, T),
        low(1, 3, T, T),
        full(FB, T, T),
        full(FB, T, T),
        full(FB, T, T),
        low(FB, T, T),
        low(FB, T, T),
        low(FB, T, T),
        low(FB, T, T),
        full(FB, T, T),
        low(FB, T, T),
        full(2 * FB, T, T),
        low(MB + 2, T, T),
        full(MB, T, T),
        full(MB, T, T),
        full(MB, T, T),
        low(MB, T, T),
        low(MB, T, T),
        low(MB, T, T),
        low(MB, T, T),
        full(MB, T, T),
        low(MB, T, T),
        full(MB, T, T),
        low(MB, T, T),
        full(2 * MB, T, T),
        full(2 * MB, T, T),
        full(2, T, T),
        index(2 * FB),
        index(FB + 2),
        index(2 * MB),
        index(MB + 2),
        index(2 * MB),
        index(FB),
        index(2),
        index(MB),
        low(2, T, T),
        low(2, T, T),
        low(2, T, T),
        low(2, T, T),
        low(2, T, T),
        low(2, T, T),
        low(2, T, T),
        low(2, T, T),
        pltpu.VMEM((8, T), jnp.int32),
        pltpu.VMEM((nx - 1, 8, T), jnp.int32),
        pltpu.VMEM((ny - 1, 8, T), jnp.int32),
        low(ny, HALF, T),
        low(nx, HALF, T),
        low(HALF, T),
        low(nx - 1, HALF, T),
        low(nx - 1, HALF, T),
        low(ny - 1, HALF, T),
        low(ny - 1, HALF, T),
        low(T, T),
        low(T, T),
        low(T, T),
        low(nx - 1, HALF, T),
        low(ny - 1, HALF, T),
        low(ny - 1, HALF, T),
        low(ny - 1, HALF, T),
        low(nx - 1, HALF, T),
        low(nx - 1, HALF, T),
        full(4, T, T),
        low(3, 4 * T, T),
        low(3, NC * nx - 1, rows, T),
        low(3, ny, rows, T),
        low(3, nz, rows, T),
        low(3, 4 * T, T),
        low(FB, T, T),
        low(FB, T, T),
        pltpu.SemaphoreType.DMA((20,)),
        pltpu.SemaphoreType.DMA((copies,)),
        pltpu.SemaphoreType.DMA((copies,)),
    ]

    def body(*refs):
        kernel(nx, ndp, *refs)

    node_grad, weight_grad = pl.pallas_call(
        body,
        out_shape=(
            jax.ShapeDtypeStruct((FB, T, T), BF16),
            jax.ShapeDtypeStruct((3, 4 * T, T), BF16),
        ),
        in_specs=[anywhere] * 15,
        out_specs=(anywhere, anywhere),
        scratch_shapes=scratch,
        compiler_params=pltpu.CompilerParams(
            collective_id=0, has_side_effects=True, vmem_limit_bytes=64 * 1024 * 1024
        ),
        name="mesh_step",
    )(
        nodes.reshape(FB, T, T),
        cotangent.reshape(FB, T, T),
        weights,
        fine_tiles,
        fine_cols.T,
        fine_export,
        pool_tiles,
        pool_cols.T,
        mid_tiles,
        mid_cols,
        mid_export,
        top_pool_tiles,
        top_pool_cols,
        top_tiles,
        top_cols,
    )
    node_grad, weight_grad = written(node_grad, weight_grad)
    return node_grad.reshape(nodes.shape), weight_grad.reshape(weights.shape)


def solution(mesh):
    nx, ndp = mesh.shape["dom"] // NY, mesh.shape["dp"]

    def run(*args):
        return on_device(nx, ndp, *args)

    return jax.shard_map(
        run,
        mesh=mesh,
        in_specs=(
            P("dp", "dom", None),
            P("dp", "dom", None),
            P(),
            P("dom", None, None, None),
            P("dom", None),
            P("dom", None, None),
            P("dom", None, None, None),
            P("dom", None),
            P("dom", None, None, None),
            P("dom", None),
            P("dom", None, None),
            P("dom", None, None, None),
            P("dom", None),
            P("dom", None, None, None),
            P("dom", None),
        ),
        out_specs=(P("dp", "dom", None), P()),
        check_vma=False,
    )
```

```python
import jax
import jax.numpy as jnp
from jax import lax
from jax.experimental import pallas as pl
from jax.experimental.pallas import tpu as pltpu
from jax.sharding import PartitionSpec as P

NY = 8
NC = 2
T = 128
HALF = T // 2
FB, MB, TB = 16, 4, 1
GROUP = 8
F32, BF16 = jnp.float32, jnp.bfloat16
MESH = pl.DeviceIdType.MESH


def dot(a, b):
    return jnp.dot(a, b, preferred_element_type=F32)


def dot_bt(a, b):
    return lax.dot_general(a, b, (((1,), (1,)), ((), ())), preferred_element_type=F32)


def dot_at(a, b):
    return lax.dot_general(a, b, (((0,), (0,)), ((), ())), preferred_element_type=F32)


def logistic(s):
    return 0.5 * jnp.tanh(0.5 * s) + 0.5


def slope(s):
    q = logistic(s)
    return q * (1.0 + s * (1.0 - q))


def far_first(number):
    return sorted(range(1, number), key=lambda i: -min(i, number - i))


def flat(blocks):
    return blocks.reshape(-1, T)


def tiled(rows):
    return rows.reshape(-1, T, T)


def picked_rows(export, source):
    columns = [
        jnp.transpose(jnp.broadcast_to(export[i : i + 1].astype(F32), (T, T))) for i in range(2)
    ]
    lane = lax.broadcasted_iota(jnp.int32, (T, T), 1).astype(F32)
    total = jnp.zeros((2 * T, T), F32)
    for pair in range(source.shape[0] // 2):
        onehot = jnp.concatenate(
            [
                jnp.concatenate(
                    [
                        jnp.where(column - T * (2 * pair + half) == lane, 1.0, 0.0)
                        for half in range(2)
                    ],
                    axis=1,
                )
                for column in columns
            ],
            axis=0,
        ).astype(BF16)
        total = total + dot(onehot, flat(source[2 * pair : 2 * pair + 2]))
    return tiled(total.astype(BF16))


def placed_rows(export, block, rows):
    row = lax.broadcasted_iota(jnp.int32, (T, T), 0) + block * T
    onehot = jnp.concatenate(
        [jnp.where(export[i : i + 1] == row, 1.0, 0.0) for i in range(2)], axis=1
    ).astype(BF16)
    return dot(onehot, rows)


def link(column, number, targets, prev, last, parts=(True, True)):
    def before(s, carry):
        mine = column(s)
        best = jnp.int32(-1)
        for t in range(number):
            best = jnp.where((column(t) == mine) & (t < s), t, best)
        prev[s] = best
        return carry

    def final(j, carry):
        best = jnp.int32(-1)
        for t in range(number):
            best = jnp.where(column(t) == j, t, best)
        last[j] = best
        return carry

    if parts[0]:
        lax.fori_loop(0, number, before, 0)
    if parts[1]:
        lax.fori_loop(0, targets, final, 0)


def linked(pieces, at):
    return jnp.where(at >= 0, 1.0, 0.0) * pieces[jnp.maximum(at, 0)]


def chain(pieces, prev, number):
    def step(s, carry):
        pieces[s] = pieces[s] + linked(pieces, prev[s])
        return carry

    lax.fori_loop(0, number, step, 0)


def kernel(
    nx,
    ndp,
    nodes,
    cotangent,
    weights,
    fine_tiles,
    fine_cols,
    fine_export,
    pool_tiles,
    pool_cols,
    mid_tiles,
    mid_cols,
    mid_export,
    upper_tiles,
    upper_cols,
    top_tiles,
    top_cols,
    node_grad,
    weight_grad,
    fcols,
    fexport,
    pcols,
    mcols,
    mexport,
    ucols,
    tcols,
    S,
    COT,
    M,
    FT,
    PT,
    MT,
    UT,
    TT,
    PART,
    PRE1,
    PRE2,
    ACT1,
    ACT2,
    MSG,
    OUT,
    GN,
    GM,
    PIECE,
    MS,
    MPART,
    MPRE1,
    MPRE2,
    MACT1,
    MACT2,
    MMSG,
    MOUT,
    GRADM,
    GRADML,
    MGN,
    MGM,
    MPIECE,
    PPIECE,
    UPIECE,
    fprev,
    flast,
    mprev,
    mlast,
    pprev,
    plast,
    uprev,
    ulast,
    HALO_S,
    HALO_R,
    MHALO_S,
    MHALO_R,
    BACK_S,
    BACK_R,
    MBACK_S,
    MBACK_R,
    COL_S,
    COL_R,
    COLY_R,
    YG,
    XG,
    PARTNER,
    SEL_S,
    SEL_R,
    SELY_S,
    SELY_R,
    P1_S,
    P1_R,
    P2_S,
    P2_R,
    P2Y_R,
    PY_S,
    PY_R,
    PX_S,
    PX_R,
    WACC,
    W_S,
    W_R,
    W_Y,
    W_Z,
    W_O,
    GF,
    ONODE,
    load_sem,
    send_sem,
    recv_sem,
):
    ny = NY
    ndom = nx * ny
    dp = lax.axis_index("dp")
    dom = lax.axis_index("dom")
    x = lax.div(dom, ny)
    y = lax.rem(dom, ny)
    nz = ndp // NC
    z = lax.div(dp, NC)
    core = lax.rem(dp, NC)

    left = (dp, lax.rem(dom + ndom - 1, ndom))
    right = (dp, lax.rem(dom + 1, ndom))

    def at_x(i):
        return (dp, lax.rem(x + i, nx) * ny + y)

    def at_y(i):
        return (dp, x * ny + lax.rem(y + i, ny))

    def at_z(i):
        return (lax.rem(z + i, nz) * NC + core, dom)

    def at_cx(c, i):
        return (z * NC + lax.rem(core + c, NC), lax.rem(x + i, nx) * ny + y)

    x_order = far_first(nx)
    y_order = far_first(ny)
    z_order = far_first(nz)
    cx_order = [(c, i) for c in range(NC) for i in range(nx) if (c, i) != (0, 0)]
    partners = (
        [left, right]
        + [at_cx(c, i) for c, i in cx_order]
        + [at_y(i) for i in y_order]
        + [at_z(i) for i in z_order]
    )
    started = []

    def send(src, dst, device):
        number = len(started)
        copy = pltpu.make_async_remote_copy(
            src_ref=src,
            dst_ref=dst,
            send_sem=send_sem.at[number],
            recv_sem=recv_sem.at[number],
            device_id=device,
            device_id_type=MESH,
        )
        copy.start()
        started.append(copy)
        return copy

    loads = []

    def load(src, dst):
        copy = pltpu.make_async_copy(src, dst, load_sem.at[len(loads)])
        copy.start()
        loads.append(copy)
        return copy

    got_nodes = load(nodes, S.at[pl.ds(0, FB)])
    got_export = load(fine_export, fexport)
    barrier = pltpu.get_barrier_semaphore()
    for partner in partners:
        pl.semaphore_signal(barrier, inc=1, device_id=partner, device_id_type=MESH)

    has_left = jnp.where(dom > 0, 1.0, 0.0).astype(F32)
    has_right = jnp.where(dom < ndom - 1, 1.0, 0.0).astype(F32)

    def level(l):
        return [M[l, i] for i in range(4)]

    rows = 4 * T // (NC * nx)

    def chunk(c, i):
        number = lax.rem(core + c, NC) * nx + lax.rem(x + i, nx)
        return pl.ds(pl.multiple_of(number * rows, rows), rows)

    def scattered(store, slots):
        return [
            send(store.at[chunk(c, i)], slots.at[n], at_cx(c, i))
            for n, (c, i) in enumerate(cx_order)
        ]

    def scatter_sum(copies, store, slots):
        for copy in copies:
            copy.wait_recv()
        total = store[chunk(0, 0)].astype(F32)
        for n in range(len(cx_order)):
            total = total + slots[n].astype(F32)
        return total.astype(BF16)

    def shown_y(value, slots):
        slots[y] = value
        return [send(slots.at[y], slots.at[y], at_y(i)) for i in y_order]

    def shown_z(value, slots):
        slots[z] = value
        return [send(slots.at[z], slots.at[z], at_z(i)) for i in z_order]

    def slot_sum(copies, slots, number):
        for copy in copies:
            copy.wait_recv()
        total = slots[0].astype(F32)
        for i in range(1, number):
            total = total + slots[i].astype(F32)
        return total.astype(BF16)

    def gathered(store):
        mine = store.at[chunk(0, 0)]
        return [send(mine, mine, at_cx(c, i)) for c, i in cx_order]

    got_export.wait()
    got_nodes.wait()
    got_tcols = load(top_cols, tcols)
    got_pcols = load(pool_cols, pcols)
    got_ucols = load(upper_cols, ucols)
    got_cot = load(cotangent, COT)
    got_pool = load(pool_tiles, PT)
    got_upper = load(upper_tiles, UT)
    got_weights = load(weights, M)
    got_fine = load(fine_tiles, FT)
    got_fcols = load(fine_cols, fcols)
    got_mid = load(mid_tiles, MT)
    got_mcols = load(mid_cols, mcols)
    got_mexport = load(mid_export, mexport)
    got_top = load(top_tiles, TT)
    HALO_S[...] = picked_rows(fexport[0], S.at[pl.ds(0, FB)])
    pl.semaphore_wait(barrier, len(partners))
    halo = [send(HALO_S.at[1], HALO_R.at[0], right), send(HALO_S.at[0], HALO_R.at[1], left)]
    got_tcols.wait()
    COL_S[...] = jnp.full((8, T), tcols[0, 2], jnp.int32)
    cols_sent = [send(COL_S, COL_R.at[i - 1], at_x(i)) for i in x_order]
    cols_sent += [send(COL_S, COLY_R.at[i - 1], at_y(i)) for i in y_order]

    for copy in (got_cot, got_pool, got_pcols, got_upper, got_ucols):
        copy.wait()
    for m in range(MB):
        pooled = dot(PT[m, 0], COT[pcols[0, m]]) + dot(PT[m, 1], COT[pcols[1, m]])
        GRADM[m] = pooled
        GRADML[m] = pooled.astype(BF16)
    grad_top = dot(UT[0, 0], GRADML[ucols[0, 0]]) + dot(UT[0, 1], GRADML[ucols[0, 1]])
    for copy in (got_weights, got_fine, got_fcols):
        copy.wait()

    def fine_own(g, carry):
        base = g * GROUP
        m0 = M[0, 0]
        u = flat(S[pl.ds(base, GROUP)])
        PRE1[pl.ds(base, GROUP)] = tiled(dot(u, m0))
        for b in range(GROUP):
            PART[base + b] = dot(FT[base + b, 0], S[base + b])
        return carry

    lax.fori_loop(0, FB // GROUP, fine_own, 0)

    for copy in halo:
        copy.wait_recv()
    S[FB] = HALO_R[0] * has_left.astype(BF16)
    S[FB + 1] = HALO_R[1] * has_right.astype(BF16)

    def forward(u, v, own_pre, m):
        pre1 = own_pre + dot(v, m[1])
        act1 = (pre1 * logistic(pre1)).astype(BF16)
        pre2 = dot(act1, m[2])
        act2 = (pre2 * logistic(pre2)).astype(BF16)
        return pre1, act1, pre2, act2

    def fine_forward(g, carry):
        base = g * GROUP
        m = level(0)
        messages = []
        for b in range(GROUP):
            r = base + b
            messages.append(
                (
                    PART[r]
                    + dot(FT[r, 1], S[fcols[1, r]])
                    + dot(FT[r, 2], S[fcols[2, r]])
                ).astype(BF16)
            )
        v = jnp.concatenate(messages, axis=0)
        here = pl.ds(base, GROUP)
        u = flat(S[here])
        pre1, act1, pre2, act2 = forward(u, v, flat(PRE1[here]), m)
        MSG[here] = tiled(v)
        PRE1[here] = tiled(pre1)
        ACT1[here] = tiled(act1)
        PRE2[here] = tiled(pre2)
        ACT2[here] = tiled(act2)
        OUT[here] = tiled((u.astype(F32) + dot(act2, m[3])).astype(BF16))
        return carry

    lax.fori_loop(0, FB // GROUP, fine_forward, 0)

    for m in range(MB):
        MS[m] = (dot(PT[m, 0], OUT[pcols[0, m]]) + dot(PT[m, 1], OUT[pcols[1, m]])).astype(BF16)
    got_mexport.wait()
    MHALO_S[...] = picked_rows(mexport[0], MS[0:MB])
    mid_halo = [send(MHALO_S.at[1], MHALO_R.at[0], right), send(MHALO_S.at[0], MHALO_R.at[1], left)]
    got_mid.wait()
    got_mcols.wait()
    mm = level(1)
    mu = flat(MS[0:MB])
    MPRE1[...] = tiled(dot(mu, mm[0]))
    for r in range(MB):
        MPART[r] = dot(MT[r, 0], MS[r])
    got_top.wait()
    link(lambda s: ucols[0, s], 2, MB, uprev, ulast)

    def fine_links(*parts):
        column = lambda s: fcols[1 + lax.div(s, FB), lax.rem(s, FB)]
        link(column, 2 * FB, FB + 2, fprev, flast, parts)

    fine_links(True, False)
    for copy in mid_halo:
        copy.wait_recv()
    MS[MB] = MHALO_R[0] * has_left.astype(BF16)
    MS[MB + 1] = MHALO_R[1] * has_right.astype(BF16)
    mv = jnp.concatenate(
        [
            (
                MPART[r] + dot(MT[r, 1], MS[mcols[r, 1]]) + dot(MT[r, 2], MS[mcols[r, 2]])
            ).astype(BF16)
            for r in range(MB)
        ],
        axis=0,
    )
    pre1, act1, pre2, act2 = forward(mu, mv, flat(MPRE1[...]), mm)
    MOUT[...] = tiled((mu.astype(F32) + dot(act2, mm[3])).astype(BF16))
    top_in = (dot(UT[0, 0], MOUT[ucols[0, 0]]) + dot(UT[0, 1], MOUT[ucols[0, 1]])).astype(BF16)

    YG[0] = top_in[0:HALF]
    XG[0] = top_in[HALF:T]
    along_y = [send(YG.at[0], YG.at[i], at_y(i)) for i in y_order]
    along_x = [send(XG.at[0], XG.at[i], at_x(i)) for i in x_order]
    partner = send(YG.at[0], PARTNER, at_x(nx // 2))
    MMSG[...] = tiled(mv)
    MACT1[...] = tiled(act1)
    MACT2[...] = tiled(act2)
    MPRE1[...] = tiled(slope(pre1))
    MPRE2[...] = tiled(slope(pre2))

    def fine_slopes(g, carry):
        here = pl.ds(g * 2, 2)
        PRE1[here] = slope(PRE1[here])
        PRE2[here] = slope(PRE2[here])
        return carry

    lax.fori_loop(0, FB // 2, fine_slopes, 0)
    tm = level(2)
    top_own = dot(top_in, tm[0])
    top_part = dot(TT[0, 0], top_in)
    for copy in cols_sent:
        copy.wait_recv()
    cols = [COL_S[0:1]] + [COL_R[i, 0:1] for i in range(nx - 1)]
    cols_y = [COL_S[0:1]] + [COLY_R[i, 0:1] for i in range(ny - 1)]

    def chosen(column, blocks, sources):
        total = jnp.zeros((HALF, T), BF16)
        for k, source in enumerate(sources):
            total = total + jnp.where(column == source, 1.0, 0.0).astype(BF16) * blocks[k]
        return total

    by_x = [lax.rem(x + nx - k, nx) * ny + y for k in range(nx)]
    by_y = [x * ny + lax.rem(y + ny - k, ny) for k in range(ny)]
    for copy in along_x:
        copy.wait_recv()
    chosen_y = []
    for i in y_order:
        SELY_S[i - 1] = chosen(cols_y[ny - i], XG, by_x)
        chosen_y.append(send(SELY_S.at[i - 1], SELY_R.at[i - 1], at_y(i)))
    lower = chosen(cols[0], XG, by_x)
    for copy in along_y:
        copy.wait_recv()
    chosen_x = []
    for i in x_order:
        SEL_S[i - 1] = chosen(cols[nx - i], YG, by_y)
        chosen_x.append(send(SEL_S.at[i - 1], SEL_R.at[i - 1], at_x(i)))
    upper = chosen(cols[0], YG, by_y)
    partner.wait_recv()
    across = jnp.concatenate([PARTNER[...], XG[nx // 2]], axis=0)
    top_part = top_part + dot(TT[0, 1], across)
    link(lambda s: pcols[lax.div(s, MB), lax.rem(s, MB)], 2 * MB, FB, pprev, plast)
    link(lambda s: mcols[lax.rem(s, MB), 1 + lax.div(s, MB)], 2 * MB, MB + 2, mprev, mlast)
    fine_links(False, True)
    for copy in chosen_y + chosen_x:
        copy.wait_recv()
    for i in range(ny - 1):
        lower = lower + SELY_R[i]
    for i in range(nx - 1):
        upper = upper + SEL_R[i]
    third = jnp.concatenate([upper, lower], axis=0)
    top_msg = (top_part + dot(TT[0, 2], third)).astype(BF16)
    pre1, act1, pre2, act2 = forward(top_in, top_msg, top_own, tm)

    def back_to_first(g, slope1, slope2, m):
        gb = g.astype(BF16)
        gs = (dot_bt(gb, m[3]) * slope2).astype(BF16)
        gf = (dot_bt(gs, m[2]) * slope1).astype(BF16)
        return gb, gs, gf

    def backward(g, slope1, slope2, m):
        gb, gs, gf = back_to_first(g, slope1, slope2, m)
        return gb, gs, gf, dot_bt(gf, m[1]).astype(BF16)

    def terms(u, v, act1, act2, gb, gs, gf):
        return dot_at(u, gf), dot_at(v, gf), dot_at(act1, gs), dot_at(act2, gb)

    gb, gs, gf, gm = backward(grad_top, slope(pre1), slope(pre2), tm)
    P2_S[...] = dot_at(TT[0, 2], gm).astype(BF16)
    back_x = [send(P2_S.at[pl.ds(0, HALF)], P2_R.at[i - 1], at_x(i)) for i in x_order]
    back_y = [send(P2_S.at[pl.ds(HALF, HALF)], P2Y_R.at[i - 1], at_y(i)) for i in y_order]
    P1_S[...] = dot_at(TT[0, 1], gm).astype(BF16)
    back_half = send(P1_S, P1_R, at_x(nx // 2))
    grad_top_in = grad_top + dot_bt(gf, tm[0]) + dot_at(TT[0, 0], gm)
    for i, term in enumerate(terms(top_in, top_msg, act1, act2, gb, gs, gf)):
        W_S[2, pl.ds(i * T, T)] = term.astype(BF16)
    for copy in back_x:
        copy.wait_recv()
    upper_parts = [P2_S[0:HALF].astype(F32)] + [P2_R[i].astype(F32) for i in range(nx - 1)]

    def summed(target, columns, pieces):
        total = jnp.zeros((HALF, T), F32)
        for column, piece in zip(columns, pieces):
            total = total + jnp.where(column == target, 1.0, 0.0) * piece
        return total

    summed_y = []
    for i in y_order:
        target = x * ny + lax.rem(y + i, ny)
        PY_S[i - 1] = summed(target, cols, upper_parts).astype(BF16)
        summed_y.append(send(PY_S.at[i - 1], PY_R.at[i - 1], at_y(i)))
    upper = summed(dom, cols, upper_parts)
    for copy in back_y:
        copy.wait_recv()
    lower_parts = [P2_S[HALF:T].astype(F32)] + [P2Y_R[i].astype(F32) for i in range(ny - 1)]
    summed_x = []
    for i in x_order:
        target = lax.rem(x + i, nx) * ny + y
        PX_S[i - 1] = summed(target, cols_y, lower_parts).astype(BF16)
        summed_x.append(send(PX_S.at[i - 1], PX_R.at[i - 1], at_x(i)))
    lower = summed(dom, cols_y, lower_parts)
    top_sum = scattered(W_S.at[2], W_R.at[2])
    back_half.wait_recv()
    grad_top_in = grad_top_in + P1_R[...].astype(F32)
    for copy in summed_y + summed_x:
        copy.wait_recv()
    for i in range(ny - 1):
        upper = upper + PY_R[i].astype(F32)
    for i in range(nx - 1):
        lower = lower + PX_R[i].astype(F32)
    grad_top_in = grad_top_in + jnp.concatenate([upper, lower], axis=0)

    top_sum = shown_z(scatter_sum(top_sum, W_S.at[2], W_R.at[2]), W_Z.at[2])

    low = grad_top_in.astype(BF16)
    for s in range(2):
        UPIECE[s] = dot_at(UT[0, s], low)
    chain(UPIECE, uprev, 2)
    for m in range(MB):
        GRADM[m] = GRADM[m] + linked(UPIECE, ulast[m])
    g = flat(GRADM[...])
    gb, gs, gf, gm = backward(g, flat(MPRE1[...]), flat(MPRE2[...]), mm)
    MGM[...] = tiled(gm)
    for r in range(MB):
        MPIECE[r] = dot_at(MT[r, 1], MGM[r])
        MPIECE[MB + r] = dot_at(MT[r, 2], MGM[r])
    chain(MPIECE, mprev, 2 * MB)
    MBACK_S[0] = linked(MPIECE, mlast[MB]).astype(BF16)
    MBACK_S[1] = linked(MPIECE, mlast[MB + 1]).astype(BF16)
    mid_back = [send(MBACK_S.at[1], MBACK_R.at[0], right), send(MBACK_S.at[0], MBACK_R.at[1], left)]
    MGN[...] = tiled(g + dot_bt(gf, mm[0]))
    for r in range(MB):
        MGN[r] = MGN[r] + dot_at(MT[r, 0], MGM[r]) + linked(MPIECE, mlast[r])
    for i, term in enumerate(
        terms(flat(MS[0:MB]), flat(MMSG[...]), flat(MACT1[...]), flat(MACT2[...]), gb, gs, gf)
    ):
        W_S[1, pl.ds(i * T, T)] = term.astype(BF16)

    mid_sum = scattered(W_S.at[1], W_R.at[1])

    for copy in mid_back:
        copy.wait_recv()
    back_rows = jnp.concatenate(
        [MBACK_R[0] * has_left.astype(BF16), MBACK_R[1] * has_right.astype(BF16)], axis=0
    )
    for r in range(MB):
        MGN[r] = MGN[r] + placed_rows(mexport[0], r, back_rows)
    for m in range(MB):
        low = MGN[m].astype(BF16)
        for k in range(2):
            PPIECE[k * MB + m] = dot_at(PT[m, k], low)
    chain(PPIECE, pprev, 2 * MB)

    top_sum = shown_y(slot_sum(top_sum, W_Z.at[2], nz), W_Y.at[2])
    WACC[...] = jnp.zeros_like(WACC)

    def fine_backward(g, carry):
        base = g * GROUP
        here = pl.ds(base, GROUP)
        m = level(0)
        grad = jnp.concatenate(
            [COT[base + b].astype(F32) + linked(PPIECE, plast[base + b]) for b in range(GROUP)],
            axis=0,
        )
        gb, gs, gf = back_to_first(grad, flat(PRE1[here]), flat(PRE2[here]), m)
        GN[here] = tiled(grad)
        GF[here] = tiled(gf)
        for i, term in enumerate(
            terms(flat(S[here]), flat(MSG[here]), flat(ACT1[here]), flat(ACT2[here]), gb, gs, gf)
        ):
            WACC[i] = WACC[i] + term
        return carry

    lax.fori_loop(0, FB // GROUP, fine_backward, 0)
    W_S[0] = flat(WACC[...]).astype(BF16)
    fine_sum = scattered(W_S.at[0], W_R.at[0])
    mid_sum = shown_z(scatter_sum(mid_sum, W_S.at[1], W_R.at[1]), W_Z.at[1])

    def fine_rows(g, carry):
        here = pl.ds(g * GROUP, GROUP)
        gf = flat(GF[here])
        GM[here] = tiled(dot_bt(gf, M[0, 1]).astype(BF16))
        GN[here] = GN[here] + tiled(dot_bt(gf, M[0, 0]))
        return carry

    lax.fori_loop(0, FB // GROUP, fine_rows, 0)

    def fine_pieces(g, carry):
        for b in range(4):
            r = g * 4 + b
            grad = GM[r]
            PIECE[r] = dot_at(FT[r, 1], grad)
            PIECE[FB + r] = dot_at(FT[r, 2], grad)
            GN[r] = GN[r] + dot_at(FT[r, 0], grad)
        return carry

    lax.fori_loop(0, FB // 4, fine_pieces, 0)
    chain(PIECE, fprev, 2 * FB)
    BACK_S[0] = linked(PIECE, flast[FB]).astype(BF16)
    BACK_S[1] = linked(PIECE, flast[FB + 1]).astype(BF16)
    back = [send(BACK_S.at[1], BACK_R.at[0], right), send(BACK_S.at[0], BACK_R.at[1], left)]

    half = rows // 2
    value = scatter_sum(fine_sum, W_S.at[0], W_R.at[0])
    first = shown_y(value[0:half], W_Y.at[0, :, 0:half])
    second = shown_z(value[half:rows], W_Z.at[0, :, half:rows])
    W_O[2, chunk(0, 0)] = slot_sum(top_sum, W_Y.at[2], ny)
    top_sum = gathered(W_O.at[2])
    mid_sum = shown_y(slot_sum(mid_sum, W_Z.at[1], nz), W_Y.at[1])

    first = shown_z(slot_sum(first, W_Y.at[0, :, 0:half], ny), W_Z.at[0, :, 0:half])
    second = shown_y(slot_sum(second, W_Z.at[0, :, half:rows], nz), W_Y.at[0, :, half:rows])

    for copy in back:
        copy.wait_recv()
    back_rows = jnp.concatenate(
        [BACK_R[0] * has_left.astype(BF16), BACK_R[1] * has_right.astype(BF16)], axis=0
    )
    fexp = fexport[0]

    def finish(g, carry):
        for b in range(4):
            r = g * 4 + b
            ONODE[r] = (
                GN[r] + linked(PIECE, flast[r]) + placed_rows(fexp, r, back_rows)
            ).astype(BF16)
        return carry

    lax.fori_loop(0, FB // 4, finish, 0)
    put_nodes = load(ONODE, node_grad)
    W_O[1, chunk(0, 0)] = slot_sum(mid_sum, W_Y.at[1], ny)
    mid_sum = gathered(W_O.at[1])
    W_O[0, chunk(0, 0)] = jnp.concatenate(
        [
            slot_sum(first, W_Z.at[0, :, 0:half], nz),
            slot_sum(second, W_Y.at[0, :, half:rows], ny),
        ],
        axis=0,
    )
    fine_sum = gathered(W_O.at[0])
    for copy in top_sum + mid_sum:
        copy.wait_recv()
    put_upper = load(W_O.at[pl.ds(1, 2)], weight_grad.at[pl.ds(1, 2)])
    for copy in fine_sum:
        copy.wait_recv()
    put_fine = load(W_O.at[0], weight_grad.at[0])
    for copy in started:
        copy.wait_send()
    put_nodes.wait()
    put_upper.wait()
    put_fine.wait()


def write_kernel(node_in, weight_in, node_out, weight_out, nodes, low, full, sem):
    fetch = [pltpu.make_async_copy(weight_in.at[l], low.at[l], sem.at[l]) for l in range(3)]
    put = [pltpu.make_async_copy(full.at[l], weight_out.at[l], sem.at[3 + l]) for l in range(3)]
    node_fetch = pltpu.make_async_copy(node_in, nodes, sem.at[6])
    node_put = pltpu.make_async_copy(nodes, node_out, sem.at[7])
    for copy in fetch:
        copy.start()
    node_fetch.start()
    for l in range(3):
        fetch[l].wait()
        full[l] = low[l].astype(F32)
        put[l].start()
    node_fetch.wait()
    node_put.start()
    for copy in put:
        copy.wait()
    node_put.wait()


def written(node_grad, weight_grad):
    anywhere = pl.BlockSpec(memory_space=pl.ANY)
    return pl.pallas_call(
        write_kernel,
        out_shape=(
            jax.ShapeDtypeStruct(node_grad.shape, BF16),
            jax.ShapeDtypeStruct(weight_grad.shape, F32),
        ),
        in_specs=[anywhere] * 2,
        out_specs=(anywhere, anywhere),
        scratch_shapes=[
            pltpu.VMEM(node_grad.shape, BF16),
            pltpu.VMEM(weight_grad.shape, BF16),
            pltpu.VMEM(weight_grad.shape, F32),
            pltpu.SemaphoreType.DMA((8,)),
        ],
        compiler_params=pltpu.CompilerParams(vmem_limit_bytes=64 * 1024 * 1024),
        name="write_results",
    )(node_grad, weight_grad)


def on_device(nx, ndp, *args):
    (
        nodes,
        cotangent,
        weights,
        fine_tiles,
        fine_cols,
        fine_export,
        pool_tiles,
        pool_cols,
        mid_tiles,
        mid_cols,
        mid_export,
        top_pool_tiles,
        top_pool_cols,
        top_tiles,
        top_cols,
    ) = args
    ny = NY
    anywhere = pl.BlockSpec(memory_space=pl.ANY)

    def low(*shape):
        return pltpu.VMEM(shape, BF16)

    def full(*shape):
        return pltpu.VMEM(shape, F32)

    def index(number):
        return pltpu.SMEM((number,), jnp.int32)

    nz = ndp // NC
    rows = 4 * T // (NC * nx)
    copies = (
        4 * 2
        + (nx - 1 + ny - 1) * 5
        + 2
        + 3 * 2 * (NC * nx - 1)
        + 4 * (ny - 1 + nz - 1)
    )
    scratch = [
        pltpu.SMEM((3, FB), jnp.int32),
        pltpu.VMEM((1, 2, T), jnp.int32),
        pltpu.SMEM((2, MB), jnp.int32),
        pltpu.SMEM((MB, 3), jnp.int32),
        pltpu.VMEM((1, 2, T), jnp.int32),
        pltpu.SMEM((1, 2), jnp.int32),
        pltpu.SMEM((1, 3), jnp.int32),
        low(FB + 2, T, T),
        low(FB, T, T),
        low(3, 4, T, T),
        low(FB, 3, T, T),
        low(MB, 2, T, T),
        low(MB, 3, T, T),
        low(1, 2, T, T),
        low(1, 3, T, T),
        full(FB, T, T),
        full(FB, T, T),
        full(FB, T, T),
        low(FB, T, T),
        low(FB, T, T),
        low(FB, T, T),
        low(FB, T, T),
        full(FB, T, T),
        low(FB, T, T),
        full(2 * FB, T, T),
        low(MB + 2, T, T),
        full(MB, T, T),
        full(MB, T, T),
        full(MB, T, T),
        low(MB, T, T),
        low(MB, T, T),
        low(MB, T, T),
        low(MB, T, T),
        full(MB, T, T),
        low(MB, T, T),
        full(MB, T, T),
        low(MB, T, T),
        full(2 * MB, T, T),
        full(2 * MB, T, T),
        full(2, T, T),
        index(2 * FB),
        index(FB + 2),
        index(2 * MB),
        index(MB + 2),
        index(2 * MB),
        index(FB),
        index(2),
        index(MB),
        low(2, T, T),
        low(2, T, T),
        low(2, T, T),
        low(2, T, T),
        low(2, T, T),
        low(2, T, T),
        low(2, T, T),
        low(2, T, T),
        pltpu.VMEM((8, T), jnp.int32),
        pltpu.VMEM((nx - 1, 8, T), jnp.int32),
        pltpu.VMEM((ny - 1, 8, T), jnp.int32),
        low(ny, HALF, T),
        low(nx, HALF, T),
        low(HALF, T),
        low(nx - 1, HALF, T),
        low(nx - 1, HALF, T),
        low(ny - 1, HALF, T),
        low(ny - 1, HALF, T),
        low(T, T),
        low(T, T),
        low(T, T),
        low(nx - 1, HALF, T),
        low(ny - 1, HALF, T),
        low(ny - 1, HALF, T),
        low(ny - 1, HALF, T),
        low(nx - 1, HALF, T),
        low(nx - 1, HALF, T),
        full(4, T, T),
        low(3, 4 * T, T),
        low(3, NC * nx - 1, rows, T),
        low(3, ny, rows, T),
        low(3, nz, rows, T),
        low(3, 4 * T, T),
        low(FB, T, T),
        low(FB, T, T),
        pltpu.SemaphoreType.DMA((20,)),
        pltpu.SemaphoreType.DMA((copies,)),
        pltpu.SemaphoreType.DMA((copies,)),
    ]

    def body(*refs):
        kernel(nx, ndp, *refs)

    node_grad, weight_grad = pl.pallas_call(
        body,
        out_shape=(
            jax.ShapeDtypeStruct((FB, T, T), BF16),
            jax.ShapeDtypeStruct((3, 4 * T, T), BF16),
        ),
        in_specs=[anywhere] * 15,
        out_specs=(anywhere, anywhere),
        scratch_shapes=scratch,
        compiler_params=pltpu.CompilerParams(
            collective_id=0, has_side_effects=True, vmem_limit_bytes=64 * 1024 * 1024
        ),
        name="mesh_step",
    )(
        nodes.reshape(FB, T, T),
        cotangent.reshape(FB, T, T),
        weights,
        fine_tiles,
        fine_cols.T,
        fine_export,
        pool_tiles,
        pool_cols.T,
        mid_tiles,
        mid_cols,
        mid_export,
        top_pool_tiles,
        top_pool_cols,
        top_tiles,
        top_cols,
    )
    node_grad, weight_grad = written(node_grad, weight_grad)
    return node_grad.reshape(nodes.shape), weight_grad.reshape(weights.shape)


def solution(mesh):
    nx, ndp = mesh.shape["dom"] // NY, mesh.shape["dp"]

    def run(*args):
        return on_device(nx, ndp, *args)

    return jax.shard_map(
        run,
        mesh=mesh,
        in_specs=(
            P("dp", "dom", None),
            P("dp", "dom", None),
            P(),
            P("dom", None, None, None),
            P("dom", None),
            P("dom", None, None),
            P("dom", None, None, None),
            P("dom", None),
            P("dom", None, None, None),
            P("dom", None),
            P("dom", None, None),
            P("dom", None, None, None),
            P("dom", None),
            P("dom", None, None, None),
            P("dom", None),
        ),
        out_specs=(P("dp", "dom", None), P()),
        check_vma=False,
    )
```
